32 devices in a mesh: atom: 8 (over y, x, core), mode: 4 (over z).
Axes of the slice: x: 2, y: 2, z: 4, core: 2. Of those that a mesh axis runs over, the one named last changes fastest.
Arguments:
- eigvec: bfloat16 [3, 2048, 1024], P(None, 'atom', 'mode'), may hold values from -0.078125 to 0.078125
- force: float32 [3, 3, 16, 2048], P(None, None, None, 'atom'), may hold values from -12 to 12
- bond: float32 [3, 16, 2048], P(None, None, 'atom'), may hold values from -6 to 6
- nbr: int32 [16, 2048], P(None, 'atom'), may hold values from 0 to 2047, as said below
- band: int32 [2, 1024], P(None, 'mode'), may hold values from 0 to 1024, as said below
- freq: float32 [1024], P('mode'), may hold values from 0.5 to 4, as said below
Outputs:
- diffusivity: float32 [1024], P('mode')
- conductivity: float32 [1024], P('mode')
The draws below stay inside these ranges and needn't reach their ends.
Inputs may be any that keep to these rules, and one draw needn't show every extreme that they name: `nbr`: each entry is an atom whose position in atom order differs from that of its own atom by 1 to 128, counted cyclically over the 2048 atoms; the distance 128 occurs in every draw. For every mode i: max(0, i - 128) <= band[0, i] <= i < band[1, i] <= min(1024, i + 129); both outer limits are reached at some mode. `freq`: strictly increasing along the modes.
All inputs are finite; a program needn't handle non-finite values.
Results may differ from the reference program's by a relative error of at most 0.00057.
Values may be sent and summed in bfloat16 or wider, within the bound.
No kernel may reach another device: no remote copies, remote signals or barrier semaphores. Data moves between devices by JAX's collectives and lax.ppermute only.
A program may use at most 64 MiB of HBM per device.

```python
import math
import jax
import jax.numpy as jnp
from jax import lax

ATOM_DEV = 256
MODE_DEV = 256
NBR = 16
RIM = 128
HALF = 128
BROAD = 128
ATOMS = 2048
MODES = 1024
N_ATOM = 8
N_MODE = 4


def draw_nbr(key, part):
    first_key = jax.random.fold_in(key, 11)
    second_key = jax.random.fold_in(key, 12)
    third_key = jax.random.fold_in(key, 13)
    magnitude = jax.random.randint(first_key, (NBR, ATOMS), 1, RIM + 1)
    direction = 2 * jax.random.randint(second_key, (NBR, ATOMS), 0, 2) - 1
    chosen = jax.random.randint(third_key, (), 0, ATOMS)
    atom_ids = jnp.arange(ATOMS, dtype=jnp.int32)
    slot_ids = jnp.arange(NBR, dtype=jnp.int32)[:, None]
    magnitude = jnp.where((slot_ids == 0) & (atom_ids[None, :] == chosen), RIM, magnitude)
    return ((atom_ids[None, :] + direction * magnitude) % ATOMS).astype(jnp.int32)


def draw_band(key, part):
    lower_key = jax.random.fold_in(key, 21)
    upper_key = jax.random.fold_in(key, 22)
    chosen_key = jax.random.fold_in(key, 23)
    below = jax.random.randint(lower_key, (MODES,), 0, HALF + 1)
    above = jax.random.randint(upper_key, (MODES,), 0, HALF + 1)
    chosen = jax.random.randint(chosen_key, (), HALF, MODES - HALF - 1)
    mode_ids = jnp.arange(MODES, dtype=jnp.int32)
    below = jnp.where(mode_ids == chosen, HALF, below)
    above = jnp.where(mode_ids == chosen, HALF, above)
    lower_end = jnp.maximum(mode_ids - below, 0)
    upper_end = jnp.minimum(mode_ids + 1 + above, MODES)
    return jnp.stack([lower_end, upper_end]).astype(jnp.int32)


def draw_freq(key, part):
    spacing = jax.random.uniform(key, (MODES,), minval=0.2, maxval=1.8)
    rising = jnp.cumsum(spacing)
    return (0.5 + 3.5 * rising / rising[-1]).astype(jnp.float32)


def levels(stream_key, extent, shards, least, top_value):
    def one(dim, shards_of):
        steps = jax.random.uniform(jax.random.fold_in(jax.random.fold_in(stream_key, 6), dim), (shards_of,), jnp.float32, least / len(shards), top_value / len(shards))
        return jnp.repeat(jnp.exp(steps), extent[dim] // shards_of).reshape((-1,) + (1,) * (len(extent) - dim - 1))

    level = one(*shards[0])
    for cut in shards[1:]:
        level = level * one(*cut)
    return level


def centred(rng, extent, scale, most, shards=(), kind=jnp.bfloat16):
    array = scale * jax.random.normal(rng, extent, jnp.float32)
    if shards:
        array = array * levels(rng, extent, shards, -0.22, 0.18)
    return jnp.clip(array, -most, most).astype(kind)


def setup_inputs(seed: int = 0) -> dict:
    arg_keys = jax.random.split(jax.random.key(seed), 7)
    eigvec = centred(arg_keys[0], (3, ATOMS, MODES), ((3 * ATOMS) ** -0.5), 0.078125, ((1, 8), (2, 4)))
    force = centred(arg_keys[1], (3, 3, NBR, ATOMS), 2.0, 12.0, ((3, 8),), jnp.float32)
    bond = centred(arg_keys[2], (3, NBR, ATOMS), 1.0, 6.0, ((2, 8),), jnp.float32)
    nbr = draw_nbr(jax.random.fold_in(arg_keys[6], 71), 0)
    band = draw_band(jax.random.fold_in(arg_keys[6], 71), 0)
    freq = draw_freq(jax.random.fold_in(arg_keys[6], 71), 0)
    return {"eigvec": eigvec, "force": force, "bond": bond, "nbr": nbr, "band": band, "freq": freq}


def capacity_of(spectral):
    return spectral * spectral * jnp.exp(spectral) / (jnp.expm1(spectral) ** 2)


def pair_weight(own_freq, partner_freq, own_ids, partner_ids, lower_end, upper_end, broaden):
    inside = (partner_ids[:, None] >= lower_end[None, :]) & (partner_ids[:, None] < upper_end[None, :]) & (partner_ids[:, None] != own_ids[None, :])
    detune = own_freq[None, :] - partner_freq[:, None]
    lorentz = (broaden / math.pi) / (detune * detune + broaden * broaden)
    factor = (own_freq[None, :] + partner_freq[:, None]) ** 2 / (4.0 * own_freq[None, :] * partner_freq[:, None])
    return jnp.where(inside, lorentz * factor, 0.0)


def reference(eigvec, force, bond, nbr, band, freq):
    mode_count = MODE_DEV * N_MODE
    partner_span = MODE_DEV + 2 * HALF
    broaden = BROAD * (jnp.max(freq) - jnp.min(freq)) / (mode_count - 1)
    padded_freq = jnp.pad(freq, (HALF, HALF), constant_values=1.0)

    def one_block(block_index):
        mode_start = block_index * MODE_DEV
        own_columns = lax.dynamic_slice_in_dim(eigvec, mode_start, MODE_DEV, 2)

        def atom_step(atom_block, running_pair):
            atom_start = (atom_block * ATOM_DEV).astype(jnp.int32)
            eig_rows = lax.dynamic_slice_in_dim(eigvec, atom_start, ATOM_DEV, 1)
            wide_rows = jnp.pad(eig_rows, ((0, 0), (0, 0), (HALF, HALF)))
            partner_rows = lax.dynamic_slice_in_dim(wide_rows, mode_start, partner_span, 2)
            neighbours = lax.dynamic_slice_in_dim(nbr, atom_start, ATOM_DEV, 1)
            gathered = jnp.take(own_columns, neighbours, axis=1)
            force_rows = lax.dynamic_slice_in_dim(force, atom_start, ATOM_DEV, 3)
            bond_rows = lax.dynamic_slice_in_dim(bond, atom_start, ATOM_DEV, 2)
            coupling = (bond_rows[:, None, None] * force_rows[None]).astype(jnp.bfloat16)
            flux_image = jnp.einsum("kcdna,dnai->kcai", coupling.astype(jnp.float32), gathered.astype(jnp.float32)).astype(jnp.bfloat16)
            return running_pair + jnp.einsum("caj,kcai->kji", partner_rows.astype(jnp.float32), flux_image.astype(jnp.float32))

        start_pair = jnp.zeros((3, partner_span, MODE_DEV), jnp.float32)
        pair_terms = lax.fori_loop(0, N_ATOM, atom_step, start_pair)
        strength = jnp.sum(pair_terms * pair_terms, axis=0)
        own_freq = lax.dynamic_slice_in_dim(freq, mode_start, MODE_DEV)
        partner_freq = lax.dynamic_slice_in_dim(padded_freq, mode_start, partner_span)
        own_ids = mode_start + jnp.arange(MODE_DEV, dtype=jnp.int32)
        partner_ids = mode_start - HALF + jnp.arange(partner_span, dtype=jnp.int32)
        lower_end = lax.dynamic_slice_in_dim(band[0], mode_start, MODE_DEV)
        upper_end = lax.dynamic_slice_in_dim(band[1], mode_start, MODE_DEV)
        weight = pair_weight(own_freq, partner_freq, own_ids, partner_ids, lower_end, upper_end, broaden)
        return math.pi / (3.0 * own_freq * own_freq) * jnp.sum(weight * strength, axis=0)

    diffusivity = lax.map(one_block, jnp.arange(N_MODE, dtype=jnp.int32)).reshape(mode_count)
    conductivity = jnp.cumsum(capacity_of(freq) * diffusivity) / MODE_DEV
    return diffusivity, conductivity
```

```python
import functools
import math

import jax
import jax.numpy as jnp
from jax import lax
from jax.experimental import pallas as pl
from jax.experimental.pallas import tpu as pltpu
from jax.sharding import PartitionSpec as P

RIM = 128
HALF = 128
BROAD = 128
GROUP = 16
EXTRA = 16
F32 = jnp.float32
BF16 = jnp.bfloat16
VMEM = pl.BlockSpec(memory_space=pltpu.VMEM)


def iota(shape, dim):
    return lax.broadcasted_iota(jnp.int32, shape, dim)


def coupling_kernel(atoms, force_ref, bond_ref, nbr_ref, out_ref, cpl_ref):
    comps, _, slots, own = force_ref.shape
    wide = slots * GROUP
    span = own + RIM
    start = lax.axis_index("atom") * own
    offset = nbr_ref[...] - start
    offset = jnp.where(offset < -RIM, offset + atoms, offset)
    offset = jnp.where(offset >= own + RIM, offset - atoms, offset)
    place = jnp.transpose((offset - RIM).astype(F32)).astype(BF16)
    spread = jnp.where(iota((slots, wide), 1) // GROUP == iota((slots, wide), 0), 1.0, 0.0).astype(BF16)
    same = iota((GROUP, wide), 0) == iota((GROUP, wide), 1) % GROUP
    placed = jnp.dot(place, spread, preferred_element_type=F32)
    bonds = [jnp.transpose(bond_ref[k]) for k in range(comps)]
    for c in range(comps):
        for d in range(comps):
            column = jnp.transpose(force_ref[c, d])
            for k in range(comps):
                cpl_ref[(k * comps + c) * comps + d] = (bonds[k] * column).astype(BF16)
    own_ids = iota((own, wide), 0) - RIM
    halves = own // RIM
    for h in range(halves):
        rim_ids = iota((RIM, wide), 0) + (-2 * RIM if h == 0 else own - RIM)
        ids = jnp.concatenate([own_ids, rim_ids], axis=0)
        for g in range(RIM // GROUP):
            base = h * RIM + g * GROUP
            row = jnp.sum(jnp.where(same, placed[base : base + GROUP], 0.0), axis=0, keepdims=True)
            hot = jnp.where(ids == row.astype(jnp.int32), 1.0, 0.0).astype(BF16)
            part = cpl_ref[:, base : base + GROUP, :].reshape(comps**3 * GROUP, slots)
            diag = jnp.dot(part, spread, preferred_element_type=F32).reshape(comps**3, GROUP, wide)
            diag = jnp.where(same[None], diag, 0.0).astype(BF16).reshape(comps**3 * GROUP, wide)
            block = lax.dot_general(diag, hot, (((1,), (1,)), ((), ())), preferred_element_type=F32)
            block = block.astype(BF16)
            for kc in range(comps * comps):
                rows = slice(kc * RIM + g * GROUP, kc * RIM + (g + 1) * GROUP)
                for d in range(comps):
                    top = (kc * comps + d) * GROUP
                    piece = block[top : top + GROUP]
                    out_ref[h, rows, d * own : (d + 1) * own] = piece[:, :own]
                    left = comps * own + d * RIM
                    out_ref[h, rows, left : left + RIM] = piece[:, own:span]


def coupling_matrix(force, bond, nbr, atoms):
    comps, _, slots, own = force.shape
    size = comps * (own + RIM)
    return pl.pallas_call(
        functools.partial(coupling_kernel, atoms),
        out_shape=jax.ShapeDtypeStruct((own // RIM, comps * comps * RIM, size), BF16),
        in_specs=[VMEM] * 3,
        out_specs=VMEM,
        scratch_shapes=[pltpu.VMEM((comps**3, own, slots), BF16)],
        compiler_params=pltpu.CompilerParams(vmem_limit_bytes=40 * 2**20),
        cost_estimate=pl.CostEstimate(flops=4 * 10**9, bytes_accessed=6 * 10**6, transcendentals=0),
    )(force, bond, nbr)


def pair_kernel(cpl_ref, own_ref, rim_one, rim_two, halo_one, halo_two, keep_ref, send_ref, rows_ref, flux_ref):
    comps, own, modes = own_ref.shape
    depth = comps * own
    place = lax.axis_index("atom")
    odd = lax.rem(place, 2) == 1
    high = lax.rem(lax.axis_index("mode"), 2) == 1
    for h in range(2):
        rows_ref[h, 0:depth] = own_ref[...].reshape(depth, modes)
    one = rim_one[...].reshape(comps * RIM, modes)
    two = rim_two[...].reshape(comps * RIM, modes)
    rows_ref[0, depth:] = jnp.where(odd, one, two)
    rows_ref[1, depth:] = jnp.where(odd, two, one)
    for h in range(2):
        image = jnp.dot(cpl_ref[h], rows_ref[h], preferred_element_type=F32).astype(BF16)
        for k in range(comps):
            for c in range(comps):
                top = (k * comps + c) * RIM
                flux_ref[c, h * RIM : (h + 1) * RIM, k * modes : (k + 1) * modes] = image[top : top + RIM]
    flux = flux_ref[...].reshape(depth, comps * modes)
    contract = (((0,), (0,)), ((), ()))
    pairs = lax.dot_general(own_ref[...].reshape(depth, modes), flux, contract, preferred_element_type=F32)
    first = halo_one[...].reshape(depth, HALF)
    second = halo_two[...].reshape(depth, HALF)
    before = jnp.where(high, first, second)
    after = jnp.where(high, second, first)
    low_flux = jnp.concatenate([flux[:, k * modes : k * modes + HALF] for k in range(comps)], axis=1)
    high_flux = jnp.concatenate([flux[:, k * modes + HALF : (k + 1) * modes] for k in range(comps)], axis=1)
    below = lax.dot_general(before, low_flux, contract, preferred_element_type=F32)
    above = lax.dot_general(after, high_flux, contract, preferred_element_type=F32)
    lower = iota((HALF, HALF), 0) > iota((HALF, HALF), 1)
    equal = iota((HALF, HALF), 0) == iota((HALF, HALF), 1)
    second_core = odd
    for k in range(comps):
        left, middle, right = k * modes, k * modes + HALF, (k + 1) * modes
        sets = []
        for part in range(2):
            if part == 0:
                main = pairs[0:HALF, left:middle]
                low = below[:, k * HALF : (k + 1) * HALF]
                up = pairs[HALF : 2 * HALF, left:middle]
            else:
                main = pairs[HALF : 2 * HALF, middle:right]
                low = pairs[0:HALF, middle:right]
                up = above[:, k * HALF : (k + 1) * HALF]
            edge = jnp.sum(jnp.where(equal, low, 0.0), axis=0, keepdims=True)
            edge = jnp.broadcast_to(edge, (EXTRA, HALF))
            sets.append(jnp.concatenate([main, jnp.where(lower, low, up), edge], axis=0))
        keep_ref[k] = jnp.where(second_core, sets[1], sets[0])
        send_ref[k] = jnp.where(second_core, sets[0], sets[1]).astype(BF16)


def pair_parts(matrix, eigvec, rim_one, rim_two, halo_one, halo_two):
    comps, own, modes = eigvec.shape
    shape = (comps, 2 * HALF + EXTRA, HALF)
    return pl.pallas_call(
        pair_kernel,
        out_shape=(jax.ShapeDtypeStruct(shape, F32), jax.ShapeDtypeStruct(shape, BF16)),
        in_specs=[VMEM] * 6,
        out_specs=(VMEM, VMEM),
        scratch_shapes=[
            pltpu.VMEM((own // RIM, comps * (own + RIM), modes), BF16),
            pltpu.VMEM((comps, own, comps * modes), BF16),
        ],
        compiler_params=pltpu.CompilerParams(vmem_limit_bytes=40 * 2**20),
        cost_estimate=pl.CostEstimate(flops=2 * 10**9, bytes_accessed=6 * 10**6, transcendentals=0),
    )(matrix, eigvec, rim_one, rim_two, halo_one, halo_two)


def weigh_kernel(modes, count, table_ref, eta_ref, band_ref, main_one, main_two, side_one, side_two, out_ref):
    part = lax.rem(lax.axis_index("atom"), 2)
    block = lax.axis_index("mode")
    base = block * (modes // HALF) + part
    start = block * modes + part * HALF
    prev = table_ref[pl.ds(base, 1), :]
    freq = table_ref[pl.ds(base + 1, 1), :]
    following = table_ref[pl.ds(base + 2, 1), :]
    low_end = band_ref[pl.ds(part, 1), :]
    high_end = band_ref[pl.ds(part + 2, 1), :]
    eta = eta_ref[0:1, :]

    def column(row):
        return jnp.transpose(jnp.broadcast_to(row, (HALF, HALF)))

    def weight(partner_freq, partner_ids, own_ids):
        inside = (partner_ids >= low_end) & (partner_ids < high_end) & (partner_ids != own_ids)
        detune = freq - partner_freq
        lorentz = (eta / math.pi) / (detune * detune + eta * eta)
        total = freq + partner_freq
        factor = total * total / (4.0 * freq * partner_freq)
        return jnp.where(inside, lorentz * factor, 0.0)

    rows = iota((HALF, HALF), 0)
    own_ids = start + iota((HALF, HALF), 1)
    lower = rows > iota((HALF, HALF), 1)
    main_weight = weight(column(freq), start + rows, own_ids)
    side_freq = jnp.where(lower, column(prev), column(following))
    side_weight = weight(side_freq, start + rows + jnp.where(lower, -HALF, HALF), own_ids)
    edge_own = start + iota((1, HALF), 1)
    edge_weight = weight(prev, edge_own - HALF, edge_own)
    comps = main_one.shape[0]
    main_strength = jnp.zeros((HALF, HALF), F32)
    side_strength = jnp.zeros((HALF, HALF), F32)
    edge_strength = jnp.zeros((1, HALF), F32)
    for k in range(comps):
        main = main_one[k].astype(F32) + main_two[k].astype(F32)
        side = side_one[k].astype(F32) + side_two[k].astype(F32)
        main_strength += main * main
        side_strength += side[:HALF] * side[:HALF]
        edge = side[HALF : HALF + 1]
        edge_strength += edge * edge
    total = jnp.sum(main_weight * main_strength + side_weight * side_strength, axis=0, keepdims=True)
    total += edge_weight * edge_strength
    out_ref[...] = math.pi / (3.0 * freq * freq) * total


def weigh(table, eta, band, main_one, main_two, side_one, side_two, modes, count):
    return pl.pallas_call(
        functools.partial(weigh_kernel, modes, count),
        out_shape=jax.ShapeDtypeStruct((1, HALF), F32),
        in_specs=[VMEM] * 7,
        out_specs=VMEM,
        cost_estimate=pl.CostEstimate(flops=10**6, bytes_accessed=10**6, transcendentals=0),
    )(table, eta, band, main_one, main_two, side_one, side_two)


def running_kernel(own_ref, other_ref, capacity_ref, diff_ref, run_ref, total_ref):
    modes = capacity_ref.shape[1]
    odd = lax.rem(lax.axis_index("atom"), 2) == 1
    own, other = own_ref[...], other_ref[...]
    diff = jnp.concatenate([jnp.where(odd, other, own), jnp.where(odd, own, other)], axis=1)
    diff_ref[...] = diff
    carried = capacity_ref[...] * diff
    until = jnp.where(iota((modes, modes), 0) <= iota((modes, modes), 1), 1.0, 0.0)
    running = jnp.dot(
        jnp.broadcast_to(carried, (8, modes)), until, precision=lax.Precision.HIGHEST, preferred_element_type=F32
    )
    run_ref[...] = running[0:1]
    total_ref[...] = jnp.broadcast_to(running[0:1, modes - 1 : modes], total_ref.shape)


def running_sum(own, other, capacity):
    modes = capacity.shape[1]
    row = jax.ShapeDtypeStruct((1, modes), F32)
    return pl.pallas_call(
        running_kernel,
        out_shape=(row, row, jax.ShapeDtypeStruct((1, HALF), F32)),
        in_specs=[VMEM] * 3,
        out_specs=(VMEM,) * 3,
    )(own, other, capacity)


def swap(x, axis, bit):
    return lax.ppermute(x, axis, [(i, i ^ bit) for i in range(lax.axis_size(axis))])


def bits_of(axis):
    return [1 << b for b in range(lax.axis_size(axis).bit_length() - 1)]


def rounded_sum(own, other):
    total = own.astype(F32) + other.astype(F32)
    return lax.reduce_precision(total, 8, 7).astype(BF16)


def body(eigvec, force, bond, nbr, band, freq):
    domains, blocks = lax.axis_size("atom"), lax.axis_size("mode")
    comps, own, modes = eigvec.shape
    atoms, count = own * domains, modes * blocks
    place, block = lax.axis_index("atom"), lax.axis_index("mode")
    odd, high = lax.rem(place, 2), lax.rem(block, 2)

    inner = [(i, i ^ 1) for i in range(domains)]
    outer = [(i, (i + 1) % domains if i % 2 else (i - 1) % domains) for i in range(domains)]
    rim_two = lax.ppermute(lax.dynamic_slice_in_dim(eigvec, (own - RIM) * odd, RIM, 1), "atom", outer)
    rim_one = lax.ppermute(lax.dynamic_slice_in_dim(eigvec, (own - RIM) * (1 - odd), RIM, 1), "atom", inner)
    near = [(i, i ^ 1) for i in range(blocks)]
    far = [(i, i + 1 if i % 2 else i - 1) for i in range(1, blocks - 1)]
    halo_one = lax.ppermute(lax.dynamic_slice_in_dim(eigvec, (modes - HALF) * (1 - high), HALF, 2), "mode", near)
    halo_two = lax.ppermute(lax.dynamic_slice_in_dim(eigvec, (modes - HALF) * high, HALF, 2), "mode", far)

    matrix = coupling_matrix(force, bond, nbr, atoms)
    keep, send = pair_parts(matrix, eigvec, rim_one, rim_two, halo_one, halo_two)

    spectrum = freq.reshape(1, modes)
    for bit in bits_of("mode"):
        other = swap(spectrum, "mode", bit)
        upper = (block & bit) != 0
        spectrum = jnp.where(
            upper, jnp.concatenate([other, spectrum], axis=0), jnp.concatenate([spectrum, other], axis=0)
        )
    eta = BROAD * (jnp.max(spectrum) - jnp.min(spectrum)) / (count - 1)
    eta = jnp.broadcast_to(eta, (8, HALF))
    table = jnp.pad(spectrum.reshape(count // HALF, HALF), ((1, 1), (0, 0)), constant_values=1.0)
    ends = band.reshape(2 * modes // HALF, HALF)
    capacity = (freq * freq * jnp.exp(freq) / jnp.expm1(freq) ** 2).reshape(1, modes)

    both = rounded_sum(keep, swap(send, "atom", 1))
    main, side = both[:, :HALF], both[:, HALF:]
    steps = bits_of("atom")[1:]
    for step, (one, two) in enumerate(zip(steps, reversed(steps))):
        main_other, side_other = swap(main, "atom", one), swap(side, "atom", two)
        if step < len(steps) - 1:
            main, side = rounded_sum(main, main_other), rounded_sum(side, side_other)
    diff_own = weigh(table, eta, ends, main, main_other, side, side_other, modes, count)

    diff, running, total = running_sum(diff_own, swap(diff_own, "atom", 1), capacity)
    earlier = jnp.zeros_like(total)
    for bit in bits_of("mode"):
        other = swap(total, "mode", bit)
        earlier = earlier + jnp.where((block & bit) != 0, other, 0.0)
        total = total + other
    conductivity = (earlier[0, 0] + running) / modes
    return diff.reshape(modes), conductivity.reshape(modes)


def solution(mesh):
    in_specs = (
        P(None, "atom", "mode"),
        P(None, None, None, "atom"),
        P(None, None, "atom"),
        P(None, "atom"),
        P(None, "mode"),
        P("mode"),
    )
    out_specs = (P("mode"), P("mode"))
    return jax.shard_map(body, mesh=mesh, in_specs=in_specs, out_specs=out_specs, check_vma=False)
```

```python
import functools
import math

import jax
import jax.numpy as jnp
from jax import lax
from jax.experimental import pallas as pl
from jax.experimental.pallas import tpu as pltpu
from jax.sharding import PartitionSpec as P

RIM = 128
HALF = 128
BROAD = 128
GROUP = 16
EXTRA = 16
F32 = jnp.float32
BF16 = jnp.bfloat16
VMEM = pl.BlockSpec(memory_space=pltpu.VMEM)
ANY = pl.BlockSpec(memory_space=pl.ANY)
SMALL = 8 * 2**20
LARGE = 24 * 2**20


def iota(shape, dim):
    return lax.broadcasted_iota(jnp.int32, shape, dim)


def edge_kernel(eig_ref, freq_ref, inner_ref, outer_ref, near_ref, far_ref, sems):
    comps, own, modes = eig_ref.shape
    odd = lax.rem(lax.axis_index("atom"), 2)
    high = lax.rem(lax.axis_index("mode"), 2)

    def rows(flag):
        return pl.ds(pl.multiple_of(flag * (own - RIM), RIM), RIM)

    def columns(flag):
        return pl.ds(pl.multiple_of(flag * (modes - HALF), HALF), HALF)

    copies = [
        pltpu.make_async_copy(eig_ref.at[:, rows(odd), :], outer_ref, sems.at[0]),
        pltpu.make_async_copy(eig_ref.at[:, rows(1 - odd), :], inner_ref, sems.at[1]),
        pltpu.make_async_copy(eig_ref.at[:, :, columns(1 - high)], near_ref.at[:, pl.ds(0, own), :], sems.at[2]),
        pltpu.make_async_copy(eig_ref.at[:, :, columns(high)], far_ref.at[:, pl.ds(0, own), :], sems.at[3]),
    ]
    for copy in copies:
        copy.start()
    freq = freq_ref[...]
    rest = jnp.where(iota((EXTRA, HALF), 0) < EXTRA // 2, freq[:, 0:HALF], freq[:, modes - HALF : modes])
    for part in range(comps):
        piece = rest.astype(BF16)
        rest = rest - piece.astype(F32)
        near_ref[part, own : own + EXTRA, :] = piece
        far_ref[part, own : own + EXTRA, :] = piece
    for copy in copies:
        copy.wait()


def edges(eigvec, freq):
    comps, own, modes = eigvec.shape
    rim = jax.ShapeDtypeStruct((comps, RIM, modes), BF16)
    halo = jax.ShapeDtypeStruct((comps, own + EXTRA, HALF), BF16)
    return pl.pallas_call(
        edge_kernel,
        out_shape=(rim, rim, halo, halo),
        in_specs=[ANY, VMEM],
        out_specs=(VMEM,) * 4,
        scratch_shapes=[pltpu.SemaphoreType.DMA((4,))],
        compiler_params=pltpu.CompilerParams(vmem_limit_bytes=SMALL),
        cost_estimate=pl.CostEstimate(flops=10**4, bytes_accessed=10**6, transcendentals=0),
    )(eigvec, freq)


def coupling_kernel(atoms, force_hbm, bond_hbm, nbr_hbm, out_ref, force_ref, bond_ref, nbr_ref, cpl_ref, sems):
    copies = [
        pltpu.make_async_copy(nbr_hbm, nbr_ref, sems.at[0]),
        pltpu.make_async_copy(bond_hbm, bond_ref, sems.at[1]),
        pltpu.make_async_copy(force_hbm, force_ref, sems.at[2]),
    ]
    for copy in copies:
        copy.start()
    for copy in copies:
        copy.wait()
    comps, _, slots, own = force_ref.shape
    wide = slots * GROUP
    span = own + RIM
    start = lax.axis_index("atom") * own
    offset = nbr_ref[...] - start
    offset = jnp.where(offset < -RIM, offset + atoms, offset)
    offset = jnp.where(offset >= own + RIM, offset - atoms, offset)
    place = jnp.transpose((offset - RIM).astype(F32)).astype(BF16)
    spread = jnp.where(iota((slots, wide), 1) // GROUP == iota((slots, wide), 0), 1.0, 0.0).astype(BF16)
    same = iota((GROUP, wide), 0) == iota((GROUP, wide), 1) % GROUP
    placed = jnp.dot(place, spread, preferred_element_type=F32)
    bonds = [jnp.transpose(bond_ref[k]) for k in range(comps)]
    for c in range(comps):
        for d in range(comps):
            column = jnp.transpose(force_ref[c, d])
            for k in range(comps):
                cpl_ref[(k * comps + c) * comps + d] = (bonds[k] * column).astype(BF16)
    own_ids = iota((own, wide), 0) - RIM
    halves = own // RIM
    for h in range(halves):
        rim_ids = iota((RIM, wide), 0) + (-2 * RIM if h == 0 else own - RIM)
        ids = jnp.concatenate([own_ids, rim_ids], axis=0)
        for g in range(RIM // GROUP):
            base = h * RIM + g * GROUP
            row = jnp.sum(jnp.where(same, placed[base : base + GROUP], 0.0), axis=0, keepdims=True)
            hot = jnp.where(ids == row.astype(jnp.int32), 1.0, 0.0).astype(BF16)
            part = cpl_ref[:, base : base + GROUP, :].reshape(comps**3 * GROUP, slots)
            diag = jnp.dot(part, spread, preferred_element_type=F32).reshape(comps**3, GROUP, wide)
            diag = jnp.where(same[None], diag, 0.0).astype(BF16).reshape(comps**3 * GROUP, wide)
            block = lax.dot_general(diag, hot, (((1,), (1,)), ((), ())), preferred_element_type=F32)
            block = block.astype(BF16)
            for kc in range(comps * comps):
                rows = slice(kc * RIM + g * GROUP, kc * RIM + (g + 1) * GROUP)
                for d in range(comps):
                    top = (kc * comps + d) * GROUP
                    piece = block[top : top + GROUP]
                    out_ref[h, rows, d * own : (d + 1) * own] = piece[:, :own]
                    left = comps * own + d * RIM
                    out_ref[h, rows, left : left + RIM] = piece[:, own:span]


def coupling_matrix(force, bond, nbr, atoms):
    comps, _, slots, own = force.shape
    size = comps * (own + RIM)
    return pl.pallas_call(
        functools.partial(coupling_kernel, atoms),
        out_shape=jax.ShapeDtypeStruct((own // RIM, comps * comps * RIM, size), BF16),
        in_specs=[ANY] * 3,
        out_specs=VMEM,
        scratch_shapes=[
            pltpu.VMEM(force.shape, force.dtype),
            pltpu.VMEM(bond.shape, bond.dtype),
            pltpu.VMEM(nbr.shape, nbr.dtype),
            pltpu.VMEM((comps**3, own, slots), BF16),
            pltpu.SemaphoreType.DMA((3,)),
        ],
        compiler_params=pltpu.CompilerParams(vmem_limit_bytes=LARGE),
        cost_estimate=pl.CostEstimate(flops=4 * 10**9, bytes_accessed=6 * 10**6, transcendentals=0),
    )(force, bond, nbr)


def pair_kernel(cpl_ref, own_ref, rim_one, rim_two, halo_one, halo_two, keep_ref, send_ref, rows_ref, flux_ref):
    comps, own, modes = own_ref.shape
    depth = comps * own
    place = lax.axis_index("atom")
    odd = lax.rem(place, 2) == 1
    high = lax.rem(lax.axis_index("mode"), 2) == 1
    for h in range(2):
        rows_ref[h, 0:depth] = own_ref[...].reshape(depth, modes)
    one = rim_one[...].reshape(comps * RIM, modes)
    two = rim_two[...].reshape(comps * RIM, modes)
    rows_ref[0, depth:] = jnp.where(odd, one, two)
    rows_ref[1, depth:] = jnp.where(odd, two, one)
    for h in range(2):
        image = jnp.dot(cpl_ref[h], rows_ref[h], preferred_element_type=F32).astype(BF16)
        for k in range(comps):
            for c in range(comps):
                top = (k * comps + c) * RIM
                flux_ref[c, h * RIM : (h + 1) * RIM, k * modes : (k + 1) * modes] = image[top : top + RIM]
    flux = flux_ref[...].reshape(depth, comps * modes)
    contract = (((0,), (0,)), ((), ()))
    pairs = lax.dot_general(own_ref[...].reshape(depth, modes), flux, contract, preferred_element_type=F32)
    first = halo_one[:, 0:own, :].reshape(depth, HALF)
    second = halo_two[:, 0:own, :].reshape(depth, HALF)
    before = jnp.where(high, first, second)
    after = jnp.where(high, second, first)
    low_flux = jnp.concatenate([flux[:, k * modes : k * modes + HALF] for k in range(comps)], axis=1)
    high_flux = jnp.concatenate([flux[:, k * modes + HALF : (k + 1) * modes] for k in range(comps)], axis=1)
    below = lax.dot_general(before, low_flux, contract, preferred_element_type=F32)
    above = lax.dot_general(after, high_flux, contract, preferred_element_type=F32)
    lower = iota((HALF, HALF), 0) > iota((HALF, HALF), 1)
    equal = iota((HALF, HALF), 0) == iota((HALF, HALF), 1)
    second_core = odd
    for k in range(comps):
        left, middle, right = k * modes, k * modes + HALF, (k + 1) * modes
        sets = []
        for part in range(2):
            if part == 0:
                main = pairs[0:HALF, left:middle]
                low = below[:, k * HALF : (k + 1) * HALF]
                up = pairs[HALF : 2 * HALF, left:middle]
            else:
                main = pairs[HALF : 2 * HALF, middle:right]
                low = pairs[0:HALF, middle:right]
                up = above[:, k * HALF : (k + 1) * HALF]
            edge = jnp.sum(jnp.where(equal, low, 0.0), axis=0, keepdims=True)
            edge = jnp.broadcast_to(edge, (EXTRA, HALF))
            sets.append(jnp.concatenate([main, jnp.where(lower, low, up), edge], axis=0))
        keep_ref[k] = jnp.where(second_core, sets[1], sets[0])
        send_ref[k] = jnp.where(second_core, sets[0], sets[1]).astype(BF16)


def pair_parts(matrix, eigvec, rim_one, rim_two, halo_one, halo_two):
    comps, own, modes = eigvec.shape
    shape = (comps, 2 * HALF + EXTRA, HALF)
    return pl.pallas_call(
        pair_kernel,
        out_shape=(jax.ShapeDtypeStruct(shape, F32), jax.ShapeDtypeStruct(shape, BF16)),
        in_specs=[VMEM] * 6,
        out_specs=(VMEM, VMEM),
        scratch_shapes=[
            pltpu.VMEM((own // RIM, comps * (own + RIM), modes), BF16),
            pltpu.VMEM((comps, own, comps * modes), BF16),
        ],
        compiler_params=pltpu.CompilerParams(vmem_limit_bytes=LARGE),
        cost_estimate=pl.CostEstimate(flops=2 * 10**9, bytes_accessed=6 * 10**6, transcendentals=0),
    )(matrix, eigvec, rim_one, rim_two, halo_one, halo_two)


def halo_freq(halo_ref, own):
    total = jnp.zeros((EXTRA, HALF), F32)
    for part in reversed(range(halo_ref.shape[0])):
        total = halo_ref[part, own : own + EXTRA, :].astype(F32) + total
    return total[0:1], total[EXTRA // 2 : EXTRA // 2 + 1]


def ends_kernel(own, freq_ref, halo_ref, out_ref):
    modes = freq_ref.shape[1]
    rows = (freq_ref[:, 0:HALF], freq_ref[:, modes - HALF : modes], *halo_freq(halo_ref, own))
    least = jnp.min(functools.reduce(jnp.minimum, rows), axis=1, keepdims=True)
    most = jnp.max(functools.reduce(jnp.maximum, rows), axis=1, keepdims=True)
    out_ref[...] = jnp.where(iota(out_ref.shape, 0) < 4, least, most)


def weigh_kernel(count, own, freq_ref, ends_ref, band_ref, halo_one, halo_two, main_one, main_two, side_one, side_two, out_ref):
    comps = main_one.shape[0]
    modes = freq_ref.shape[1]
    second = lax.rem(lax.axis_index("atom"), 2) == 1
    high = lax.rem(lax.axis_index("mode"), 2) == 1
    shift = jnp.where(second, HALF, 0)
    start = lax.axis_index("mode") * modes + shift
    (one_first, one_last), (two_first, two_last) = halo_freq(halo_one, own), halo_freq(halo_two, own)
    one, two = jnp.where(high, one_last, one_first), jnp.where(high, two_first, two_last)
    outside = jnp.where(high == second, two, one)
    inside = jnp.where(second, freq_ref[:, 0:HALF], freq_ref[:, HALF:modes])
    freq = jnp.where(second, freq_ref[:, HALF:modes], freq_ref[:, 0:HALF])
    prev = jnp.where(second, inside, outside)
    following = jnp.where(second, outside, inside)
    prev = jnp.where(start == 0, 1.0, prev)
    following = jnp.where(start == count - HALF, 1.0, following)
    band = jnp.where(second, band_ref[:, HALF:modes], band_ref[:, 0:HALF])
    low_end, high_end = band[0:1], band[1:2]
    eta = BROAD * (ends_ref[7:8, :] - ends_ref[0:1, :]) / (count - 1)

    def column(row):
        return jnp.transpose(jnp.broadcast_to(row, (HALF, HALF)))

    def weight(partner_freq, partner_ids, own_ids):
        within = (partner_ids >= low_end) & (partner_ids < high_end) & (partner_ids != own_ids)
        detune = freq - partner_freq
        total = freq + partner_freq
        scale = (eta / math.pi) * (total * total)
        value = scale / ((detune * detune + eta * eta) * (4.0 * freq * partner_freq))
        return jnp.where(within, value, 0.0)

    rows = iota((HALF, HALF), 0)
    own_ids = start + iota((HALF, HALF), 1)
    lower = rows > iota((HALF, HALF), 1)
    main_weight = weight(column(freq), start + rows, own_ids)
    side_freq = jnp.where(lower, column(prev), column(following))
    side_weight = weight(side_freq, start + rows + jnp.where(lower, -HALF, HALF), own_ids)
    edge_own = start + iota((1, HALF), 1)
    edge_weight = weight(prev, edge_own - HALF, edge_own)
    main_strength = jnp.zeros((HALF, HALF), F32)
    side_strength = jnp.zeros((HALF, HALF), F32)
    edge_strength = jnp.zeros((1, HALF), F32)
    for k in range(comps):
        main = main_one[k].astype(F32) + main_two[k].astype(F32)
        side = side_one[k].astype(F32) + side_two[k].astype(F32)
        main_strength += main * main
        side_strength += side[:HALF] * side[:HALF]
        edge = side[HALF : HALF + 1]
        edge_strength += edge * edge
    total = jnp.sum(main_weight * main_strength + side_weight * side_strength, axis=0, keepdims=True)
    total += edge_weight * edge_strength
    diff = math.pi / (3.0 * freq * freq) * total
    grown = jnp.exp(freq)
    carried = freq * freq * grown / ((grown - 1.0) * (grown - 1.0)) * diff
    out_ref[0:1] = diff
    out_ref[1:2] = carried
    out_ref[2:8] = jnp.broadcast_to(jnp.sum(carried, axis=1, keepdims=True), (6, HALF))


def local_call(kernel, out_shape, *operands):
    return pl.pallas_call(
        kernel,
        out_shape=out_shape,
        in_specs=[VMEM] * len(operands),
        out_specs=jax.tree.map(lambda _: VMEM, out_shape),
        compiler_params=pltpu.CompilerParams(vmem_limit_bytes=SMALL),
        cost_estimate=pl.CostEstimate(flops=10**6, bytes_accessed=10**6, transcendentals=0),
    )(*operands)


def running_kernel(modes, own_ref, other_ref, diff_ref, run_ref):
    odd = lax.rem(lax.axis_index("atom"), 2) == 1
    own, other = own_ref[...], other_ref[...]
    whole = jnp.concatenate([jnp.where(odd, other, own), jnp.where(odd, own, other)], axis=1)
    diff_ref[...] = whole[0:1]
    until = jnp.where(iota((modes, modes), 0) <= iota((modes, modes), 1), 1.0, 0.0)
    running = jnp.dot(whole, until, precision=lax.Precision.HIGHEST, preferred_element_type=F32)
    run_ref[...] = running[1:2]


def last_kernel(run_ref, earlier_ref, out_ref):
    modes = run_ref.shape[1]
    out_ref[...] = (run_ref[...] + earlier_ref[0:1, 0:1]) / modes


def swap(x, axis, bit):
    return lax.ppermute(x, axis, [(i, i ^ bit) for i in range(lax.axis_size(axis))])


def bits_of(axis):
    return [1 << b for b in range(lax.axis_size(axis).bit_length() - 1)]


def rounded_sum(own, other):
    total = own.astype(F32) + other.astype(F32)
    return lax.reduce_precision(total, 8, 7).astype(BF16)


def body(eigvec, force, bond, nbr, band, freq):
    domains, blocks = lax.axis_size("atom"), lax.axis_size("mode")
    comps, own, modes = eigvec.shape
    atoms, count = own * domains, modes * blocks
    block = lax.axis_index("mode")
    freq_row = freq.reshape(1, modes)

    inner = [(i, i ^ 1) for i in range(domains)]
    outer = [(i, (i + 1) % domains if i % 2 else (i - 1) % domains) for i in range(domains)]
    near = [(i, i ^ 1) for i in range(blocks)]
    far = [(i, i + 1 if i % 2 else i - 1) for i in range(1, blocks - 1)]
    inner_edge, outer_edge, near_edge, far_edge = edges(eigvec, freq_row)
    rim_two = lax.ppermute(outer_edge, "atom", outer)
    rim_one = lax.ppermute(inner_edge, "atom", inner)
    halo_one = lax.ppermute(near_edge, "mode", near)
    halo_two = lax.ppermute(far_edge, "mode", far)

    matrix = coupling_matrix(force, bond, nbr, atoms)
    keep, send = pair_parts(matrix, eigvec, rim_one, rim_two, halo_one, halo_two)

    tile = jax.ShapeDtypeStruct((8, HALF), F32)
    row = jax.ShapeDtypeStruct((1, modes), F32)
    ends = local_call(functools.partial(ends_kernel, own), tile, freq_row, halo_one)

    both = rounded_sum(keep, swap(send, "atom", 1))
    main, side = both[:, :HALF], both[:, HALF:]
    steps = bits_of("atom")[1:]
    for step, (one, two) in enumerate(zip(steps, reversed(steps))):
        main_other, side_other = swap(main, "atom", one), swap(side, "atom", two)
        if step < len(steps) - 1:
            main = rounded_sum(main, main_other)
            if step == 0:
                ends, main = lax.optimization_barrier((ends, main))
            side = rounded_sum(side, side_other)
    for bit in bits_of("mode")[1:]:
        other = swap(ends, "mode", bit)
        ends = jnp.where(iota((8, HALF), 0) < 4, jnp.minimum(ends, other), jnp.maximum(ends, other))
    summary = local_call(
        functools.partial(weigh_kernel, count, own),
        tile, freq_row, ends, band, halo_one, halo_two, main, main_other, side, side_other,
    )

    other = swap(summary, "atom", 1)
    diff, running = local_call(functools.partial(running_kernel, modes), (row, row), summary, other)
    total = summary + other
    earlier = jnp.zeros_like(total)
    for bit in bits_of("mode"):
        other = swap(total, "mode", bit)
        earlier = earlier + jnp.where((block & bit) != 0, other, 0.0)
        total = total + other
    conductivity = local_call(last_kernel, row, running, earlier[2:3])
    return diff.reshape(modes), conductivity.reshape(modes)


def solution(mesh):
    in_specs = (
        P(None, "atom", "mode"),
        P(None, None, None, "atom"),
        P(None, None, "atom"),
        P(None, "atom"),
        P(None, "mode"),
        P("mode"),
    )
    out_specs = (P("mode"), P("mode"))
    return jax.shard_map(body, mesh=mesh, in_specs=in_specs, out_specs=out_specs, check_vma=False)
```

```python
import functools
import math

import jax
import jax.numpy as jnp
from jax import lax
from jax.experimental import pallas as pl
from jax.experimental.pallas import tpu as pltpu
from jax.sharding import PartitionSpec as P

RIM = 128
HALF = 128
BROAD = 128
GROUP = 16
EXTRA = 16
F32 = jnp.float32
BF16 = jnp.bfloat16
VMEM = pl.BlockSpec(memory_space=pltpu.VMEM)
HBM = pl.BlockSpec(memory_space=pltpu.HBM)
SMALL = 8 * 2**20
LARGE = 24 * 2**20


def iota(shape, dim):
    return lax.broadcasted_iota(jnp.int32, shape, dim)


def stage_kernel(eig_hbm, freq_hbm, force_hbm, bond_hbm, nbr_hbm, *refs):
    inner_ref, outer_ref, near_ref, far_ref, freq_ref, force_ref, bond_ref, nbr_ref, sems = refs
    comps, own, modes = eig_hbm.shape
    odd = lax.rem(lax.axis_index("atom"), 2)
    high = lax.rem(lax.axis_index("mode"), 2)

    def rows(flag):
        return pl.ds(pl.multiple_of(flag * (own - RIM), RIM), RIM)

    def columns(flag):
        return pl.ds(pl.multiple_of(flag * (modes - HALF), HALF), HALF)

    moves = (
        (freq_hbm, freq_ref),
        (eig_hbm.at[:, rows(odd), :], outer_ref),
        (eig_hbm.at[:, rows(1 - odd), :], inner_ref),
        (eig_hbm.at[:, :, columns(1 - high)], near_ref.at[:, pl.ds(0, own), :]),
        (eig_hbm.at[:, :, columns(high)], far_ref.at[:, pl.ds(0, own), :]),
        (nbr_hbm, nbr_ref),
        (bond_hbm, bond_ref),
        (force_hbm, force_ref),
    )
    copies = [pltpu.make_async_copy(*move, sems.at[i]) for i, move in enumerate(moves)]
    for copy in copies:
        copy.start()
    copies[0].wait()
    freq = freq_ref[...]
    rest = jnp.where(iota((EXTRA, HALF), 0) < EXTRA // 2, freq[:, 0:HALF], freq[:, modes - HALF : modes])
    for part in range(comps):
        piece = rest.astype(BF16)
        rest = rest - piece.astype(F32)
        near_ref[part, own : own + EXTRA, :] = piece
        far_ref[part, own : own + EXTRA, :] = piece
    for copy in copies[1:]:
        copy.wait()


def stage(eigvec, freq, force, bond, nbr):
    comps, own, modes = eigvec.shape
    rim = jax.ShapeDtypeStruct((comps, RIM, modes), BF16)
    halo = jax.ShapeDtypeStruct((comps, own + EXTRA, HALF), BF16)
    same = [jax.ShapeDtypeStruct(x.shape, x.dtype) for x in (freq, force, bond, nbr)]
    return pl.pallas_call(
        stage_kernel,
        out_shape=(rim, rim, halo, halo, *same),
        in_specs=[HBM] * 5,
        out_specs=(VMEM,) * 8,
        scratch_shapes=[pltpu.SemaphoreType.DMA((8,))],
        compiler_params=pltpu.CompilerParams(vmem_limit_bytes=SMALL),
        cost_estimate=pl.CostEstimate(flops=10**4, bytes_accessed=10**6, transcendentals=0),
    )(eigvec, freq, force, bond, nbr)


def coupling_kernel(atoms, force_ref, bond_ref, nbr_ref, out_ref, cpl_ref):
    comps, _, slots, own = force_ref.shape
    wide = slots * GROUP
    span = own + RIM
    start = lax.axis_index("atom") * own
    offset = nbr_ref[...] - start
    offset = jnp.where(offset < -RIM, offset + atoms, offset)
    offset = jnp.where(offset >= own + RIM, offset - atoms, offset)
    place = jnp.transpose((offset - RIM).astype(F32)).astype(BF16)
    spread = jnp.where(iota((slots, wide), 1) // GROUP == iota((slots, wide), 0), 1.0, 0.0).astype(BF16)
    same = iota((GROUP, wide), 0) == iota((GROUP, wide), 1) % GROUP
    placed = jnp.dot(place, spread, preferred_element_type=F32)
    bonds = [jnp.transpose(bond_ref[k]) for k in range(comps)]
    for c in range(comps):
        for d in range(comps):
            column = jnp.transpose(force_ref[c, d])
            for k in range(comps):
                cpl_ref[(k * comps + c) * comps + d] = (bonds[k] * column).astype(BF16)
    own_ids = iota((own, wide), 0) - RIM
    halves = own // RIM
    for h in range(halves):
        rim_ids = iota((RIM, wide), 0) + (-2 * RIM if h == 0 else own - RIM)
        ids = jnp.concatenate([own_ids, rim_ids], axis=0)
        for g in range(RIM // GROUP):
            base = h * RIM + g * GROUP
            row = jnp.sum(jnp.where(same, placed[base : base + GROUP], 0.0), axis=0, keepdims=True)
            hot = jnp.where(ids == row.astype(jnp.int32), 1.0, 0.0).astype(BF16)
            part = cpl_ref[:, base : base + GROUP, :].reshape(comps**3 * GROUP, slots)
            diag = jnp.dot(part, spread, preferred_element_type=F32).reshape(comps**3, GROUP, wide)
            diag = jnp.where(same[None], diag, 0.0).astype(BF16).reshape(comps**3 * GROUP, wide)
            block = lax.dot_general(diag, hot, (((1,), (1,)), ((), ())), preferred_element_type=F32)
            block = block.astype(BF16)
            for kc in range(comps * comps):
                rows = slice(kc * RIM + g * GROUP, kc * RIM + (g + 1) * GROUP)
                for d in range(comps):
                    top = (kc * comps + d) * GROUP
                    piece = block[top : top + GROUP]
                    out_ref[h, rows, d * own : (d + 1) * own] = piece[:, :own]
                    left = comps * own + d * RIM
                    out_ref[h, rows, left : left + RIM] = piece[:, own:span]


def coupling_matrix(force, bond, nbr, atoms):
    comps, _, slots, own = force.shape
    size = comps * (own + RIM)
    return pl.pallas_call(
        functools.partial(coupling_kernel, atoms),
        out_shape=jax.ShapeDtypeStruct((own // RIM, comps * comps * RIM, size), BF16),
        in_specs=[VMEM] * 3,
        out_specs=VMEM,
        scratch_shapes=[pltpu.VMEM((comps**3, own, slots), BF16)],
        compiler_params=pltpu.CompilerParams(vmem_limit_bytes=LARGE),
        cost_estimate=pl.CostEstimate(flops=4 * 10**9, bytes_accessed=6 * 10**6, transcendentals=0),
    )(force, bond, nbr)


def pair_kernel(cpl_ref, own_ref, rim_one, rim_two, halo_one, halo_two, keep_ref, send_ref, rows_ref, flux_ref):
    comps, own, modes = own_ref.shape
    depth = comps * own
    place = lax.axis_index("atom")
    odd = lax.rem(place, 2) == 1
    high = lax.rem(lax.axis_index("mode"), 2) == 1
    for h in range(2):
        rows_ref[h, 0:depth] = own_ref[...].reshape(depth, modes)
    one = rim_one[...].reshape(comps * RIM, modes)
    two = rim_two[...].reshape(comps * RIM, modes)
    rows_ref[0, depth:] = jnp.where(odd, one, two)
    rows_ref[1, depth:] = jnp.where(odd, two, one)
    for h in range(2):
        image = jnp.dot(cpl_ref[h], rows_ref[h], preferred_element_type=F32).astype(BF16)
        for k in range(comps):
            for c in range(comps):
                top = (k * comps + c) * RIM
                flux_ref[c, h * RIM : (h + 1) * RIM, k * modes : (k + 1) * modes] = image[top : top + RIM]
    flux = flux_ref[...].reshape(depth, comps * modes)
    contract = (((0,), (0,)), ((), ()))
    pairs = lax.dot_general(own_ref[...].reshape(depth, modes), flux, contract, preferred_element_type=F32)
    first = halo_one[:, 0:own, :].reshape(depth, HALF)
    second = halo_two[:, 0:own, :].reshape(depth, HALF)
    before = jnp.where(high, first, second)
    after = jnp.where(high, second, first)
    low_flux = jnp.concatenate([flux[:, k * modes : k * modes + HALF] for k in range(comps)], axis=1)
    high_flux = jnp.concatenate([flux[:, k * modes + HALF : (k + 1) * modes] for k in range(comps)], axis=1)
    below = lax.dot_general(before, low_flux, contract, preferred_element_type=F32)
    above = lax.dot_general(after, high_flux, contract, preferred_element_type=F32)
    lower = iota((HALF, HALF), 0) > iota((HALF, HALF), 1)
    equal = iota((HALF, HALF), 0) == iota((HALF, HALF), 1)
    second_core = odd
    for k in range(comps):
        left, middle, right = k * modes, k * modes + HALF, (k + 1) * modes
        sets = []
        for part in range(2):
            if part == 0:
                main = pairs[0:HALF, left:middle]
                low = below[:, k * HALF : (k + 1) * HALF]
                up = pairs[HALF : 2 * HALF, left:middle]
            else:
                main = pairs[HALF : 2 * HALF, middle:right]
                low = pairs[0:HALF, middle:right]
                up = above[:, k * HALF : (k + 1) * HALF]
            edge = jnp.sum(jnp.where(equal, low, 0.0), axis=0, keepdims=True)
            edge = jnp.broadcast_to(edge, (EXTRA, HALF))
            sets.append(jnp.concatenate([main, jnp.where(lower, low, up), edge], axis=0))
        keep_ref[k] = jnp.where(second_core, sets[1], sets[0])
        send_ref[k] = jnp.where(second_core, sets[0], sets[1]).astype(BF16)


def pair_parts(matrix, eigvec, rim_one, rim_two, halo_one, halo_two):
    comps, own, modes = eigvec.shape
    shape = (comps, 2 * HALF + EXTRA, HALF)
    return pl.pallas_call(
        pair_kernel,
        out_shape=(jax.ShapeDtypeStruct(shape, F32), jax.ShapeDtypeStruct(shape, BF16)),
        in_specs=[VMEM] * 6,
        out_specs=(VMEM, VMEM),
        scratch_shapes=[
            pltpu.VMEM((own // RIM, comps * (own + RIM), modes), BF16),
            pltpu.VMEM((comps, own, comps * modes), BF16),
        ],
        compiler_params=pltpu.CompilerParams(vmem_limit_bytes=LARGE),
        cost_estimate=pl.CostEstimate(flops=2 * 10**9, bytes_accessed=6 * 10**6, transcendentals=0),
    )(matrix, eigvec, rim_one, rim_two, halo_one, halo_two)


def halo_freq(halo_ref, own):
    total = jnp.zeros((EXTRA, HALF), F32)
    for part in reversed(range(halo_ref.shape[0])):
        total = halo_ref[part, own : own + EXTRA, :].astype(F32) + total
    return total[0:1], total[EXTRA // 2 : EXTRA // 2 + 1]


def ends_kernel(own, freq_ref, halo_ref, out_ref):
    modes = freq_ref.shape[1]
    rows = (freq_ref[:, 0:HALF], freq_ref[:, modes - HALF : modes], *halo_freq(halo_ref, own))
    least = jnp.min(functools.reduce(jnp.minimum, rows), axis=1, keepdims=True)
    most = jnp.max(functools.reduce(jnp.maximum, rows), axis=1, keepdims=True)
    out_ref[...] = jnp.where(iota(out_ref.shape, 0) < 4, least, most)


def weigh_kernel(count, own, freq_ref, ends_ref, band_ref, halo_one, halo_two, pair_one, pair_two, out_ref):
    comps = pair_one.shape[0]
    modes = freq_ref.shape[1]
    second = lax.rem(lax.axis_index("atom"), 2) == 1
    high = lax.rem(lax.axis_index("mode"), 2) == 1
    shift = jnp.where(second, HALF, 0)
    start = lax.axis_index("mode") * modes + shift
    (one_first, one_last), (two_first, two_last) = halo_freq(halo_one, own), halo_freq(halo_two, own)
    one, two = jnp.where(high, one_last, one_first), jnp.where(high, two_first, two_last)
    outside = jnp.where(high == second, two, one)
    inside = jnp.where(second, freq_ref[:, 0:HALF], freq_ref[:, HALF:modes])
    freq = jnp.where(second, freq_ref[:, HALF:modes], freq_ref[:, 0:HALF])
    prev = jnp.where(second, inside, outside)
    following = jnp.where(second, outside, inside)
    prev = jnp.where(start == 0, 1.0, prev)
    following = jnp.where(start == count - HALF, 1.0, following)
    band = jnp.where(second, band_ref[:, HALF:modes], band_ref[:, 0:HALF])
    low_end, high_end = band[0:1], band[1:2]
    eta = BROAD * (ends_ref[7:8, :] - ends_ref[0:1, :]) / (count - 1)

    def column(row):
        return jnp.transpose(jnp.broadcast_to(row, (HALF, HALF)))

    def weight(partner_freq, partner_ids, own_ids):
        within = (partner_ids >= low_end) & (partner_ids < high_end) & (partner_ids != own_ids)
        detune = freq - partner_freq
        total = freq + partner_freq
        scale = (eta / math.pi) * (total * total)
        value = scale / ((detune * detune + eta * eta) * (4.0 * freq * partner_freq))
        return jnp.where(within, value, 0.0)

    rows = iota((HALF, HALF), 0)
    own_ids = start + iota((HALF, HALF), 1)
    lower = rows > iota((HALF, HALF), 1)
    main_weight = weight(column(freq), start + rows, own_ids)
    side_freq = jnp.where(lower, column(prev), column(following))
    side_weight = weight(side_freq, start + rows + jnp.where(lower, -HALF, HALF), own_ids)
    edge_own = start + iota((1, HALF), 1)
    edge_weight = weight(prev, edge_own - HALF, edge_own)
    main_strength = jnp.zeros((HALF, HALF), F32)
    side_strength = jnp.zeros((HALF, HALF), F32)
    edge_strength = jnp.zeros((1, HALF), F32)
    for k in range(comps):
        pair = pair_one[k].astype(F32) + pair_two[k].astype(F32)
        main, side, edge = pair[:HALF], pair[HALF : 2 * HALF], pair[2 * HALF : 2 * HALF + 1]
        main_strength += main * main
        side_strength += side * side
        edge_strength += edge * edge
    total = jnp.sum(main_weight * main_strength + side_weight * side_strength, axis=0, keepdims=True)
    total += edge_weight * edge_strength
    diff = math.pi / (3.0 * freq * freq) * total
    grown = jnp.exp(freq)
    carried = freq * freq * grown / ((grown - 1.0) * (grown - 1.0)) * diff
    out_ref[0:1] = diff
    out_ref[1:2] = carried
    out_ref[2:8] = jnp.broadcast_to(jnp.sum(carried, axis=1, keepdims=True), (6, HALF))


def local_call(kernel, out_shape, *operands):
    return pl.pallas_call(
        kernel,
        out_shape=out_shape,
        in_specs=[VMEM] * len(operands),
        out_specs=jax.tree.map(lambda _: VMEM, out_shape),
        compiler_params=pltpu.CompilerParams(vmem_limit_bytes=SMALL),
        cost_estimate=pl.CostEstimate(flops=10**6, bytes_accessed=10**6, transcendentals=0),
    )(*operands)


def running_kernel(modes, own_ref, other_ref, diff_ref, run_ref):
    odd = lax.rem(lax.axis_index("atom"), 2) == 1
    own, other = own_ref[...], other_ref[...]
    whole = jnp.concatenate([jnp.where(odd, other, own), jnp.where(odd, own, other)], axis=1)
    diff_ref[...] = whole[0:1]
    until = jnp.where(iota((modes, modes), 0) <= iota((modes, modes), 1), 1.0, 0.0)
    running = jnp.dot(whole, until, precision=lax.Precision.HIGHEST, preferred_element_type=F32)
    run_ref[...] = running[1:2]


def last_kernel(run_ref, earlier_ref, out_ref):
    modes = run_ref.shape[1]
    out_ref[...] = (run_ref[...] + earlier_ref[0:1, 0:1]) / modes


def swap(x, axis, bit):
    return lax.ppermute(x, axis, [(i, i ^ bit) for i in range(lax.axis_size(axis))])


def bits_of(axis):
    return [1 << b for b in range(lax.axis_size(axis).bit_length() - 1)]


def rounded_sum(own, other):
    total = own.astype(F32) + other.astype(F32)
    return lax.reduce_precision(total, 8, 7).astype(BF16)


def body(eigvec, force, bond, nbr, band, freq):
    domains, blocks = lax.axis_size("atom"), lax.axis_size("mode")
    comps, own, modes = eigvec.shape
    atoms, count = own * domains, modes * blocks
    block = lax.axis_index("mode")
    staged = stage(eigvec, freq.reshape(1, modes), force, bond, nbr)
    inner_edge, outer_edge, near_edge, far_edge, freq_row, force, bond, nbr = staged

    inner = [(i, i ^ 1) for i in range(domains)]
    outer = [(i, (i + 1) % domains if i % 2 else (i - 1) % domains) for i in range(domains)]
    near = [(i, i ^ 1) for i in range(blocks)]
    far = [(i, i + 1 if i % 2 else i - 1) for i in range(1, blocks - 1)]
    rim_two = lax.ppermute(outer_edge, "atom", outer)
    rim_one = lax.ppermute(inner_edge, "atom", inner)
    halo_one = lax.ppermute(near_edge, "mode", near)
    halo_two = lax.ppermute(far_edge, "mode", far)

    matrix = coupling_matrix(force, bond, nbr, atoms)
    keep, send = pair_parts(matrix, eigvec, rim_one, rim_two, halo_one, halo_two)

    tile = jax.ShapeDtypeStruct((8, HALF), F32)
    row = jax.ShapeDtypeStruct((1, modes), F32)
    ends = local_call(functools.partial(ends_kernel, own), tile, freq_row, halo_one)

    total = rounded_sum(keep, swap(send, "atom", 1))
    steps = bits_of("atom")[1:]
    for step, (one, two) in enumerate(zip(steps, reversed(steps))):
        total_other = lax.ppermute(total, "atom", [(i, i ^ (two if i % 2 else one)) for i in range(domains)])
        if step < len(steps) - 1:
            total = rounded_sum(total, total_other)
            if step == 0:
                ends, total = lax.optimization_barrier((ends, total))
    for bit in bits_of("mode")[1:]:
        other = swap(ends, "mode", bit)
        ends = jnp.where(iota((8, HALF), 0) < 4, jnp.minimum(ends, other), jnp.maximum(ends, other))
    summary = local_call(
        functools.partial(weigh_kernel, count, own),
        tile, freq_row, ends, band, halo_one, halo_two, total, total_other,
    )

    other = swap(summary, "atom", 1)
    diff, running = local_call(functools.partial(running_kernel, modes), (row, row), summary, other)
    total = summary + other
    earlier = jnp.zeros_like(total)
    for bit in bits_of("mode"):
        other = swap(total, "mode", bit)
        earlier = earlier + jnp.where((block & bit) != 0, other, 0.0)
        total = total + other
    conductivity = local_call(last_kernel, row, running, earlier[2:3])
    return diff.reshape(modes), conductivity.reshape(modes)


def solution(mesh):
    in_specs = (
        P(None, "atom", "mode"),
        P(None, None, None, "atom"),
        P(None, None, "atom"),
        P(None, "atom"),
        P(None, "mode"),
        P("mode"),
    )
    out_specs = (P("mode"), P("mode"))
    return jax.shard_map(body, mesh=mesh, in_specs=in_specs, out_specs=out_specs, check_vma=False)
```

```python
import functools
import math

import jax
import jax.numpy as jnp
from jax import lax
from jax.experimental import pallas as pl
from jax.experimental.pallas import tpu as pltpu
from jax.sharding import PartitionSpec as P

RIM = 128
HALF = 128
BROAD = 128
GROUP = 16
EXTRA = 16
F32 = jnp.float32
BF16 = jnp.bfloat16
VMEM = pl.BlockSpec(memory_space=pltpu.VMEM)
HBM = pl.BlockSpec(memory_space=pltpu.HBM)
SMALL = 8 * 2**20
COST = 10**10
LARGE = 24 * 2**20


def iota(shape, dim):
    return lax.broadcasted_iota(jnp.int32, shape, dim)


def rim_kernel(eig_ref, inner_ref, outer_ref, sems):
    own = eig_ref.shape[1]
    odd = lax.rem(lax.axis_index("atom"), 2)
    copies = []
    for place, (flag, ref) in enumerate(((odd, outer_ref), (1 - odd, inner_ref))):
        rows = pl.ds(pl.multiple_of(flag * (own - RIM), RIM), RIM)
        copies.append(pltpu.make_async_copy(eig_ref.at[:, rows, :], ref, sems.at[place]))
    for copy in copies:
        copy.start()
    for copy in copies:
        copy.wait()


def halo_kernel(eig_ref, freq_ref, near_ref, far_ref, sems):
    comps, own, modes = eig_ref.shape
    high = lax.rem(lax.axis_index("mode"), 2)
    copies = []
    for place, (flag, ref) in enumerate(((1 - high, near_ref), (high, far_ref))):
        columns = pl.ds(pl.multiple_of(flag * (modes - HALF), HALF), HALF)
        target = ref.at[:, pl.ds(0, own), :]
        copies.append(pltpu.make_async_copy(eig_ref.at[:, :, columns], target, sems.at[place]))
    for copy in copies:
        copy.start()
    freq = freq_ref[...]
    rest = jnp.where(iota((EXTRA, HALF), 0) < EXTRA // 2, freq[:, 0:HALF], freq[:, modes - HALF : modes])
    for part in range(comps):
        piece = rest.astype(BF16)
        rest = rest - piece.astype(F32)
        near_ref[part, own : own + EXTRA, :] = piece
        far_ref[part, own : own + EXTRA, :] = piece
    for copy in copies:
        copy.wait()


def edge_call(kernel, shape, cost, *operands):
    return pl.pallas_call(
        kernel,
        out_shape=(jax.ShapeDtypeStruct(shape, BF16),) * 2,
        in_specs=[VMEM] * len(operands),
        out_specs=(VMEM,) * 2,
        scratch_shapes=[pltpu.SemaphoreType.DMA((2,))],
        compiler_params=pltpu.CompilerParams(vmem_limit_bytes=SMALL),
        cost_estimate=pl.CostEstimate(flops=cost, bytes_accessed=10**6, transcendentals=0),
    )(*operands)


def coupling_kernel(atoms, force_ref, bond_ref, nbr_ref, eig_ref, image_ref, rim_ref, cpl_ref, own_ref):
    comps, _, slots, own = force_ref.shape
    wide = slots * GROUP
    span = own + RIM
    start = lax.axis_index("atom") * own
    offset = nbr_ref[...] - start
    offset = jnp.where(offset < -RIM, offset + atoms, offset)
    offset = jnp.where(offset >= own + RIM, offset - atoms, offset)
    place = jnp.transpose((offset - RIM).astype(F32)).astype(BF16)
    spread = jnp.where(iota((slots, wide), 1) // GROUP == iota((slots, wide), 0), 1.0, 0.0).astype(BF16)
    same = iota((GROUP, wide), 0) == iota((GROUP, wide), 1) % GROUP
    placed = jnp.dot(place, spread, preferred_element_type=F32)
    bonds = [jnp.transpose(bond_ref[k]) for k in range(comps)]
    for c in range(comps):
        for d in range(comps):
            column = jnp.transpose(force_ref[c, d])
            for k in range(comps):
                cpl_ref[(k * comps + c) * comps + d] = (bonds[k] * column).astype(BF16)
    own_ids = iota((own, wide), 0) - RIM
    halves = own // RIM
    for h in range(halves):
        rim_ids = iota((RIM, wide), 0) + (-2 * RIM if h == 0 else own - RIM)
        ids = jnp.concatenate([own_ids, rim_ids], axis=0)
        for g in range(RIM // GROUP):
            base = h * RIM + g * GROUP
            row = jnp.sum(jnp.where(same, placed[base : base + GROUP], 0.0), axis=0, keepdims=True)
            hot = jnp.where(ids == row.astype(jnp.int32), 1.0, 0.0).astype(BF16)
            part = cpl_ref[:, base : base + GROUP, :].reshape(comps**3 * GROUP, slots)
            diag = jnp.dot(part, spread, preferred_element_type=F32).reshape(comps**3, GROUP, wide)
            diag = jnp.where(same[None], diag, 0.0).astype(BF16).reshape(comps**3 * GROUP, wide)
            block = lax.dot_general(diag, hot, (((1,), (1,)), ((), ())), preferred_element_type=F32)
            block = block.astype(BF16)
            for kc in range(comps * comps):
                rows = slice(kc * RIM + g * GROUP, kc * RIM + (g + 1) * GROUP)
                for d in range(comps):
                    top = (kc * comps + d) * GROUP
                    piece = block[top : top + GROUP]
                    own_ref[h, rows, d * own : (d + 1) * own] = piece[:, :own]
                    rim_ref[h, rows, d * RIM : (d + 1) * RIM] = piece[:, own:span]
        eig = eig_ref[...].reshape(comps * own, eig_ref.shape[2])
        image_ref[h] = jnp.dot(own_ref[h], eig, preferred_element_type=F32)


def own_image(force, bond, nbr, eigvec, atoms):
    comps, _, slots, own = force.shape
    halves, rows = own // RIM, comps * comps * RIM
    return pl.pallas_call(
        functools.partial(coupling_kernel, atoms),
        out_shape=(
            jax.ShapeDtypeStruct((halves, rows, eigvec.shape[2]), F32),
            jax.ShapeDtypeStruct((halves, rows, comps * RIM), BF16),
        ),
        in_specs=[VMEM] * 4,
        out_specs=(VMEM,) * 2,
        scratch_shapes=[
            pltpu.VMEM((comps**3, own, slots), BF16),
            pltpu.VMEM((halves, rows, comps * own), BF16),
        ],
        compiler_params=pltpu.CompilerParams(vmem_limit_bytes=LARGE),
        cost_estimate=pl.CostEstimate(flops=4 * 10**9, bytes_accessed=6 * 10**6, transcendentals=0),
    )(force, bond, nbr, eigvec)


def pair_kernel(image_ref, cpl_ref, own_ref, rim_one, rim_two, halo_one, halo_two, keep_ref, send_ref, flux_ref):
    comps, own, modes = own_ref.shape
    depth = comps * own
    place = lax.axis_index("atom")
    odd = lax.rem(place, 2) == 1
    high = lax.rem(lax.axis_index("mode"), 2) == 1
    one = rim_one[...].reshape(comps * RIM, modes)
    two = rim_two[...].reshape(comps * RIM, modes)
    for h, rim in enumerate((jnp.where(odd, one, two), jnp.where(odd, two, one))):
        image = (image_ref[h] + jnp.dot(cpl_ref[h], rim, preferred_element_type=F32)).astype(BF16)
        for k in range(comps):
            for c in range(comps):
                top = (k * comps + c) * RIM
                flux_ref[c, h * RIM : (h + 1) * RIM, k * modes : (k + 1) * modes] = image[top : top + RIM]
    flux = flux_ref[...].reshape(depth, comps * modes)
    contract = (((0,), (0,)), ((), ()))
    pairs = lax.dot_general(own_ref[...].reshape(depth, modes), flux, contract, preferred_element_type=F32)
    first = halo_one[:, 0:own, :].reshape(depth, HALF)
    second = halo_two[:, 0:own, :].reshape(depth, HALF)
    before = jnp.where(high, first, second)
    after = jnp.where(high, second, first)
    low_flux = jnp.concatenate([flux[:, k * modes : k * modes + HALF] for k in range(comps)], axis=1)
    high_flux = jnp.concatenate([flux[:, k * modes + HALF : (k + 1) * modes] for k in range(comps)], axis=1)
    below = lax.dot_general(before, low_flux, contract, preferred_element_type=F32)
    above = lax.dot_general(after, high_flux, contract, preferred_element_type=F32)
    lower = iota((HALF, HALF), 0) > iota((HALF, HALF), 1)
    equal = iota((HALF, HALF), 0) == iota((HALF, HALF), 1)
    second_core = odd
    for k in range(comps):
        left, middle, right = k * modes, k * modes + HALF, (k + 1) * modes
        sets = []
        for part in range(2):
            if part == 0:
                main = pairs[0:HALF, left:middle]
                low = below[:, k * HALF : (k + 1) * HALF]
                up = pairs[HALF : 2 * HALF, left:middle]
            else:
                main = pairs[HALF : 2 * HALF, middle:right]
                low = pairs[0:HALF, middle:right]
                up = above[:, k * HALF : (k + 1) * HALF]
            edge = jnp.sum(jnp.where(equal, low, 0.0), axis=0, keepdims=True)
            edge = jnp.broadcast_to(edge, (EXTRA, HALF))
            sets.append(jnp.concatenate([main, jnp.where(lower, low, up), edge], axis=0))
        keep_ref[k] = jnp.where(second_core, sets[1], sets[0])
        send_ref[k] = jnp.where(second_core, sets[0], sets[1]).astype(BF16)


def pair_parts(image, matrix, eigvec, rim_one, rim_two, halo_one, halo_two):
    comps, own, modes = eigvec.shape
    shape = (comps, 2 * HALF + EXTRA, HALF)
    return pl.pallas_call(
        pair_kernel,
        out_shape=(jax.ShapeDtypeStruct(shape, F32), jax.ShapeDtypeStruct(shape, BF16)),
        in_specs=[VMEM] * 7,
        out_specs=(VMEM, VMEM),
        scratch_shapes=[
            pltpu.VMEM((comps, own, comps * modes), BF16),
        ],
        compiler_params=pltpu.CompilerParams(vmem_limit_bytes=LARGE),
        cost_estimate=pl.CostEstimate(flops=2 * 10**9, bytes_accessed=6 * 10**6, transcendentals=0),
    )(image, matrix, eigvec, rim_one, rim_two, halo_one, halo_two)


def halo_freq(halo_ref, own):
    total = jnp.zeros((EXTRA, HALF), F32)
    for part in reversed(range(halo_ref.shape[0])):
        total = halo_ref[part, own : own + EXTRA, :].astype(F32) + total
    return total[0:1], total[EXTRA // 2 : EXTRA // 2 + 1]


def ends_kernel(own, freq_ref, halo_ref, out_ref):
    modes = freq_ref.shape[1]
    rows = (freq_ref[:, 0:HALF], freq_ref[:, modes - HALF : modes], *halo_freq(halo_ref, own))
    least = jnp.min(functools.reduce(jnp.minimum, rows), axis=1, keepdims=True)
    most = jnp.max(functools.reduce(jnp.maximum, rows), axis=1, keepdims=True)
    out_ref[...] = jnp.where(iota(out_ref.shape, 0) < 4, least, most)


def weigh_kernel(count, own, freq_ref, ends_ref, band_ref, halo_one, halo_two, pair_one, pair_two, out_ref):
    comps = pair_one.shape[0]
    modes = freq_ref.shape[1]
    second = lax.rem(lax.axis_index("atom"), 2) == 1
    high = lax.rem(lax.axis_index("mode"), 2) == 1
    shift = jnp.where(second, HALF, 0)
    start = lax.axis_index("mode") * modes + shift
    (one_first, one_last), (two_first, two_last) = halo_freq(halo_one, own), halo_freq(halo_two, own)
    one, two = jnp.where(high, one_last, one_first), jnp.where(high, two_first, two_last)
    outside = jnp.where(high == second, two, one)
    inside = jnp.where(second, freq_ref[:, 0:HALF], freq_ref[:, HALF:modes])
    freq = jnp.where(second, freq_ref[:, HALF:modes], freq_ref[:, 0:HALF])
    prev = jnp.where(second, inside, outside)
    following = jnp.where(second, outside, inside)
    prev = jnp.where(start == 0, 1.0, prev)
    following = jnp.where(start == count - HALF, 1.0, following)
    band = jnp.where(second, band_ref[:, HALF:modes], band_ref[:, 0:HALF])
    low_end, high_end = band[0:1], band[1:2]
    eta = BROAD * (ends_ref[7:8, :] - ends_ref[0:1, :]) / (count - 1)

    def column(row):
        return jnp.transpose(jnp.broadcast_to(row, (HALF, HALF)))

    def weight(partner_freq, partner_ids, own_ids):
        within = (partner_ids >= low_end) & (partner_ids < high_end) & (partner_ids != own_ids)
        detune = freq - partner_freq
        total = freq + partner_freq
        scale = (eta / math.pi) * (total * total)
        value = scale / ((detune * detune + eta * eta) * (4.0 * freq * partner_freq))
        return jnp.where(within, value, 0.0)

    rows = iota((HALF, HALF), 0)
    own_ids = start + iota((HALF, HALF), 1)
    lower = rows > iota((HALF, HALF), 1)
    main_weight = weight(column(freq), start + rows, own_ids)
    side_freq = jnp.where(lower, column(prev), column(following))
    side_weight = weight(side_freq, start + rows + jnp.where(lower, -HALF, HALF), own_ids)
    edge_own = start + iota((1, HALF), 1)
    edge_weight = weight(prev, edge_own - HALF, edge_own)
    main_strength = jnp.zeros((HALF, HALF), F32)
    side_strength = jnp.zeros((HALF, HALF), F32)
    edge_strength = jnp.zeros((1, HALF), F32)
    for k in range(comps):
        pair = pair_one[k].astype(F32) + pair_two[k].astype(F32)
        main, side, edge = pair[:HALF], pair[HALF : 2 * HALF], pair[2 * HALF : 2 * HALF + 1]
        main_strength += main * main
        side_strength += side * side
        edge_strength += edge * edge
    total = jnp.sum(main_weight * main_strength + side_weight * side_strength, axis=0, keepdims=True)
    total += edge_weight * edge_strength
    diff = math.pi / (3.0 * freq * freq) * total
    grown = jnp.exp(freq)
    carried = freq * freq * grown / ((grown - 1.0) * (grown - 1.0)) * diff
    out_ref[0:1] = diff
    out_ref[1:2] = carried
    out_ref[2:8] = jnp.broadcast_to(jnp.sum(carried, axis=1, keepdims=True), (6, HALF))


def local_call(kernel, out_shape, *operands):
    return pl.pallas_call(
        kernel,
        out_shape=out_shape,
        in_specs=[VMEM] * len(operands),
        out_specs=jax.tree.map(lambda _: VMEM, out_shape),
        compiler_params=pltpu.CompilerParams(vmem_limit_bytes=SMALL),
        cost_estimate=pl.CostEstimate(flops=10**6, bytes_accessed=10**6, transcendentals=0),
    )(*operands)


def running_kernel(modes, own_ref, other_ref, diff_ref, run_ref):
    odd = lax.rem(lax.axis_index("atom"), 2) == 1
    own, other = own_ref[...], other_ref[...]
    whole = jnp.concatenate([jnp.where(odd, other, own), jnp.where(odd, own, other)], axis=1)
    diff_ref[...] = whole[0:1]
    until = jnp.where(iota((modes, modes), 0) <= iota((modes, modes), 1), 1.0, 0.0)
    running = jnp.dot(whole, until, precision=lax.Precision.HIGHEST, preferred_element_type=F32)
    run_ref[...] = running[1:2]


def last_kernel(run_ref, earlier_ref, out_ref):
    modes = run_ref.shape[1]
    out_ref[...] = (run_ref[...] + earlier_ref[0:1, 0:1]) / modes


def swap(x, axis, bit):
    return lax.ppermute(x, axis, [(i, i ^ bit) for i in range(lax.axis_size(axis))])


def bits_of(axis):
    return [1 << b for b in range(lax.axis_size(axis).bit_length() - 1)]


def rounded_sum(own, other):
    total = own.astype(F32) + other.astype(F32)
    return lax.reduce_precision(total, 8, 7).astype(BF16)


def body(eigvec, force, bond, nbr, band, freq):
    domains, blocks = lax.axis_size("atom"), lax.axis_size("mode")
    comps, own, modes = eigvec.shape
    atoms, count = own * domains, modes * blocks
    block = lax.axis_index("mode")
    freq_row = freq.reshape(1, modes)
    inner = [(i, i ^ 1) for i in range(domains)]
    outer = [(i, (i + 1) % domains if i % 2 else (i - 1) % domains) for i in range(domains)]
    near = [(i, i ^ 1) for i in range(blocks)]
    far = [(i, i + 1 if i % 2 else i - 1) for i in range(1, blocks - 1)]
    inner_edge, outer_edge = edge_call(rim_kernel, (comps, RIM, modes), COST, eigvec)
    outer_edge, later = lax.optimization_barrier((outer_edge, freq_row))
    near_edge, far_edge = edge_call(halo_kernel, (comps, own + EXTRA, HALF), COST, eigvec, later)
    rim_two = lax.ppermute(outer_edge, "atom", outer)
    rim_one = lax.ppermute(inner_edge, "atom", inner)
    halo_one = lax.ppermute(near_edge, "mode", near)
    halo_two = lax.ppermute(far_edge, "mode", far)

    image, matrix = own_image(force, bond, nbr, eigvec, atoms)
    keep, send = pair_parts(image, matrix, eigvec, rim_one, rim_two, halo_one, halo_two)

    tile = jax.ShapeDtypeStruct((8, HALF), F32)
    row = jax.ShapeDtypeStruct((1, modes), F32)
    total = rounded_sum(keep, swap(send, "atom", 1))
    total, own_freq = lax.optimization_barrier((total, freq_row))
    ends = local_call(functools.partial(ends_kernel, own), tile, own_freq, halo_one)
    steps = bits_of("atom")[1:]
    for step, (one, two) in enumerate(zip(steps, reversed(steps))):
        total_other = lax.ppermute(total, "atom", [(i, i ^ (two if i % 2 else one)) for i in range(domains)])
        if step < len(steps) - 1:
            total = rounded_sum(total, total_other)
    for bit in bits_of("mode")[1:]:
        other = swap(ends, "mode", bit)
        ends = jnp.where(iota((8, HALF), 0) < 4, jnp.minimum(ends, other), jnp.maximum(ends, other))
    summary = local_call(
        functools.partial(weigh_kernel, count, own),
        tile, freq_row, ends, band, halo_one, halo_two, total, total_other,
    )

    other = swap(summary, "atom", 1)
    diff, running = local_call(functools.partial(running_kernel, modes), (row, row), summary, other)
    total = summary + other
    parts = [(bit, swap(total, "mode", bit)) for bit in reversed(range(1, blocks))]
    earlier = sum(jnp.where((block ^ bit) < block, part, 0.0) for bit, part in parts)
    conductivity = local_call(last_kernel, row, running, earlier[2:3])
    return diff.reshape(modes), conductivity.reshape(modes)


def solution(mesh):
    in_specs = (
        P(None, "atom", "mode"),
        P(None, None, None, "atom"),
        P(None, None, "atom"),
        P(None, "atom"),
        P(None, "mode"),
        P("mode"),
    )
    out_specs = (P("mode"), P("mode"))
    return jax.shard_map(body, mesh=mesh, in_specs=in_specs, out_specs=out_specs, check_vma=False)
```

```python
import functools
import math

import jax
import jax.numpy as jnp
from jax import lax
from jax.experimental import pallas as pl
from jax.experimental.pallas import tpu as pltpu
from jax.sharding import PartitionSpec as P

RIM = 128
HALF = 128
BROAD = 128
GROUP = 16
EXTRA = 16
F32 = jnp.float32
BF16 = jnp.bfloat16
VMEM = pl.BlockSpec(memory_space=pltpu.VMEM)
HBM = pl.BlockSpec(memory_space=pltpu.HBM)
SMALL = 8 * 2**20
COST = 10**10
LARGE = 24 * 2**20


def iota(shape, dim):
    return lax.broadcasted_iota(jnp.int32, shape, dim)


def rim_kernel(eig_ref, inner_ref, outer_ref, sems):
    own = eig_ref.shape[1]
    odd = lax.rem(lax.axis_index("atom"), 2)
    copies = []
    for place, (flag, ref) in enumerate(((odd, outer_ref), (1 - odd, inner_ref))):
        rows = pl.ds(pl.multiple_of(flag * (own - RIM), RIM), RIM)
        copies.append(pltpu.make_async_copy(eig_ref.at[:, rows, :], ref, sems.at[place]))
    for copy in copies:
        copy.start()
    for copy in copies:
        copy.wait()


def halo_kernel(eig_ref, freq_ref, near_ref, far_ref, sems):
    comps, own, modes = eig_ref.shape
    high = lax.rem(lax.axis_index("mode"), 2)
    copies = []
    for place, (flag, ref) in enumerate(((1 - high, near_ref), (high, far_ref))):
        columns = pl.ds(pl.multiple_of(flag * (modes - HALF), HALF), HALF)
        target = ref.at[:, pl.ds(0, own), :]
        copies.append(pltpu.make_async_copy(eig_ref.at[:, :, columns], target, sems.at[place]))
    for copy in copies:
        copy.start()
    freq = freq_ref[...]
    rest = jnp.where(iota((EXTRA, HALF), 0) < EXTRA // 2, freq[:, 0:HALF], freq[:, modes - HALF : modes])
    for part in range(comps):
        piece = rest.astype(BF16)
        rest = rest - piece.astype(F32)
        near_ref[part, own : own + EXTRA, :] = piece
        far_ref[part, own : own + EXTRA, :] = piece
    for copy in copies:
        copy.wait()


def edge_call(kernel, shape, cost, *operands):
    return pl.pallas_call(
        kernel,
        out_shape=(jax.ShapeDtypeStruct(shape, BF16),) * 2,
        in_specs=[VMEM] * len(operands),
        out_specs=(VMEM,) * 2,
        scratch_shapes=[pltpu.SemaphoreType.DMA((2,))],
        compiler_params=pltpu.CompilerParams(vmem_limit_bytes=SMALL),
        cost_estimate=pl.CostEstimate(flops=cost, bytes_accessed=10**6, transcendentals=0),
    )(*operands)


def coupling_kernel(atoms, force_ref, bond_ref, nbr_ref, eig_ref, image_ref, rim_ref, cpl_ref, own_ref):
    comps, _, slots, own = force_ref.shape
    wide = slots * GROUP
    span = own + RIM
    start = lax.axis_index("atom") * own
    offset = nbr_ref[...] - start
    offset = jnp.where(offset < -RIM, offset + atoms, offset)
    offset = jnp.where(offset >= own + RIM, offset - atoms, offset)
    place = jnp.transpose((offset - RIM).astype(F32)).astype(BF16)
    spread = jnp.where(iota((slots, wide), 1) // GROUP == iota((slots, wide), 0), 1.0, 0.0).astype(BF16)
    same = iota((GROUP, wide), 0) == iota((GROUP, wide), 1) % GROUP
    placed = jnp.dot(place, spread, preferred_element_type=F32)
    bonds = [jnp.transpose(bond_ref[k]) for k in range(comps)]
    for c in range(comps):
        for d in range(comps):
            column = jnp.transpose(force_ref[c, d])
            for k in range(comps):
                cpl_ref[(k * comps + c) * comps + d] = (bonds[k] * column).astype(BF16)
    own_ids = iota((own, wide), 0) - RIM
    halves = own // RIM
    for h in range(halves):
        rim_ids = iota((RIM, wide), 0) + (-2 * RIM if h == 0 else own - RIM)
        ids = jnp.concatenate([own_ids, rim_ids], axis=0)
        for g in range(RIM // GROUP):
            base = h * RIM + g * GROUP
            row = jnp.sum(jnp.where(same, placed[base : base + GROUP], 0.0), axis=0, keepdims=True)
            hot = jnp.where(ids == row.astype(jnp.int32), 1.0, 0.0).astype(BF16)
            part = cpl_ref[:, base : base + GROUP, :].reshape(comps**3 * GROUP, slots)
            diag = jnp.dot(part, spread, preferred_element_type=F32).reshape(comps**3, GROUP, wide)
            diag = jnp.where(same[None], diag, 0.0).astype(BF16).reshape(comps**3 * GROUP, wide)
            block = lax.dot_general(diag, hot, (((1,), (1,)), ((), ())), preferred_element_type=F32)
            block = block.astype(BF16)
            for kc in range(comps * comps):
                rows = slice(kc * RIM + g * GROUP, kc * RIM + (g + 1) * GROUP)
                for d in range(comps):
                    top = (kc * comps + d) * GROUP
                    piece = block[top : top + GROUP]
                    own_ref[h, rows, d * own : (d + 1) * own] = piece[:, :own]
                    rim_ref[h, rows, d * RIM : (d + 1) * RIM] = piece[:, own:span]
        eig = eig_ref[...].reshape(comps * own, eig_ref.shape[2])
        image_ref[h] = jnp.dot(own_ref[h], eig, preferred_element_type=F32)


def own_image(force, bond, nbr, eigvec, atoms):
    comps, _, slots, own = force.shape
    halves, rows = own // RIM, comps * comps * RIM
    return pl.pallas_call(
        functools.partial(coupling_kernel, atoms),
        out_shape=(
            jax.ShapeDtypeStruct((halves, rows, eigvec.shape[2]), F32),
            jax.ShapeDtypeStruct((halves, rows, comps * RIM), BF16),
        ),
        in_specs=[VMEM] * 4,
        out_specs=(VMEM,) * 2,
        scratch_shapes=[
            pltpu.VMEM((comps**3, own, slots), BF16),
            pltpu.VMEM((halves, rows, comps * own), BF16),
        ],
        compiler_params=pltpu.CompilerParams(vmem_limit_bytes=LARGE),
        cost_estimate=pl.CostEstimate(flops=4 * 10**9, bytes_accessed=6 * 10**6, transcendentals=0),
    )(force, bond, nbr, eigvec)


def pair_kernel(image_ref, cpl_ref, own_ref, rim_one, rim_two, halo_one, halo_two, keep_ref, send_ref, flux_ref):
    comps, own, modes = own_ref.shape
    depth = comps * own
    place = lax.axis_index("atom")
    odd = lax.rem(place, 2) == 1
    high = lax.rem(lax.axis_index("mode"), 2) == 1
    one = rim_one[...].reshape(comps * RIM, modes)
    two = rim_two[...].reshape(comps * RIM, modes)
    for h, rim in enumerate((jnp.where(odd, one, two), jnp.where(odd, two, one))):
        image = (image_ref[h] + jnp.dot(cpl_ref[h], rim, preferred_element_type=F32)).astype(BF16)
        for k in range(comps):
            for c in range(comps):
                top = (k * comps + c) * RIM
                flux_ref[c, h * RIM : (h + 1) * RIM, k * modes : (k + 1) * modes] = image[top : top + RIM]
    flux = flux_ref[...].reshape(depth, comps * modes)
    contract = (((0,), (0,)), ((), ()))
    pairs = lax.dot_general(own_ref[...].reshape(depth, modes), flux, contract, preferred_element_type=F32)
    first = halo_one[:, 0:own, :].reshape(depth, HALF)
    second = halo_two[:, 0:own, :].reshape(depth, HALF)
    before = jnp.where(high, first, second)
    after = jnp.where(high, second, first)
    low_flux = jnp.concatenate([flux[:, k * modes : k * modes + HALF] for k in range(comps)], axis=1)
    high_flux = jnp.concatenate([flux[:, k * modes + HALF : (k + 1) * modes] for k in range(comps)], axis=1)
    below = lax.dot_general(before, low_flux, contract, preferred_element_type=F32)
    above = lax.dot_general(after, high_flux, contract, preferred_element_type=F32)
    lower = iota((HALF, HALF), 0) > iota((HALF, HALF), 1)
    equal = iota((HALF, HALF), 0) == iota((HALF, HALF), 1)
    second_core = odd
    for k in range(comps):
        left, middle, right = k * modes, k * modes + HALF, (k + 1) * modes
        sets = []
        for part in range(2):
            if part == 0:
                main = pairs[0:HALF, left:middle]
                low = below[:, k * HALF : (k + 1) * HALF]
                up = pairs[HALF : 2 * HALF, left:middle]
            else:
                main = pairs[HALF : 2 * HALF, middle:right]
                low = pairs[0:HALF, middle:right]
                up = above[:, k * HALF : (k + 1) * HALF]
            edge = jnp.sum(jnp.where(equal, low, 0.0), axis=0, keepdims=True)
            edge = jnp.broadcast_to(edge, (EXTRA, HALF))
            sets.append(jnp.concatenate([main, jnp.where(lower, low, up), edge], axis=0))
        keep_ref[k] = jnp.where(second_core, sets[1], sets[0])
        send_ref[k] = jnp.where(second_core, sets[0], sets[1]).astype(BF16)


def pair_parts(image, matrix, eigvec, rim_one, rim_two, halo_one, halo_two):
    comps, own, modes = eigvec.shape
    shape = (comps, 2 * HALF + EXTRA, HALF)
    return pl.pallas_call(
        pair_kernel,
        out_shape=(jax.ShapeDtypeStruct(shape, F32), jax.ShapeDtypeStruct(shape, BF16)),
        in_specs=[VMEM] * 7,
        out_specs=(VMEM, VMEM),
        scratch_shapes=[
            pltpu.VMEM((comps, own, comps * modes), BF16),
        ],
        compiler_params=pltpu.CompilerParams(vmem_limit_bytes=LARGE),
        cost_estimate=pl.CostEstimate(flops=2 * 10**9, bytes_accessed=6 * 10**6, transcendentals=0),
    )(image, matrix, eigvec, rim_one, rim_two, halo_one, halo_two)


def halo_freq(halo_ref, own):
    total = jnp.zeros((EXTRA, HALF), F32)
    for part in reversed(range(halo_ref.shape[0])):
        total = halo_ref[part, own : own + EXTRA, :].astype(F32) + total
    return total[0:1], total[EXTRA // 2 : EXTRA // 2 + 1]


def ends_kernel(own, freq_ref, halo_ref, out_ref):
    modes = freq_ref.shape[1]
    rows = (freq_ref[:, 0:HALF], freq_ref[:, modes - HALF : modes], *halo_freq(halo_ref, own))
    least = jnp.min(functools.reduce(jnp.minimum, rows), axis=1, keepdims=True)
    most = jnp.max(functools.reduce(jnp.maximum, rows), axis=1, keepdims=True)
    out_ref[...] = jnp.where(iota(out_ref.shape, 0) < 4, least, most)


def weigh_kernel(count, own, freq_ref, ends_ref, band_ref, halo_one, halo_two, pair_one, pair_two, out_ref):
    comps = pair_one.shape[0]
    modes = freq_ref.shape[1]
    second = lax.rem(lax.axis_index("atom"), 2) == 1
    high = lax.rem(lax.axis_index("mode"), 2) == 1
    shift = jnp.where(second, HALF, 0)
    start = lax.axis_index("mode") * modes + shift
    (one_first, one_last), (two_first, two_last) = halo_freq(halo_one, own), halo_freq(halo_two, own)
    one, two = jnp.where(high, one_last, one_first), jnp.where(high, two_first, two_last)
    outside = jnp.where(high == second, two, one)
    inside = jnp.where(second, freq_ref[:, 0:HALF], freq_ref[:, HALF:modes])
    freq = jnp.where(second, freq_ref[:, HALF:modes], freq_ref[:, 0:HALF])
    prev = jnp.where(second, inside, outside)
    following = jnp.where(second, outside, inside)
    prev = jnp.where(start == 0, 1.0, prev)
    following = jnp.where(start == count - HALF, 1.0, following)
    band = jnp.where(second, band_ref[:, HALF:modes], band_ref[:, 0:HALF])
    low_end, high_end = band[0:1], band[1:2]
    eta = BROAD * (ends_ref[7:8, :] - ends_ref[0:1, :]) / (count - 1)

    def column(row):
        return jnp.transpose(jnp.broadcast_to(row, (HALF, HALF)))

    def weight(partner_freq, partner_ids, own_ids):
        within = (partner_ids >= low_end) & (partner_ids < high_end) & (partner_ids != own_ids)
        detune = freq - partner_freq
        total = freq + partner_freq
        scale = (eta / math.pi) * (total * total)
        value = scale / ((detune * detune + eta * eta) * (4.0 * freq * partner_freq))
        return jnp.where(within, value, 0.0)

    rows = iota((HALF, HALF), 0)
    own_ids = start + iota((HALF, HALF), 1)
    lower = rows > iota((HALF, HALF), 1)
    main_weight = weight(column(freq), start + rows, own_ids)
    side_freq = jnp.where(lower, column(prev), column(following))
    side_weight = weight(side_freq, start + rows + jnp.where(lower, -HALF, HALF), own_ids)
    edge_own = start + iota((1, HALF), 1)
    edge_weight = weight(prev, edge_own - HALF, edge_own)
    main_strength = jnp.zeros((HALF, HALF), F32)
    side_strength = jnp.zeros((HALF, HALF), F32)
    edge_strength = jnp.zeros((1, HALF), F32)
    for k in range(comps):
        pair = pair_one[k].astype(F32) + pair_two[k].astype(F32)
        main, side, edge = pair[:HALF], pair[HALF : 2 * HALF], pair[2 * HALF : 2 * HALF + 1]
        main_strength += main * main
        side_strength += side * side
        edge_strength += edge * edge
    total = jnp.sum(main_weight * main_strength + side_weight * side_strength, axis=0, keepdims=True)
    total += edge_weight * edge_strength
    diff = math.pi / (3.0 * freq * freq) * total
    grown = jnp.exp(freq)
    carried = freq * freq * grown / ((grown - 1.0) * (grown - 1.0)) * diff
    out_ref[0:1] = diff
    out_ref[1:2] = carried
    out_ref[2:8] = jnp.broadcast_to(jnp.sum(carried, axis=1, keepdims=True), (6, HALF))


def local_call(kernel, out_shape, *operands):
    return pl.pallas_call(
        kernel,
        out_shape=out_shape,
        in_specs=[VMEM] * len(operands),
        out_specs=jax.tree.map(lambda _: VMEM, out_shape),
        compiler_params=pltpu.CompilerParams(vmem_limit_bytes=SMALL),
        cost_estimate=pl.CostEstimate(flops=10**6, bytes_accessed=10**6, transcendentals=0),
    )(*operands)


def running_kernel(modes, own_ref, other_ref, diff_ref, run_ref):
    odd = lax.rem(lax.axis_index("atom"), 2) == 1
    own, other = own_ref[...], other_ref[...]
    whole = jnp.concatenate([jnp.where(odd, other, own), jnp.where(odd, own, other)], axis=1)
    diff_ref[...] = whole[0:1]
    until = jnp.where(iota((modes, modes), 0) <= iota((modes, modes), 1), 1.0, 0.0)
    running = jnp.dot(whole, until, precision=lax.Precision.HIGHEST, preferred_element_type=F32)
    run_ref[...] = running[1:2]


def last_kernel(run_ref, earlier_ref, out_ref):
    modes = run_ref.shape[1]
    out_ref[...] = (run_ref[...] + earlier_ref[0:1, 0:1]) / modes


def swap(x, axis, bit):
    return lax.ppermute(x, axis, [(i, i ^ bit) for i in range(lax.axis_size(axis))])


def bits_of(axis):
    return [1 << b for b in range(lax.axis_size(axis).bit_length() - 1)]


def rounded_sum(own, other):
    total = own.astype(F32) + other.astype(F32)
    return lax.reduce_precision(total, 8, 7).astype(BF16)


def body(eigvec, force, bond, nbr, band, freq):
    domains, blocks = lax.axis_size("atom"), lax.axis_size("mode")
    comps, own, modes = eigvec.shape
    atoms, count = own * domains, modes * blocks
    block = lax.axis_index("mode")
    freq_row = freq.reshape(1, modes)
    inner = [(i, i ^ 1) for i in range(domains)]
    outer = [(i, (i + 1) % domains if i % 2 else (i - 1) % domains) for i in range(domains)]
    near = [(i, i ^ 1) for i in range(blocks)]
    far = [(i, i + 1 if i % 2 else i - 1) for i in range(1, blocks - 1)]
    inner_edge, outer_edge = edge_call(rim_kernel, (comps, RIM, modes), COST, eigvec)
    outer_edge, later = lax.optimization_barrier((outer_edge, freq_row))
    near_edge, far_edge = edge_call(halo_kernel, (comps, own + EXTRA, HALF), COST, eigvec, later)
    rim_two = lax.ppermute(outer_edge, "atom", outer)
    rim_one = lax.ppermute(inner_edge, "atom", inner)
    halo_one = lax.ppermute(near_edge, "mode", near)
    hops = []
    for a in range(domains):
        for i in range(blocks):
            inside = 0 < i < blocks - 1
            hops.append((a * blocks + i, a * blocks + (i + 1 if i % 2 else i - 1) if inside else (a ^ 1) * blocks + i))
    halo_two = lax.ppermute(far_edge, ("atom", "mode"), hops)

    image, matrix = own_image(force, bond, nbr, eigvec, atoms)
    keep, send = pair_parts(image, matrix, eigvec, rim_one, rim_two, halo_one, halo_two)

    tile = jax.ShapeDtypeStruct((8, HALF), F32)
    row = jax.ShapeDtypeStruct((1, modes), F32)
    total = rounded_sum(keep, swap(send, "atom", 1))
    total, own_freq = lax.optimization_barrier((total, freq_row))
    ends = local_call(functools.partial(ends_kernel, own), tile, own_freq, halo_one)
    steps = bits_of("atom")[1:]
    for step, (one, two) in enumerate(zip(steps, reversed(steps))):
        total_other = lax.ppermute(total, "atom", [(i, i ^ (two if i % 2 else one)) for i in range(domains)])
        if step < len(steps) - 1:
            total = rounded_sum(total, total_other)
    for bit in bits_of("mode")[1:]:
        other = swap(ends, "mode", bit)
        ends = jnp.where(iota((8, HALF), 0) < 4, jnp.minimum(ends, other), jnp.maximum(ends, other))
    summary = local_call(
        functools.partial(weigh_kernel, count, own),
        tile, freq_row, ends, band, halo_one, halo_two, total, total_other,
    )

    other = swap(summary, "atom", 1)
    diff, running = local_call(functools.partial(running_kernel, modes), (row, row), summary, other)
    total = summary + other
    parts = [(bit, swap(total, "mode", bit)) for bit in reversed(range(1, blocks))]
    earlier = sum(jnp.where((block ^ bit) < block, part, 0.0) for bit, part in parts)
    conductivity = local_call(last_kernel, row, running, earlier[2:3])
    return diff.reshape(modes), conductivity.reshape(modes)


def solution(mesh):
    in_specs = (
        P(None, "atom", "mode"),
        P(None, None, None, "atom"),
        P(None, None, "atom"),
        P(None, "atom"),
        P(None, "mode"),
        P("mode"),
    )
    out_specs = (P("mode"), P("mode"))
    return jax.shard_map(body, mesh=mesh, in_specs=in_specs, out_specs=out_specs, check_vma=False)
```

```python
import functools
import math

import jax
import jax.numpy as jnp
from jax import lax
from jax.experimental import pallas as pl
from jax.experimental.pallas import tpu as pltpu
from jax.sharding import PartitionSpec as P

RIM = 128
HALF = 128
BROAD = 128
GROUP = 16
EXTRA = 16
F32 = jnp.float32
BF16 = jnp.bfloat16
VMEM = pl.BlockSpec(memory_space=pltpu.VMEM)
HBM = pl.BlockSpec(memory_space=pltpu.HBM)
SMALL = 8 * 2**20
COST = 10**10
LARGE = 24 * 2**20


def iota(shape, dim):
    return lax.broadcasted_iota(jnp.int32, shape, dim)


def rim_kernel(eig_ref, inner_ref, outer_ref, sems):
    own = eig_ref.shape[1]
    odd = lax.rem(lax.axis_index("atom"), 2)
    copies = []
    for place, (flag, ref) in enumerate(((odd, outer_ref), (1 - odd, inner_ref))):
        rows = pl.ds(pl.multiple_of(flag * (own - RIM), RIM), RIM)
        copies.append(pltpu.make_async_copy(eig_ref.at[:, rows, :], ref, sems.at[place]))
    for copy in copies:
        copy.start()
    for copy in copies:
        copy.wait()


def halo_kernel(eig_ref, freq_ref, near_ref, far_ref, sems):
    comps, own, modes = eig_ref.shape
    high = lax.rem(lax.axis_index("mode"), 2)
    copies = []
    for place, (flag, ref) in enumerate(((1 - high, near_ref), (high, far_ref))):
        columns = pl.ds(pl.multiple_of(flag * (modes - HALF), HALF), HALF)
        target = ref.at[:, pl.ds(0, own), :]
        copies.append(pltpu.make_async_copy(eig_ref.at[:, :, columns], target, sems.at[place]))
    for copy in copies:
        copy.start()
    freq = freq_ref[...]
    rest = jnp.where(iota((EXTRA, HALF), 0) < EXTRA // 2, freq[:, 0:HALF], freq[:, modes - HALF : modes])
    for part in range(comps):
        piece = rest.astype(BF16)
        rest = rest - piece.astype(F32)
        near_ref[part, own : own + EXTRA, :] = piece
        far_ref[part, own : own + EXTRA, :] = piece
    for copy in copies:
        copy.wait()


def edge_call(kernel, shape, cost, *operands):
    return pl.pallas_call(
        kernel,
        out_shape=(jax.ShapeDtypeStruct(shape, BF16),) * 2,
        in_specs=[VMEM] * len(operands),
        out_specs=(VMEM,) * 2,
        scratch_shapes=[pltpu.SemaphoreType.DMA((2,))],
        compiler_params=pltpu.CompilerParams(vmem_limit_bytes=SMALL),
        cost_estimate=pl.CostEstimate(flops=cost, bytes_accessed=10**6, transcendentals=0),
    )(*operands)


def coupling_kernel(atoms, force_ref, bond_ref, nbr_ref, eig_ref, image_ref, rim_ref, *scratch):
    cpl_ref, diag_ref, hot_ref, own_ref = scratch
    comps, _, slots, own = force_ref.shape
    wide = slots * GROUP
    span = own + RIM
    start = lax.axis_index("atom") * own
    offset = nbr_ref[...] - start
    offset = jnp.where(offset < -RIM, offset + atoms, offset)
    offset = jnp.where(offset >= own + RIM, offset - atoms, offset)
    place = jnp.transpose((offset - RIM).astype(F32)).astype(BF16)
    spread = jnp.where(iota((slots, wide), 1) // GROUP == iota((slots, wide), 0), 1.0, 0.0).astype(BF16)
    same = iota((GROUP, wide), 0) == iota((GROUP, wide), 1) % GROUP
    placed = jnp.dot(place, spread, preferred_element_type=F32)
    bonds = [jnp.transpose(bond_ref[k]) for k in range(comps)]
    for c in range(comps):
        for d in range(comps):
            column = jnp.transpose(force_ref[c, d])
            for k in range(comps):
                cpl_ref[(k * comps + c) * comps + d] = (bonds[k] * column).astype(BF16)
    own_ids = iota((own, wide), 0) - RIM
    halves, groups, tall = own // RIM, RIM // GROUP, comps**3 * GROUP
    for h in range(halves):
        rim_ids = iota((RIM, wide), 0) + (-2 * RIM if h == 0 else own - RIM)
        ids = jnp.concatenate([own_ids, rim_ids], axis=0)
        for g in range(groups):
            base = h * RIM + g * GROUP
            row = jnp.sum(jnp.where(same, placed[base : base + GROUP], 0.0), axis=0, keepdims=True)
            hot_ref[h * groups + g] = jnp.where(ids == row.astype(jnp.int32), 1.0, 0.0).astype(BF16)
            part = cpl_ref[:, base : base + GROUP, :].reshape(tall, slots)
            diag = jnp.dot(part, spread, preferred_element_type=F32).reshape(comps**3, GROUP, wide)
            diag_ref[h * groups + g] = jnp.where(same[None], diag, 0.0).astype(BF16).reshape(tall, wide)
    eig = eig_ref[...].reshape(comps * own, eig_ref.shape[2])
    for h in range(halves):
        for g in range(groups):
            diag, hot = diag_ref[h * groups + g], hot_ref[h * groups + g]
            block = lax.dot_general(diag, hot, (((1,), (1,)), ((), ())), preferred_element_type=F32)
            block = block.astype(BF16)
            for kc in range(comps * comps):
                rows = slice(kc * RIM + g * GROUP, kc * RIM + (g + 1) * GROUP)
                for d in range(comps):
                    top = (kc * comps + d) * GROUP
                    piece = block[top : top + GROUP]
                    own_ref[h, rows, d * own : (d + 1) * own] = piece[:, :own]
                    rim_ref[h, rows, d * RIM : (d + 1) * RIM] = piece[:, own:span]
        image_ref[h] = jnp.dot(own_ref[h], eig, preferred_element_type=F32)


def own_image(force, bond, nbr, eigvec, atoms):
    comps, _, slots, own = force.shape
    halves, rows = own // RIM, comps * comps * RIM
    return pl.pallas_call(
        functools.partial(coupling_kernel, atoms),
        out_shape=(
            jax.ShapeDtypeStruct((halves, rows, eigvec.shape[2]), F32),
            jax.ShapeDtypeStruct((halves, rows, comps * RIM), BF16),
        ),
        in_specs=[VMEM] * 4,
        out_specs=(VMEM,) * 2,
        scratch_shapes=[
            pltpu.VMEM((comps**3, own, slots), BF16),
            pltpu.VMEM((own // GROUP, comps**3 * GROUP, slots * GROUP), BF16),
            pltpu.VMEM((own // GROUP, own + RIM, slots * GROUP), BF16),
            pltpu.VMEM((halves, rows, comps * own), BF16),
        ],
        compiler_params=pltpu.CompilerParams(vmem_limit_bytes=LARGE),
        cost_estimate=pl.CostEstimate(flops=4 * 10**9, bytes_accessed=6 * 10**6, transcendentals=0),
    )(force, bond, nbr, eigvec)


def pair_kernel(image_ref, cpl_ref, own_ref, rim_one, rim_two, halo_one, halo_two, keep_ref, send_ref, flux_ref):
    comps, own, modes = own_ref.shape
    depth = comps * own
    place = lax.axis_index("atom")
    odd = lax.rem(place, 2) == 1
    high = lax.rem(lax.axis_index("mode"), 2) == 1
    one = rim_one[...].reshape(comps * RIM, modes)
    two = rim_two[...].reshape(comps * RIM, modes)
    for h, rim in enumerate((jnp.where(odd, one, two), jnp.where(odd, two, one))):
        image = (image_ref[h] + jnp.dot(cpl_ref[h], rim, preferred_element_type=F32)).astype(BF16)
        for k in range(comps):
            for c in range(comps):
                top = (k * comps + c) * RIM
                flux_ref[c, h * RIM : (h + 1) * RIM, k * modes : (k + 1) * modes] = image[top : top + RIM]
    flux = flux_ref[...].reshape(depth, comps * modes)
    contract = (((0,), (0,)), ((), ()))
    pairs = lax.dot_general(own_ref[...].reshape(depth, modes), flux, contract, preferred_element_type=F32)
    first = halo_one[:, 0:own, :].reshape(depth, HALF)
    second = halo_two[:, 0:own, :].reshape(depth, HALF)
    before = jnp.where(high, first, second)
    after = jnp.where(high, second, first)
    low_flux = jnp.concatenate([flux[:, k * modes : k * modes + HALF] for k in range(comps)], axis=1)
    high_flux = jnp.concatenate([flux[:, k * modes + HALF : (k + 1) * modes] for k in range(comps)], axis=1)
    below = lax.dot_general(before, low_flux, contract, preferred_element_type=F32)
    above = lax.dot_general(after, high_flux, contract, preferred_element_type=F32)
    lower = iota((HALF, HALF), 0) > iota((HALF, HALF), 1)
    equal = iota((HALF, HALF), 0) == iota((HALF, HALF), 1)
    second_core = odd
    for k in range(comps):
        left, middle, right = k * modes, k * modes + HALF, (k + 1) * modes
        sets = []
        for part in range(2):
            if part == 0:
                main = pairs[0:HALF, left:middle]
                low = below[:, k * HALF : (k + 1) * HALF]
                up = pairs[HALF : 2 * HALF, left:middle]
            else:
                main = pairs[HALF : 2 * HALF, middle:right]
                low = pairs[0:HALF, middle:right]
                up = above[:, k * HALF : (k + 1) * HALF]
            edge = jnp.sum(jnp.where(equal, low, 0.0), axis=0, keepdims=True)
            edge = jnp.broadcast_to(edge, (EXTRA, HALF))
            sets.append(jnp.concatenate([main, jnp.where(lower, low, up), edge], axis=0))
        keep_ref[k] = jnp.where(second_core, sets[1], sets[0])
        send_ref[k] = jnp.where(second_core, sets[0], sets[1]).astype(BF16)


def pair_parts(image, matrix, eigvec, rim_one, rim_two, halo_one, halo_two):
    comps, own, modes = eigvec.shape
    shape = (comps, 2 * HALF + EXTRA, HALF)
    return pl.pallas_call(
        pair_kernel,
        out_shape=(jax.ShapeDtypeStruct(shape, F32), jax.ShapeDtypeStruct(shape, BF16)),
        in_specs=[VMEM] * 7,
        out_specs=(VMEM, VMEM),
        scratch_shapes=[
            pltpu.VMEM((comps, own, comps * modes), BF16),
        ],
        compiler_params=pltpu.CompilerParams(vmem_limit_bytes=LARGE),
        cost_estimate=pl.CostEstimate(flops=2 * 10**9, bytes_accessed=6 * 10**6, transcendentals=0),
    )(image, matrix, eigvec, rim_one, rim_two, halo_one, halo_two)


def halo_freq(halo_ref, own):
    total = jnp.zeros((EXTRA, HALF), F32)
    for part in reversed(range(halo_ref.shape[0])):
        total = halo_ref[part, own : own + EXTRA, :].astype(F32) + total
    return total[0:1], total[EXTRA // 2 : EXTRA // 2 + 1]


def ends_kernel(own, freq_ref, halo_ref, out_ref):
    modes = freq_ref.shape[1]
    rows = (freq_ref[:, 0:HALF], freq_ref[:, modes - HALF : modes], *halo_freq(halo_ref, own))
    least = jnp.min(functools.reduce(jnp.minimum, rows), axis=1, keepdims=True)
    most = jnp.max(functools.reduce(jnp.maximum, rows), axis=1, keepdims=True)
    out_ref[...] = jnp.where(iota(out_ref.shape, 0) < 4, least, most)


def weigh_kernel(count, own, freq_ref, ends_ref, band_ref, halo_one, halo_two, main_one, main_two, side_one, side_two, out_ref):
    comps = main_one.shape[0]
    modes = freq_ref.shape[1]
    second = lax.rem(lax.axis_index("atom"), 2) == 1
    high = lax.rem(lax.axis_index("mode"), 2) == 1
    shift = jnp.where(second, HALF, 0)
    start = lax.axis_index("mode") * modes + shift
    (one_first, one_last), (two_first, two_last) = halo_freq(halo_one, own), halo_freq(halo_two, own)
    one, two = jnp.where(high, one_last, one_first), jnp.where(high, two_first, two_last)
    outside = jnp.where(high == second, two, one)
    inside = jnp.where(second, freq_ref[:, 0:HALF], freq_ref[:, HALF:modes])
    freq = jnp.where(second, freq_ref[:, HALF:modes], freq_ref[:, 0:HALF])
    prev = jnp.where(second, inside, outside)
    following = jnp.where(second, outside, inside)
    prev = jnp.where(start == 0, 1.0, prev)
    following = jnp.where(start == count - HALF, 1.0, following)
    band = jnp.where(second, band_ref[:, HALF:modes], band_ref[:, 0:HALF])
    low_end, high_end = band[0:1], band[1:2]
    eta = BROAD * (ends_ref[7:8, :] - ends_ref[0:1, :]) / (count - 1)

    def column(row):
        return jnp.transpose(jnp.broadcast_to(row, (HALF, HALF)))

    def weight(partner_freq, partner_ids, own_ids):
        within = (partner_ids >= low_end) & (partner_ids < high_end) & (partner_ids != own_ids)
        detune = freq - partner_freq
        total = freq + partner_freq
        scale = (eta / math.pi) * (total * total)
        value = scale / ((detune * detune + eta * eta) * (4.0 * freq * partner_freq))
        return jnp.where(within, value, 0.0)

    rows = iota((HALF, HALF), 0)
    own_ids = start + iota((HALF, HALF), 1)
    lower = rows > iota((HALF, HALF), 1)
    main_weight = weight(column(freq), start + rows, own_ids)
    side_freq = jnp.where(lower, column(prev), column(following))
    side_weight = weight(side_freq, start + rows + jnp.where(lower, -HALF, HALF), own_ids)
    edge_own = start + iota((1, HALF), 1)
    edge_weight = weight(prev, edge_own - HALF, edge_own)
    main_strength = jnp.zeros((HALF, HALF), F32)
    side_strength = jnp.zeros((HALF, HALF), F32)
    edge_strength = jnp.zeros((1, HALF), F32)
    for k in range(comps):
        main = main_one[k].astype(F32) + main_two[k].astype(F32)
        side = side_one[k].astype(F32) + side_two[k].astype(F32)
        main_strength += main * main
        side_strength += side[:HALF] * side[:HALF]
        edge = side[HALF : HALF + 1]
        edge_strength += edge * edge
    total = jnp.sum(main_weight * main_strength + side_weight * side_strength, axis=0, keepdims=True)
    total += edge_weight * edge_strength
    diff = math.pi / (3.0 * freq * freq) * total
    grown = jnp.exp(freq)
    carried = freq * freq * grown / ((grown - 1.0) * (grown - 1.0)) * diff
    out_ref[0:1] = diff
    out_ref[1:2] = carried
    out_ref[2:8] = jnp.broadcast_to(jnp.sum(carried, axis=1, keepdims=True), (6, HALF))


def local_call(kernel, out_shape, *operands):
    return pl.pallas_call(
        kernel,
        out_shape=out_shape,
        in_specs=[VMEM] * len(operands),
        out_specs=jax.tree.map(lambda _: VMEM, out_shape),
        compiler_params=pltpu.CompilerParams(vmem_limit_bytes=SMALL),
        cost_estimate=pl.CostEstimate(flops=10**6, bytes_accessed=10**6, transcendentals=0),
    )(*operands)


def running_kernel(modes, own_ref, other_ref, diff_ref, run_ref):
    odd = lax.rem(lax.axis_index("atom"), 2) == 1
    own, other = own_ref[...], other_ref[...]
    whole = jnp.concatenate([jnp.where(odd, other, own), jnp.where(odd, own, other)], axis=1)
    diff_ref[...] = whole[0:1]
    until = jnp.where(iota((modes, modes), 0) <= iota((modes, modes), 1), 1.0, 0.0)
    running = jnp.dot(whole, until, precision=lax.Precision.HIGHEST, preferred_element_type=F32)
    run_ref[...] = running[1:2]


def last_kernel(run_ref, earlier_ref, out_ref):
    modes = run_ref.shape[1]
    out_ref[...] = (run_ref[...] + earlier_ref[0:1, 0:1]) / modes


def swap(x, axis, bit):
    return lax.ppermute(x, axis, [(i, i ^ bit) for i in range(lax.axis_size(axis))])


def bits_of(axis):
    return [1 << b for b in range(lax.axis_size(axis).bit_length() - 1)]


def rounded_sum(own, other):
    total = own.astype(F32) + other.astype(F32)
    return lax.reduce_precision(total, 8, 7).astype(BF16)


def body(eigvec, force, bond, nbr, band, freq):
    domains, blocks = lax.axis_size("atom"), lax.axis_size("mode")
    comps, own, modes = eigvec.shape
    atoms, count = own * domains, modes * blocks
    block = lax.axis_index("mode")
    freq_row = freq.reshape(1, modes)
    inner = [(i, i ^ 1) for i in range(domains)]
    outer = [(i, (i + 1) % domains if i % 2 else (i - 1) % domains) for i in range(domains)]
    near = [(i, i ^ 1) for i in range(blocks)]
    far = [(i, i + 1 if i % 2 else i - 1) for i in range(1, blocks - 1)]
    inner_edge, outer_edge = edge_call(rim_kernel, (comps, RIM, modes), COST, eigvec)
    outer_edge, later = lax.optimization_barrier((outer_edge, freq_row))
    near_edge, far_edge = edge_call(halo_kernel, (comps, own + EXTRA, HALF), COST, eigvec, later)
    rim_two = lax.ppermute(outer_edge, "atom", outer)
    rim_one = lax.ppermute(inner_edge, "atom", inner)
    halo_one = lax.ppermute(near_edge, "mode", near)
    hops = []
    for a in range(domains):
        for i in range(blocks):
            inside = 0 < i < blocks - 1
            hops.append((a * blocks + i, a * blocks + (i + 1 if i % 2 else i - 1) if inside else (a ^ 1) * blocks + i))
    halo_two = lax.ppermute(far_edge, ("atom", "mode"), hops)

    image, matrix = own_image(force, bond, nbr, eigvec, atoms)
    keep, send = pair_parts(image, matrix, eigvec, rim_one, rim_two, halo_one, halo_two)

    tile = jax.ShapeDtypeStruct((8, HALF), F32)
    row = jax.ShapeDtypeStruct((1, modes), F32)
    total = rounded_sum(keep, swap(send, "atom", 1))
    total, own_freq = lax.optimization_barrier((total, freq_row))
    ends = local_call(functools.partial(ends_kernel, own), tile, own_freq, halo_one)
    main, side = total[:, :HALF], total[:, HALF:]
    steps = bits_of("atom")[1:]
    for step, (one, two) in enumerate(zip(steps, reversed(steps))):
        main_other, side_other = swap(main, "atom", one), swap(side, "atom", two)
        if step < len(steps) - 1:
            main, side = rounded_sum(main, main_other), rounded_sum(side, side_other)
    for bit in bits_of("mode")[1:]:
        other = swap(ends, "mode", bit)
        ends = jnp.where(iota((8, HALF), 0) < 4, jnp.minimum(ends, other), jnp.maximum(ends, other))
    summary = local_call(
        functools.partial(weigh_kernel, count, own),
        tile, freq_row, ends, band, halo_one, halo_two, main, main_other, side, side_other,
    )

    other = swap(summary, "atom", 1)
    diff, running = local_call(functools.partial(running_kernel, modes), (row, row), summary, other)
    total = summary + other
    parts = [(bit, swap(total, "mode", bit)) for bit in reversed(range(1, blocks))]
    earlier = sum(jnp.where((block ^ bit) < block, part, 0.0) for bit, part in parts)
    conductivity = local_call(last_kernel, row, running, earlier[2:3])
    return diff.reshape(modes), conductivity.reshape(modes)


def solution(mesh):
    in_specs = (
        P(None, "atom", "mode"),
        P(None, None, None, "atom"),
        P(None, None, "atom"),
        P(None, "atom"),
        P(None, "mode"),
        P("mode"),
    )
    out_specs = (P("mode"), P("mode"))
    return jax.shard_map(body, mesh=mesh, in_specs=in_specs, out_specs=out_specs, check_vma=False)
```

```python
import functools
import math

import jax
import jax.numpy as jnp
from jax import lax
from jax.experimental import pallas as pl
from jax.experimental.pallas import tpu as pltpu
from jax.sharding import PartitionSpec as P

RIM = 128
HALF = 128
BROAD = 128
GROUP = 16
EXTRA = 16
F32 = jnp.float32
BF16 = jnp.bfloat16
VMEM = pl.BlockSpec(memory_space=pltpu.VMEM)
HBM = pl.BlockSpec(memory_space=pltpu.HBM)
SMALL = 8 * 2**20
COST = 10**10
LARGE = 24 * 2**20


def iota(shape, dim):
    return lax.broadcasted_iota(jnp.int32, shape, dim)


def rim_kernel(eig_ref, inner_ref, outer_ref, sems):
    own = eig_ref.shape[1]
    odd = lax.rem(lax.axis_index("atom"), 2)
    copies = []
    for place, (flag, ref) in enumerate(((odd, outer_ref), (1 - odd, inner_ref))):
        rows = pl.ds(pl.multiple_of(flag * (own - RIM), RIM), RIM)
        copies.append(pltpu.make_async_copy(eig_ref.at[:, rows, :], ref, sems.at[place]))
    for copy in copies:
        copy.start()
    for copy in copies:
        copy.wait()


def halo_kernel(eig_ref, freq_ref, near_ref, far_ref, sems):
    comps, own, modes = eig_ref.shape
    high = lax.rem(lax.axis_index("mode"), 2)
    copies = []
    for place, (flag, ref) in enumerate(((1 - high, near_ref), (high, far_ref))):
        columns = pl.ds(pl.multiple_of(flag * (modes - HALF), HALF), HALF)
        target = ref.at[:, pl.ds(0, own), :]
        copies.append(pltpu.make_async_copy(eig_ref.at[:, :, columns], target, sems.at[place]))
    for copy in copies:
        copy.start()
    freq = freq_ref[...]
    rest = jnp.where(iota((EXTRA, HALF), 0) < EXTRA // 2, freq[:, 0:HALF], freq[:, modes - HALF : modes])
    for part in range(comps):
        piece = rest.astype(BF16)
        rest = rest - piece.astype(F32)
        near_ref[part, own : own + EXTRA, :] = piece
        far_ref[part, own : own + EXTRA, :] = piece
    for copy in copies:
        copy.wait()


def edge_call(kernel, shape, cost, *operands):
    return pl.pallas_call(
        kernel,
        out_shape=(jax.ShapeDtypeStruct(shape, BF16),) * 2,
        in_specs=[VMEM] * len(operands),
        out_specs=(VMEM,) * 2,
        scratch_shapes=[pltpu.SemaphoreType.DMA((2,))],
        compiler_params=pltpu.CompilerParams(vmem_limit_bytes=SMALL),
        cost_estimate=pl.CostEstimate(flops=cost, bytes_accessed=10**6, transcendentals=0),
    )(*operands)


def coupling_kernel(atoms, force_ref, bond_ref, nbr_ref, eig_ref, image_ref, rim_ref, *scratch):
    cpl_ref, diag_ref, hot_ref, own_ref = scratch
    comps, _, slots, own = force_ref.shape
    wide = slots * GROUP
    span = own + RIM
    start = lax.axis_index("atom") * own
    offset = nbr_ref[...] - start
    offset = jnp.where(offset < -RIM, offset + atoms, offset)
    offset = jnp.where(offset >= own + RIM, offset - atoms, offset)
    place = jnp.transpose((offset - RIM).astype(F32)).astype(BF16)
    spread = jnp.where(iota((slots, wide), 1) // GROUP == iota((slots, wide), 0), 1.0, 0.0).astype(BF16)
    same = iota((GROUP, wide), 0) == iota((GROUP, wide), 1) % GROUP
    placed = jnp.dot(place, spread, preferred_element_type=F32)
    bonds = [jnp.transpose(bond_ref[k]) for k in range(comps)]
    for c in range(comps):
        for d in range(comps):
            column = jnp.transpose(force_ref[c, d])
            for k in range(comps):
                cpl_ref[(k * comps + c) * comps + d] = (bonds[k] * column).astype(BF16)
    own_ids = iota((own, wide), 0) - RIM
    halves, groups, tall = own // RIM, RIM // GROUP, comps**3 * GROUP
    for h in range(halves):
        rim_ids = iota((RIM, wide), 0) + (-2 * RIM if h == 0 else own - RIM)
        ids = jnp.concatenate([own_ids, rim_ids], axis=0)
        for g in range(groups):
            base = h * RIM + g * GROUP
            row = jnp.sum(jnp.where(same, placed[base : base + GROUP], 0.0), axis=0, keepdims=True)
            hot_ref[h * groups + g] = jnp.where(ids == row.astype(jnp.int32), 1.0, 0.0).astype(BF16)
            part = cpl_ref[:, base : base + GROUP, :].reshape(tall, slots)
            diag = jnp.dot(part, spread, preferred_element_type=F32).reshape(comps**3, GROUP, wide)
            diag_ref[h * groups + g] = jnp.where(same[None], diag, 0.0).astype(BF16).reshape(tall, wide)
    eig = eig_ref[...].reshape(comps * own, eig_ref.shape[2])
    for h in range(halves):
        for g in range(groups):
            diag, hot = diag_ref[h * groups + g], hot_ref[h * groups + g]
            block = lax.dot_general(diag, hot, (((1,), (1,)), ((), ())), preferred_element_type=F32)
            block = block.astype(BF16)
            for kc in range(comps * comps):
                rows = slice(kc * RIM + g * GROUP, kc * RIM + (g + 1) * GROUP)
                for d in range(comps):
                    top = (kc * comps + d) * GROUP
                    piece = block[top : top + GROUP]
                    own_ref[h, rows, d * own : (d + 1) * own] = piece[:, :own]
                    rim_ref[h, rows, d * RIM : (d + 1) * RIM] = piece[:, own:span]
        image_ref[h] = jnp.dot(own_ref[h], eig, preferred_element_type=F32)


def own_image(force, bond, nbr, eigvec, atoms):
    comps, _, slots, own = force.shape
    halves, rows = own // RIM, comps * comps * RIM
    return pl.pallas_call(
        functools.partial(coupling_kernel, atoms),
        out_shape=(
            jax.ShapeDtypeStruct((halves, rows, eigvec.shape[2]), F32),
            jax.ShapeDtypeStruct((halves, rows, comps * RIM), BF16),
        ),
        in_specs=[VMEM] * 4,
        out_specs=(VMEM,) * 2,
        scratch_shapes=[
            pltpu.VMEM((comps**3, own, slots), BF16),
            pltpu.VMEM((own // GROUP, comps**3 * GROUP, slots * GROUP), BF16),
            pltpu.VMEM((own // GROUP, own + RIM, slots * GROUP), BF16),
            pltpu.VMEM((halves, rows, comps * own), BF16),
        ],
        compiler_params=pltpu.CompilerParams(vmem_limit_bytes=LARGE),
        cost_estimate=pl.CostEstimate(flops=4 * 10**9, bytes_accessed=6 * 10**6, transcendentals=0),
    )(force, bond, nbr, eigvec)


def pair_kernel(image_ref, cpl_ref, own_ref, rim_one, rim_two, halo_one, halo_two, keep_ref, send_ref, flux_ref):
    comps, own, modes = own_ref.shape
    depth = comps * own
    place = lax.axis_index("atom")
    odd = lax.rem(place, 2) == 1
    high = lax.rem(lax.axis_index("mode"), 2) == 1
    one = rim_one[...].reshape(comps * RIM, modes)
    two = rim_two[...].reshape(comps * RIM, modes)
    for h, rim in enumerate((jnp.where(odd, one, two), jnp.where(odd, two, one))):
        image = (image_ref[h] + jnp.dot(cpl_ref[h], rim, preferred_element_type=F32)).astype(BF16)
        for k in range(comps):
            for c in range(comps):
                top = (k * comps + c) * RIM
                flux_ref[c, h * RIM : (h + 1) * RIM, k * modes : (k + 1) * modes] = image[top : top + RIM]
    flux = flux_ref[...].reshape(depth, comps * modes)
    contract = (((0,), (0,)), ((), ()))
    pairs = lax.dot_general(own_ref[...].reshape(depth, modes), flux, contract, preferred_element_type=F32)
    first = halo_one[:, 0:own, :].reshape(depth, HALF)
    second = halo_two[:, 0:own, :].reshape(depth, HALF)
    before = jnp.where(high, first, second)
    after = jnp.where(high, second, first)
    low_flux = jnp.concatenate([flux[:, k * modes : k * modes + HALF] for k in range(comps)], axis=1)
    high_flux = jnp.concatenate([flux[:, k * modes + HALF : (k + 1) * modes] for k in range(comps)], axis=1)
    below = lax.dot_general(before, low_flux, contract, preferred_element_type=F32)
    above = lax.dot_general(after, high_flux, contract, preferred_element_type=F32)
    lower = iota((HALF, HALF), 0) > iota((HALF, HALF), 1)
    equal = iota((HALF, HALF), 0) == iota((HALF, HALF), 1)
    second_core = odd
    for k in range(comps):
        left, middle, right = k * modes, k * modes + HALF, (k + 1) * modes
        sets = []
        for part in range(2):
            if part == 0:
                main = pairs[0:HALF, left:middle]
                low = below[:, k * HALF : (k + 1) * HALF]
                up = pairs[HALF : 2 * HALF, left:middle]
            else:
                main = pairs[HALF : 2 * HALF, middle:right]
                low = pairs[0:HALF, middle:right]
                up = above[:, k * HALF : (k + 1) * HALF]
            edge = jnp.sum(jnp.where(equal, low, 0.0), axis=0, keepdims=True)
            edge = jnp.broadcast_to(edge, (EXTRA, HALF))
            sets.append(jnp.concatenate([main, jnp.where(lower, low, up), edge], axis=0))
        keep_ref[k] = jnp.where(second_core, sets[1], sets[0])
        send_ref[k] = jnp.where(second_core, sets[0], sets[1]).astype(BF16)


def pair_parts(image, matrix, eigvec, rim_one, rim_two, halo_one, halo_two):
    comps, own, modes = eigvec.shape
    shape = (comps, 2 * HALF + EXTRA, HALF)
    return pl.pallas_call(
        pair_kernel,
        out_shape=(jax.ShapeDtypeStruct(shape, F32), jax.ShapeDtypeStruct(shape, BF16)),
        in_specs=[VMEM] * 7,
        out_specs=(VMEM, VMEM),
        scratch_shapes=[
            pltpu.VMEM((comps, own, comps * modes), BF16),
        ],
        compiler_params=pltpu.CompilerParams(vmem_limit_bytes=LARGE),
        cost_estimate=pl.CostEstimate(flops=2 * 10**9, bytes_accessed=6 * 10**6, transcendentals=0),
    )(image, matrix, eigvec, rim_one, rim_two, halo_one, halo_two)


def halo_freq(halo_ref, own):
    total = jnp.zeros((EXTRA, HALF), F32)
    for part in reversed(range(halo_ref.shape[0])):
        total = halo_ref[part, own : own + EXTRA, :].astype(F32) + total
    return total[0:1], total[EXTRA // 2 : EXTRA // 2 + 1]


def ends_kernel(own, freq_ref, halo_ref, out_ref):
    modes = freq_ref.shape[1]
    rows = (freq_ref[:, 0:HALF], freq_ref[:, modes - HALF : modes], *halo_freq(halo_ref, own))
    least = jnp.min(functools.reduce(jnp.minimum, rows), axis=1, keepdims=True)
    most = jnp.max(functools.reduce(jnp.maximum, rows), axis=1, keepdims=True)
    out_ref[...] = jnp.where(iota(out_ref.shape, 0) < 4, least, most)


def weigh_kernel(count, own, freq_ref, ends_ref, band_ref, halo_one, halo_two, main_one, main_two, side_one, side_two, out_ref):
    comps = main_one.shape[0]
    modes = freq_ref.shape[1]
    second = lax.rem(lax.axis_index("atom"), 2) == 1
    high = lax.rem(lax.axis_index("mode"), 2) == 1
    shift = jnp.where(second, HALF, 0)
    start = lax.axis_index("mode") * modes + shift
    (one_first, one_last), (two_first, two_last) = halo_freq(halo_one, own), halo_freq(halo_two, own)
    one, two = jnp.where(high, one_last, one_first), jnp.where(high, two_first, two_last)
    outside = jnp.where(high == second, two, one)
    inside = jnp.where(second, freq_ref[:, 0:HALF], freq_ref[:, HALF:modes])
    freq = jnp.where(second, freq_ref[:, HALF:modes], freq_ref[:, 0:HALF])
    prev = jnp.where(second, inside, outside)
    following = jnp.where(second, outside, inside)
    prev = jnp.where(start == 0, 1.0, prev)
    following = jnp.where(start == count - HALF, 1.0, following)
    band = jnp.where(second, band_ref[:, HALF:modes], band_ref[:, 0:HALF])
    low_end, high_end = band[0:1], band[1:2]
    eta = BROAD * (ends_ref[7:8, :] - ends_ref[0:1, :]) / (count - 1)

    def column(row):
        return jnp.transpose(jnp.broadcast_to(row, (HALF, HALF)))

    def weight(partner_freq, partner_ids, own_ids):
        within = (partner_ids >= low_end) & (partner_ids < high_end) & (partner_ids != own_ids)
        detune = freq - partner_freq
        total = freq + partner_freq
        scale = (eta / math.pi) * (total * total)
        value = scale / ((detune * detune + eta * eta) * (4.0 * freq * partner_freq))
        return jnp.where(within, value, 0.0)

    rows = iota((HALF, HALF), 0)
    own_ids = start + iota((HALF, HALF), 1)
    lower = rows > iota((HALF, HALF), 1)
    main_weight = weight(column(freq), start + rows, own_ids)
    side_freq = jnp.where(lower, column(prev), column(following))
    side_weight = weight(side_freq, start + rows + jnp.where(lower, -HALF, HALF), own_ids)
    edge_own = start + iota((1, HALF), 1)
    edge_weight = weight(prev, edge_own - HALF, edge_own)
    main_strength = jnp.zeros((HALF, HALF), F32)
    side_strength = jnp.zeros((HALF, HALF), F32)
    edge_strength = jnp.zeros((1, HALF), F32)
    for k in range(comps):
        main = main_one[k].astype(F32) + main_two[k].astype(F32)
        side = side_one[k].astype(F32) + side_two[k].astype(F32)
        main_strength += main * main
        side_strength += side[:HALF] * side[:HALF]
        edge = side[HALF : HALF + 1]
        edge_strength += edge * edge
    total = jnp.sum(main_weight * main_strength + side_weight * side_strength, axis=0, keepdims=True)
    total += edge_weight * edge_strength
    diff = math.pi / (3.0 * freq * freq) * total
    grown = jnp.exp(freq)
    carried = freq * freq * grown / ((grown - 1.0) * (grown - 1.0)) * diff
    out_ref[0:1] = diff
    out_ref[1:2] = carried
    out_ref[2:8] = jnp.broadcast_to(jnp.sum(carried, axis=1, keepdims=True), (6, HALF))


def local_call(kernel, out_shape, *operands):
    return pl.pallas_call(
        kernel,
        out_shape=out_shape,
        in_specs=[VMEM] * len(operands),
        out_specs=jax.tree.map(lambda _: VMEM, out_shape),
        compiler_params=pltpu.CompilerParams(vmem_limit_bytes=SMALL),
        cost_estimate=pl.CostEstimate(flops=10**6, bytes_accessed=10**6, transcendentals=0),
    )(*operands)


def running_kernel(modes, own_ref, other_ref, diff_ref, run_ref):
    odd = lax.rem(lax.axis_index("atom"), 2) == 1
    own, other = own_ref[...], other_ref[...]
    whole = jnp.concatenate([jnp.where(odd, other, own), jnp.where(odd, own, other)], axis=1)
    diff_ref[...] = whole[0:1]
    until = jnp.where(iota((modes, modes), 0) <= iota((modes, modes), 1), 1.0, 0.0)
    running = jnp.dot(whole, until, precision=lax.Precision.HIGHEST, preferred_element_type=F32)
    run_ref[...] = running[1:2]


def last_kernel(run_ref, earlier_ref, out_ref):
    modes = run_ref.shape[1]
    out_ref[...] = (run_ref[...] + earlier_ref[0:1, 0:1]) / modes


def swap(x, axis, bit):
    return lax.ppermute(x, axis, [(i, i ^ bit) for i in range(lax.axis_size(axis))])


def bits_of(axis):
    return [1 << b for b in range(lax.axis_size(axis).bit_length() - 1)]


def rounded_sum(own, other):
    total = own.astype(F32) + other.astype(F32)
    return lax.reduce_precision(total, 8, 7).astype(BF16)


def body(eigvec, force, bond, nbr, band, freq):
    domains, blocks = lax.axis_size("atom"), lax.axis_size("mode")
    comps, own, modes = eigvec.shape
    atoms, count = own * domains, modes * blocks
    block = lax.axis_index("mode")
    freq_row = freq.reshape(1, modes)
    inner = [(i, i ^ 1) for i in range(domains)]
    outer = [(i, (i + 1) % domains if i % 2 else (i - 1) % domains) for i in range(domains)]
    near = [(i, i ^ 1) for i in range(blocks)]
    far = [(i, i + 1 if i % 2 else i - 1) for i in range(1, blocks - 1)]
    inner_edge, outer_edge = edge_call(rim_kernel, (comps, RIM, modes), COST, eigvec)
    outer_edge, later = lax.optimization_barrier((outer_edge, freq_row))
    near_edge, far_edge = edge_call(halo_kernel, (comps, own + EXTRA, HALF), COST, eigvec, later)
    far_edge, held = lax.optimization_barrier((far_edge, eigvec))
    rim_two = lax.ppermute(outer_edge, "atom", outer)
    rim_one = lax.ppermute(inner_edge, "atom", inner)
    halo_one = lax.ppermute(near_edge, "mode", near)
    hops = []
    for a in range(domains):
        for i in range(blocks):
            inside = 0 < i < blocks - 1
            hops.append((a * blocks + i, a * blocks + (i + 1 if i % 2 else i - 1) if inside else (a ^ 1) * blocks + i))
    halo_two = lax.ppermute(far_edge, ("atom", "mode"), hops)

    image, matrix = own_image(force, bond, nbr, held, atoms)
    keep, send = pair_parts(image, matrix, eigvec, rim_one, rim_two, halo_one, halo_two)

    tile = jax.ShapeDtypeStruct((8, HALF), F32)
    row = jax.ShapeDtypeStruct((1, modes), F32)
    total = rounded_sum(keep, swap(send, "atom", 1))
    total, own_freq = lax.optimization_barrier((total, freq_row))
    ends = local_call(functools.partial(ends_kernel, own), tile, own_freq, halo_one)
    main, side = total[:, :HALF], total[:, HALF:]
    steps = bits_of("atom")[1:]
    for step, (one, two) in enumerate(zip(steps, reversed(steps))):
        main_other, side_other = swap(main, "atom", one), swap(side, "atom", two)
        if step < len(steps) - 1:
            main, side = rounded_sum(main, main_other), rounded_sum(side, side_other)
    for bit in bits_of("mode")[1:]:
        other = swap(ends, "mode", bit)
        ends = jnp.where(iota((8, HALF), 0) < 4, jnp.minimum(ends, other), jnp.maximum(ends, other))
    summary = local_call(
        functools.partial(weigh_kernel, count, own),
        tile, freq_row, ends, band, halo_one, halo_two, main, main_other, side, side_other,
    )

    other = swap(summary, "atom", 1)
    diff, running = local_call(functools.partial(running_kernel, modes), (row, row), summary, other)
    total = summary + other
    parts = [(bit, swap(total, "mode", bit)) for bit in reversed(range(1, blocks))]
    earlier = sum(jnp.where((block ^ bit) < block, part, 0.0) for bit, part in parts)
    conductivity = local_call(last_kernel, row, running, earlier[2:3])
    return diff.reshape(modes), conductivity.reshape(modes)


def solution(mesh):
    in_specs = (
        P(None, "atom", "mode"),
        P(None, None, None, "atom"),
        P(None, None, "atom"),
        P(None, "atom"),
        P(None, "mode"),
        P("mode"),
    )
    out_specs = (P("mode"), P("mode"))
    return jax.shard_map(body, mesh=mesh, in_specs=in_specs, out_specs=out_specs, check_vma=False)
```

```python
import functools
import math

import jax
import jax.numpy as jnp
from jax import lax
from jax.experimental import pallas as pl
from jax.experimental.pallas import tpu as pltpu
from jax.sharding import PartitionSpec as P

RIM = 128
HALF = 128
BROAD = 128
GROUP = 16
EXTRA = 16
F32 = jnp.float32
BF16 = jnp.bfloat16
VMEM = pl.BlockSpec(memory_space=pltpu.VMEM)
HBM = pl.BlockSpec(memory_space=pltpu.HBM)
SMALL = 8 * 2**20
COST = 10**10
LARGE = 24 * 2**20


def iota(shape, dim):
    return lax.broadcasted_iota(jnp.int32, shape, dim)


def rim_kernel(eig_ref, inner_ref, outer_ref, sems):
    own = eig_ref.shape[1]
    odd = lax.rem(lax.axis_index("atom"), 2)
    copies = []
    for place, (flag, ref) in enumerate(((odd, outer_ref), (1 - odd, inner_ref))):
        rows = pl.ds(pl.multiple_of(flag * (own - RIM), RIM), RIM)
        copies.append(pltpu.make_async_copy(eig_ref.at[:, rows, :], ref, sems.at[place]))
    for copy in copies:
        copy.start()
    for copy in copies:
        copy.wait()


def halo_kernel(eig_ref, freq_ref, near_ref, far_ref, sems):
    comps, own, modes = eig_ref.shape
    high = lax.rem(lax.axis_index("mode"), 2)
    copies = []
    for place, (flag, ref) in enumerate(((1 - high, near_ref), (high, far_ref))):
        columns = pl.ds(pl.multiple_of(flag * (modes - HALF), HALF), HALF)
        target = ref.at[:, pl.ds(0, own), :]
        copies.append(pltpu.make_async_copy(eig_ref.at[:, :, columns], target, sems.at[place]))
    for copy in copies:
        copy.start()
    freq = freq_ref[...]
    rest = jnp.where(iota((EXTRA, HALF), 0) < EXTRA // 2, freq[:, 0:HALF], freq[:, modes - HALF : modes])
    for part in range(comps):
        piece = rest.astype(BF16)
        rest = rest - piece.astype(F32)
        near_ref[part, own : own + EXTRA, :] = piece
        far_ref[part, own : own + EXTRA, :] = piece
    for copy in copies:
        copy.wait()


def edge_call(kernel, shape, cost, *operands):
    return pl.pallas_call(
        kernel,
        out_shape=(jax.ShapeDtypeStruct(shape, BF16),) * 2,
        in_specs=[VMEM] * len(operands),
        out_specs=(VMEM,) * 2,
        scratch_shapes=[pltpu.SemaphoreType.DMA((2,))],
        compiler_params=pltpu.CompilerParams(vmem_limit_bytes=SMALL),
        cost_estimate=pl.CostEstimate(flops=cost, bytes_accessed=10**6, transcendentals=0),
    )(*operands)


def coupling_kernel(atoms, force_ref, bond_ref, nbr_ref, eig_ref, image_ref, rim_ref, *scratch):
    cpl_ref, diag_ref, hot_ref, own_ref = scratch
    comps, _, slots, own = force_ref.shape
    wide = slots * GROUP
    span = own + RIM
    start = lax.axis_index("atom") * own
    offset = nbr_ref[...] - start
    offset = jnp.where(offset < -RIM, offset + atoms, offset)
    offset = jnp.where(offset >= own + RIM, offset - atoms, offset)
    place = jnp.transpose((offset - RIM).astype(F32)).astype(BF16)
    spread = jnp.where(iota((slots, wide), 1) // GROUP == iota((slots, wide), 0), 1.0, 0.0).astype(BF16)
    same = iota((GROUP, wide), 0) == iota((GROUP, wide), 1) % GROUP
    placed = jnp.dot(place, spread, preferred_element_type=F32)
    bonds = [jnp.transpose(bond_ref[k]) for k in range(comps)]
    for c in range(comps):
        for d in range(comps):
            column = jnp.transpose(force_ref[c, d])
            for k in range(comps):
                cpl_ref[(k * comps + c) * comps + d] = (bonds[k] * column).astype(BF16)
    own_ids = iota((own, wide), 0) - RIM
    halves, groups, tall = own // RIM, RIM // GROUP, comps**3 * GROUP
    for h in range(halves):
        rim_ids = iota((RIM, wide), 0) + (-2 * RIM if h == 0 else own - RIM)
        ids = jnp.concatenate([own_ids, rim_ids], axis=0)
        for g in range(groups):
            base = h * RIM + g * GROUP
            row = jnp.sum(jnp.where(same, placed[base : base + GROUP], 0.0), axis=0, keepdims=True)
            hot_ref[h * groups + g] = jnp.where(ids == row.astype(jnp.int32), 1.0, 0.0).astype(BF16)
            part = cpl_ref[:, base : base + GROUP, :].reshape(tall, slots)
            diag = jnp.dot(part, spread, preferred_element_type=F32).reshape(comps**3, GROUP, wide)
            diag_ref[h * groups + g] = jnp.where(same[None], diag, 0.0).astype(BF16).reshape(tall, wide)
    eig = eig_ref[...].reshape(comps * own, eig_ref.shape[2])
    for h in range(halves):
        for g in range(groups):
            diag, hot = diag_ref[h * groups + g], hot_ref[h * groups + g]
            block = lax.dot_general(diag, hot, (((1,), (1,)), ((), ())), preferred_element_type=F32)
            block = block.astype(BF16)
            for kc in range(comps * comps):
                rows = slice(kc * RIM + g * GROUP, kc * RIM + (g + 1) * GROUP)
                for d in range(comps):
                    top = (kc * comps + d) * GROUP
                    piece = block[top : top + GROUP]
                    own_ref[h, rows, d * own : (d + 1) * own] = piece[:, :own]
                    rim_ref[h, rows, d * RIM : (d + 1) * RIM] = piece[:, own:span]
        image_ref[h] = jnp.dot(own_ref[h], eig, preferred_element_type=F32)


def own_image(force, bond, nbr, eigvec, atoms):
    comps, _, slots, own = force.shape
    halves, rows = own // RIM, comps * comps * RIM
    return pl.pallas_call(
        functools.partial(coupling_kernel, atoms),
        out_shape=(
            jax.ShapeDtypeStruct((halves, rows, eigvec.shape[2]), F32),
            jax.ShapeDtypeStruct((halves, rows, comps * RIM), BF16),
        ),
        in_specs=[VMEM] * 4,
        out_specs=(VMEM,) * 2,
        scratch_shapes=[
            pltpu.VMEM((comps**3, own, slots), BF16),
            pltpu.VMEM((own // GROUP, comps**3 * GROUP, slots * GROUP), BF16),
            pltpu.VMEM((own // GROUP, own + RIM, slots * GROUP), BF16),
            pltpu.VMEM((halves, rows, comps * own), BF16),
        ],
        compiler_params=pltpu.CompilerParams(vmem_limit_bytes=LARGE),
        cost_estimate=pl.CostEstimate(flops=4 * 10**9, bytes_accessed=6 * 10**6, transcendentals=0),
    )(force, bond, nbr, eigvec)


def main_kernel(image_ref, cpl_ref, own_ref, rim_one, rim_two, keep_ref, send_ref, cross_ref, flux_ref):
    comps, own, modes = own_ref.shape
    depth = comps * own
    odd = lax.rem(lax.axis_index("atom"), 2) == 1
    one = rim_one[...].reshape(comps * RIM, modes)
    two = rim_two[...].reshape(comps * RIM, modes)
    for h, rim in enumerate((jnp.where(odd, one, two), jnp.where(odd, two, one))):
        image = (image_ref[h] + jnp.dot(cpl_ref[h], rim, preferred_element_type=F32)).astype(BF16)
        for k in range(comps):
            for c in range(comps):
                top = (k * comps + c) * RIM
                flux_ref[c, h * RIM : (h + 1) * RIM, k * modes : (k + 1) * modes] = image[top : top + RIM]
    flux = flux_ref[...].reshape(depth, comps * modes)
    eig = own_ref[...].reshape(depth, modes)
    pairs = lax.dot_general(eig, flux, (((0,), (0,)), ((), ())), preferred_element_type=F32)
    for k in range(comps):
        left, middle, right = k * modes, k * modes + HALF, (k + 1) * modes
        first, second = pairs[0:HALF, left:middle], pairs[HALF : 2 * HALF, middle:right]
        keep_ref[k] = jnp.where(odd, second, first)
        send_ref[k] = jnp.where(odd, first, second).astype(BF16)
        cross_ref[0, k] = pairs[HALF : 2 * HALF, left:middle]
        cross_ref[1, k] = pairs[0:HALF, middle:right]


def side_kernel(flux_ref, cross_ref, halo_one, halo_two, keep_ref, send_ref):
    comps, own, wide = flux_ref.shape
    modes, depth = wide // comps, comps * own
    odd = lax.rem(lax.axis_index("atom"), 2) == 1
    high = lax.rem(lax.axis_index("mode"), 2) == 1
    flux = flux_ref[...].reshape(depth, wide)
    first = halo_one[:, 0:own, :].reshape(depth, HALF)
    second = halo_two[:, 0:own, :].reshape(depth, HALF)
    before = jnp.where(high, first, second)
    after = jnp.where(high, second, first)
    low_flux = jnp.concatenate([flux[:, k * modes : k * modes + HALF] for k in range(comps)], axis=1)
    high_flux = jnp.concatenate([flux[:, k * modes + HALF : (k + 1) * modes] for k in range(comps)], axis=1)
    contract = (((0,), (0,)), ((), ()))
    below = lax.dot_general(before, low_flux, contract, preferred_element_type=F32)
    above = lax.dot_general(after, high_flux, contract, preferred_element_type=F32)
    lower = iota((HALF, HALF), 0) > iota((HALF, HALF), 1)
    equal = iota((HALF, HALF), 0) == iota((HALF, HALF), 1)
    for k in range(comps):
        sets = []
        for part in range(2):
            outside = (below, above)[part][:, k * HALF : (k + 1) * HALF]
            low, up = (outside, cross_ref[0, k]) if part == 0 else (cross_ref[1, k], outside)
            edge = jnp.sum(jnp.where(equal, low, 0.0), axis=0, keepdims=True)
            sets.append(jnp.concatenate([jnp.where(lower, low, up), jnp.broadcast_to(edge, (EXTRA, HALF))], axis=0))
        keep_ref[k] = jnp.where(odd, sets[1], sets[0])
        send_ref[k] = jnp.where(odd, sets[0], sets[1]).astype(BF16)


def pair_call(kernel, out_shape, flops, *operands):
    return pl.pallas_call(
        kernel,
        out_shape=tuple(jax.ShapeDtypeStruct(shape, kind) for shape, kind in out_shape),
        in_specs=[VMEM] * len(operands),
        out_specs=(VMEM,) * len(out_shape),
        compiler_params=pltpu.CompilerParams(vmem_limit_bytes=LARGE),
        cost_estimate=pl.CostEstimate(flops=flops, bytes_accessed=10**6, transcendentals=0),
    )(*operands)


def halo_freq(halo_ref, own):
    total = jnp.zeros((EXTRA, HALF), F32)
    for part in reversed(range(halo_ref.shape[0])):
        total = halo_ref[part, own : own + EXTRA, :].astype(F32) + total
    return total[0:1], total[EXTRA // 2 : EXTRA // 2 + 1]


def ends_kernel(own, freq_ref, halo_ref, out_ref):
    modes = freq_ref.shape[1]
    rows = (freq_ref[:, 0:HALF], freq_ref[:, modes - HALF : modes], *halo_freq(halo_ref, own))
    least = jnp.min(functools.reduce(jnp.minimum, rows), axis=1, keepdims=True)
    most = jnp.max(functools.reduce(jnp.maximum, rows), axis=1, keepdims=True)
    out_ref[...] = jnp.where(iota(out_ref.shape, 0) < 4, least, most)


def weigh_kernel(count, own, freq_ref, ends_ref, band_ref, halo_one, halo_two, main_one, main_two, side_one, side_two, out_ref):
    comps = main_one.shape[0]
    modes = freq_ref.shape[1]
    second = lax.rem(lax.axis_index("atom"), 2) == 1
    high = lax.rem(lax.axis_index("mode"), 2) == 1
    shift = jnp.where(second, HALF, 0)
    start = lax.axis_index("mode") * modes + shift
    (one_first, one_last), (two_first, two_last) = halo_freq(halo_one, own), halo_freq(halo_two, own)
    one, two = jnp.where(high, one_last, one_first), jnp.where(high, two_first, two_last)
    outside = jnp.where(high == second, two, one)
    inside = jnp.where(second, freq_ref[:, 0:HALF], freq_ref[:, HALF:modes])
    freq = jnp.where(second, freq_ref[:, HALF:modes], freq_ref[:, 0:HALF])
    prev = jnp.where(second, inside, outside)
    following = jnp.where(second, outside, inside)
    prev = jnp.where(start == 0, 1.0, prev)
    following = jnp.where(start == count - HALF, 1.0, following)
    band = jnp.where(second, band_ref[:, HALF:modes], band_ref[:, 0:HALF])
    low_end, high_end = band[0:1], band[1:2]
    eta = BROAD * (ends_ref[7:8, :] - ends_ref[0:1, :]) / (count - 1)

    def column(row):
        return jnp.transpose(jnp.broadcast_to(row, (HALF, HALF)))

    def weight(partner_freq, partner_ids, own_ids):
        within = (partner_ids >= low_end) & (partner_ids < high_end) & (partner_ids != own_ids)
        detune = freq - partner_freq
        total = freq + partner_freq
        scale = (eta / math.pi) * (total * total)
        value = scale / ((detune * detune + eta * eta) * (4.0 * freq * partner_freq))
        return jnp.where(within, value, 0.0)

    rows = iota((HALF, HALF), 0)
    own_ids = start + iota((HALF, HALF), 1)
    lower = rows > iota((HALF, HALF), 1)
    main_weight = weight(column(freq), start + rows, own_ids)
    side_freq = jnp.where(lower, column(prev), column(following))
    side_weight = weight(side_freq, start + rows + jnp.where(lower, -HALF, HALF), own_ids)
    edge_own = start + iota((1, HALF), 1)
    edge_weight = weight(prev, edge_own - HALF, edge_own)
    main_strength = jnp.zeros((HALF, HALF), F32)
    side_strength = jnp.zeros((HALF, HALF), F32)
    edge_strength = jnp.zeros((1, HALF), F32)
    for k in range(comps):
        main = main_one[k].astype(F32) + main_two[k].astype(F32)
        side = side_one[k].astype(F32) + side_two[k].astype(F32)
        main_strength += main * main
        side_strength += side[:HALF] * side[:HALF]
        edge = side[HALF : HALF + 1]
        edge_strength += edge * edge
    total = jnp.sum(main_weight * main_strength + side_weight * side_strength, axis=0, keepdims=True)
    total += edge_weight * edge_strength
    diff = math.pi / (3.0 * freq * freq) * total
    grown = jnp.exp(freq)
    carried = freq * freq * grown / ((grown - 1.0) * (grown - 1.0)) * diff
    out_ref[0:1] = diff
    out_ref[1:2] = carried
    out_ref[2:8] = jnp.broadcast_to(jnp.sum(carried, axis=1, keepdims=True), (6, HALF))


def local_call(kernel, out_shape, *operands):
    return pl.pallas_call(
        kernel,
        out_shape=out_shape,
        in_specs=[VMEM] * len(operands),
        out_specs=jax.tree.map(lambda _: VMEM, out_shape),
        compiler_params=pltpu.CompilerParams(vmem_limit_bytes=SMALL),
        cost_estimate=pl.CostEstimate(flops=10**6, bytes_accessed=10**6, transcendentals=0),
    )(*operands)


def running_kernel(modes, own_ref, other_ref, diff_ref, run_ref):
    odd = lax.rem(lax.axis_index("atom"), 2) == 1
    own, other = own_ref[...], other_ref[...]
    whole = jnp.concatenate([jnp.where(odd, other, own), jnp.where(odd, own, other)], axis=1)
    diff_ref[...] = whole[0:1]
    until = jnp.where(iota((modes, modes), 0) <= iota((modes, modes), 1), 1.0, 0.0)
    running = jnp.dot(whole, until, precision=lax.Precision.HIGHEST, preferred_element_type=F32)
    run_ref[...] = running[1:2]


def last_kernel(run_ref, earlier_ref, out_ref):
    modes = run_ref.shape[1]
    out_ref[...] = (run_ref[...] + earlier_ref[0:1, 0:1]) / modes


def swap(x, axis, bit):
    return lax.ppermute(x, axis, [(i, i ^ bit) for i in range(lax.axis_size(axis))])


def bits_of(axis):
    return [1 << b for b in range(lax.axis_size(axis).bit_length() - 1)]


def rounded_sum(own, other):
    total = own.astype(F32) + other.astype(F32)
    return lax.reduce_precision(total, 8, 7).astype(BF16)


def body(eigvec, force, bond, nbr, band, freq):
    domains, blocks = lax.axis_size("atom"), lax.axis_size("mode")
    comps, own, modes = eigvec.shape
    atoms, count = own * domains, modes * blocks
    block = lax.axis_index("mode")
    freq_row = freq.reshape(1, modes)
    inner = [(i, i ^ 1) for i in range(domains)]
    outer = [(i, (i + 1) % domains if i % 2 else (i - 1) % domains) for i in range(domains)]
    near = [(i, i ^ 1) for i in range(blocks)]
    far = [(i, i + 1 if i % 2 else i - 1) for i in range(1, blocks - 1)]
    inner_edge, outer_edge = edge_call(rim_kernel, (comps, RIM, modes), COST, eigvec)
    outer_edge, later = lax.optimization_barrier((outer_edge, freq_row))
    near_edge, far_edge = edge_call(halo_kernel, (comps, own + EXTRA, HALF), COST, eigvec, later)
    far_edge, held = lax.optimization_barrier((far_edge, eigvec))
    rim_two = lax.ppermute(outer_edge, "atom", outer)
    rim_one = lax.ppermute(inner_edge, "atom", inner)
    halo_one = lax.ppermute(near_edge, "mode", near)
    hops = []
    for a in range(domains):
        for i in range(blocks):
            inside = 0 < i < blocks - 1
            hops.append((a * blocks + i, a * blocks + (i + 1 if i % 2 else i - 1) if inside else (a ^ 1) * blocks + i))
    halo_two = lax.ppermute(far_edge, ("atom", "mode"), hops)

    image, matrix = own_image(force, bond, nbr, held, atoms)
    square, tall = (comps, HALF, HALF), (comps, HALF + EXTRA, HALF)
    keep_main, send_main, cross, flux = pair_call(
        main_kernel,
        ((square, F32), (square, BF16), ((2, *square), F32), ((comps, own, comps * modes), BF16)),
        10**9, image, matrix, eigvec, rim_one, rim_two,
    )
    keep_side, send_side = pair_call(
        side_kernel, ((tall, F32), (tall, BF16)), 10**9, flux, cross, halo_one, halo_two
    )

    tile = jax.ShapeDtypeStruct((8, HALF), F32)
    row = jax.ShapeDtypeStruct((1, modes), F32)
    main = rounded_sum(keep_main, swap(send_main, "atom", 1))
    side = rounded_sum(keep_side, swap(send_side, "atom", 1))
    side, own_freq = lax.optimization_barrier((side, freq_row))
    ends = local_call(functools.partial(ends_kernel, own), tile, own_freq, halo_one)
    steps = bits_of("atom")[1:]
    for step, (one, two) in enumerate(zip(steps, reversed(steps))):
        main_other, side_other = swap(main, "atom", one), swap(side, "atom", two)
        if step < len(steps) - 1:
            main, side = rounded_sum(main, main_other), rounded_sum(side, side_other)
    for bit in bits_of("mode")[1:]:
        other = swap(ends, "mode", bit)
        ends = jnp.where(iota((8, HALF), 0) < 4, jnp.minimum(ends, other), jnp.maximum(ends, other))
    summary = local_call(
        functools.partial(weigh_kernel, count, own),
        tile, freq_row, ends, band, halo_one, halo_two, main, main_other, side, side_other,
    )

    other = swap(summary, "atom", 1)
    diff, running = local_call(functools.partial(running_kernel, modes), (row, row), summary, other)
    total = summary + other
    parts = [(bit, swap(total, "mode", bit)) for bit in reversed(range(1, blocks))]
    earlier = sum(jnp.where((block ^ bit) < block, part, 0.0) for bit, part in parts)
    conductivity = local_call(last_kernel, row, running, earlier[2:3])
    return diff.reshape(modes), conductivity.reshape(modes)


def solution(mesh):
    in_specs = (
        P(None, "atom", "mode"),
        P(None, None, None, "atom"),
        P(None, None, "atom"),
        P(None, "atom"),
        P(None, "mode"),
        P("mode"),
    )
    out_specs = (P("mode"), P("mode"))
    return jax.shard_map(body, mesh=mesh, in_specs=in_specs, out_specs=out_specs, check_vma=False)
```

```python
import functools
import math

import jax
import jax.numpy as jnp
from jax import lax
from jax.experimental import pallas as pl
from jax.experimental.pallas import tpu as pltpu
from jax.sharding import PartitionSpec as P

RIM = 128
HALF = 128
BROAD = 128
GROUP = 16
EXTRA = 16
F32 = jnp.float32
BF16 = jnp.bfloat16
VMEM = pl.BlockSpec(memory_space=pltpu.VMEM)
HBM = pl.BlockSpec(memory_space=pltpu.HBM)
SMALL = 8 * 2**20
COST = 10**10
LARGE = 24 * 2**20


def iota(shape, dim):
    return lax.broadcasted_iota(jnp.int32, shape, dim)


def rim_kernel(eig_ref, inner_ref, outer_ref, sems):
    own = eig_ref.shape[1]
    odd = lax.rem(lax.axis_index("atom"), 2)
    copies = []
    for place, (flag, ref) in enumerate(((odd, outer_ref), (1 - odd, inner_ref))):
        rows = pl.ds(pl.multiple_of(flag * (own - RIM), RIM), RIM)
        copies.append(pltpu.make_async_copy(eig_ref.at[:, rows, :], ref, sems.at[place]))
    for copy in copies:
        copy.start()
    for copy in copies:
        copy.wait()


def halo_kernel(eig_ref, freq_ref, near_ref, far_ref, sems):
    comps, own, modes = eig_ref.shape
    high = lax.rem(lax.axis_index("mode"), 2)
    copies = []
    for place, (flag, ref) in enumerate(((1 - high, near_ref), (high, far_ref))):
        columns = pl.ds(pl.multiple_of(flag * (modes - HALF), HALF), HALF)
        target = ref.at[:, pl.ds(0, own), :]
        copies.append(pltpu.make_async_copy(eig_ref.at[:, :, columns], target, sems.at[place]))
    for copy in copies:
        copy.start()
    freq = freq_ref[...]
    rest = jnp.where(iota((EXTRA, HALF), 0) < EXTRA // 2, freq[:, 0:HALF], freq[:, modes - HALF : modes])
    for part in range(comps):
        piece = rest.astype(BF16)
        rest = rest - piece.astype(F32)
        near_ref[part, own : own + EXTRA, :] = piece
        far_ref[part, own : own + EXTRA, :] = piece
    for copy in copies:
        copy.wait()


def edge_call(kernel, shape, cost, *operands):
    return pl.pallas_call(
        kernel,
        out_shape=(jax.ShapeDtypeStruct(shape, BF16),) * 2,
        in_specs=[VMEM] * len(operands),
        out_specs=(VMEM,) * 2,
        scratch_shapes=[pltpu.SemaphoreType.DMA((2,))],
        compiler_params=pltpu.CompilerParams(vmem_limit_bytes=SMALL),
        cost_estimate=pl.CostEstimate(flops=cost, bytes_accessed=10**6, transcendentals=0),
    )(*operands)


def coupling_kernel(atoms, force_ref, bond_ref, nbr_ref, eig_ref, image_ref, rim_ref, *scratch):
    cpl_ref, diag_ref, hot_ref, own_ref = scratch
    comps, _, slots, own = force_ref.shape
    wide = slots * GROUP
    span = own + RIM
    start = lax.axis_index("atom") * own
    offset = nbr_ref[...] - start
    offset = jnp.where(offset < -RIM, offset + atoms, offset)
    offset = jnp.where(offset >= own + RIM, offset - atoms, offset)
    place = jnp.transpose((offset - RIM).astype(F32)).astype(BF16)
    spread = jnp.where(iota((slots, wide), 1) // GROUP == iota((slots, wide), 0), 1.0, 0.0).astype(BF16)
    same = iota((GROUP, wide), 0) == iota((GROUP, wide), 1) % GROUP
    placed = jnp.dot(place, spread, preferred_element_type=F32)
    bonds = [jnp.transpose(bond_ref[k]) for k in range(comps)]
    for c in range(comps):
        for d in range(comps):
            column = jnp.transpose(force_ref[c, d])
            for k in range(comps):
                cpl_ref[(k * comps + c) * comps + d] = (bonds[k] * column).astype(BF16)
    own_ids = iota((own, wide), 0) - RIM
    halves, groups, tall = own // RIM, RIM // GROUP, comps**3 * GROUP
    for h in range(halves):
        rim_ids = iota((RIM, wide), 0) + (-2 * RIM if h == 0 else own - RIM)
        ids = jnp.concatenate([own_ids, rim_ids], axis=0)
        for g in range(groups):
            base = h * RIM + g * GROUP
            row = jnp.sum(jnp.where(same, placed[base : base + GROUP], 0.0), axis=0, keepdims=True)
            hot_ref[h * groups + g] = jnp.where(ids == row.astype(jnp.int32), 1.0, 0.0).astype(BF16)
            part = cpl_ref[:, base : base + GROUP, :].reshape(tall, slots)
            diag = jnp.dot(part, spread, preferred_element_type=F32).reshape(comps**3, GROUP, wide)
            diag_ref[h * groups + g] = jnp.where(same[None], diag, 0.0).astype(BF16).reshape(tall, wide)
    eig = eig_ref[...].reshape(comps * own, eig_ref.shape[2])
    for h in range(halves):
        for g in range(groups):
            diag, hot = diag_ref[h * groups + g], hot_ref[h * groups + g]
            block = lax.dot_general(diag, hot, (((1,), (1,)), ((), ())), preferred_element_type=F32)
            block = block.astype(BF16)
            for kc in range(comps * comps):
                rows = slice(kc * RIM + g * GROUP, kc * RIM + (g + 1) * GROUP)
                for d in range(comps):
                    top = (kc * comps + d) * GROUP
                    piece = block[top : top + GROUP]
                    own_ref[h, rows, d * own : (d + 1) * own] = piece[:, :own]
                    rim_ref[h, rows, d * RIM : (d + 1) * RIM] = piece[:, own:span]
        image_ref[h] = jnp.dot(own_ref[h], eig, preferred_element_type=F32)


def own_image(force, bond, nbr, eigvec, atoms):
    comps, _, slots, own = force.shape
    halves, rows = own // RIM, comps * comps * RIM
    return pl.pallas_call(
        functools.partial(coupling_kernel, atoms),
        out_shape=(
            jax.ShapeDtypeStruct((halves, rows, eigvec.shape[2]), F32),
            jax.ShapeDtypeStruct((halves, rows, comps * RIM), BF16),
        ),
        in_specs=[VMEM] * 4,
        out_specs=(VMEM,) * 2,
        scratch_shapes=[
            pltpu.VMEM((comps**3, own, slots), BF16),
            pltpu.VMEM((own // GROUP, comps**3 * GROUP, slots * GROUP), BF16),
            pltpu.VMEM((own // GROUP, own + RIM, slots * GROUP), BF16),
            pltpu.VMEM((halves, rows, comps * own), BF16),
        ],
        compiler_params=pltpu.CompilerParams(vmem_limit_bytes=LARGE),
        cost_estimate=pl.CostEstimate(flops=4 * 10**9, bytes_accessed=6 * 10**6, transcendentals=0),
    )(force, bond, nbr, eigvec)


def main_kernel(image_ref, cpl_ref, own_ref, rim_one, rim_two, keep_ref, send_ref, cross_ref, flux_ref):
    comps, own, modes = own_ref.shape
    depth = comps * own
    odd = lax.rem(lax.axis_index("atom"), 2) == 1
    one = rim_one[...].reshape(comps * RIM, modes)
    two = rim_two[...].reshape(comps * RIM, modes)
    for h, rim in enumerate((jnp.where(odd, one, two), jnp.where(odd, two, one))):
        image = (image_ref[h] + jnp.dot(cpl_ref[h], rim, preferred_element_type=F32)).astype(BF16)
        for k in range(comps):
            for c in range(comps):
                top = (k * comps + c) * RIM
                flux_ref[c, h * RIM : (h + 1) * RIM, k * modes : (k + 1) * modes] = image[top : top + RIM]
    flux = flux_ref[...].reshape(depth, comps * modes)
    eig = own_ref[...].reshape(depth, modes)
    pairs = lax.dot_general(eig, flux, (((0,), (0,)), ((), ())), preferred_element_type=F32)
    equal = iota((HALF, HALF), 0) == iota((HALF, HALF), 1)
    for k in range(comps):
        left, middle, right = k * modes, k * modes + HALF, (k + 1) * modes
        above, below = pairs[HALF : 2 * HALF, left:middle], pairs[0:HALF, middle:right]
        first = jnp.where(equal, above, pairs[0:HALF, left:middle])
        second = jnp.where(equal, below, pairs[HALF : 2 * HALF, middle:right])
        keep_ref[k] = jnp.where(odd, second, first)
        send_ref[k] = jnp.where(odd, first, second).astype(BF16)
        cross_ref[0, k] = above
        cross_ref[1, k] = below


def side_kernel(flux_ref, cross_ref, halo_one, halo_two, keep_ref, send_ref):
    comps, own, wide = flux_ref.shape
    modes, depth = wide // comps, comps * own
    odd = lax.rem(lax.axis_index("atom"), 2) == 1
    high = lax.rem(lax.axis_index("mode"), 2) == 1
    flux = flux_ref[...].reshape(depth, wide)
    first = halo_one[:, 0:own, :].reshape(depth, HALF)
    second = halo_two[:, 0:own, :].reshape(depth, HALF)
    before = jnp.where(high, first, second)
    after = jnp.where(high, second, first)
    low_flux = jnp.concatenate([flux[:, k * modes : k * modes + HALF] for k in range(comps)], axis=1)
    high_flux = jnp.concatenate([flux[:, k * modes + HALF : (k + 1) * modes] for k in range(comps)], axis=1)
    contract = (((0,), (0,)), ((), ()))
    below = lax.dot_general(before, low_flux, contract, preferred_element_type=F32)
    above = lax.dot_general(after, high_flux, contract, preferred_element_type=F32)
    rows, columns = iota((HALF, HALF), 0), iota((HALF, HALF), 1)
    for k in range(comps):
        here = slice(k * HALF, (k + 1) * HALF)
        first = jnp.where(rows >= columns, below[:, here], cross_ref[0, k])
        second = jnp.where(rows > columns, cross_ref[1, k], above[:, here])
        keep_ref[k] = jnp.where(odd, second, first)
        send_ref[k] = jnp.where(odd, first, second).astype(BF16)


def pair_call(kernel, out_shape, flops, *operands):
    return pl.pallas_call(
        kernel,
        out_shape=tuple(jax.ShapeDtypeStruct(shape, kind) for shape, kind in out_shape),
        in_specs=[VMEM] * len(operands),
        out_specs=(VMEM,) * len(out_shape),
        compiler_params=pltpu.CompilerParams(vmem_limit_bytes=LARGE),
        cost_estimate=pl.CostEstimate(flops=flops, bytes_accessed=10**6, transcendentals=0),
    )(*operands)


def halo_freq(halo_ref, own):
    total = jnp.zeros((EXTRA, HALF), F32)
    for part in reversed(range(halo_ref.shape[0])):
        total = halo_ref[part, own : own + EXTRA, :].astype(F32) + total
    return total[0:1], total[EXTRA // 2 : EXTRA // 2 + 1]


def ends_kernel(own, freq_ref, halo_ref, out_ref):
    modes = freq_ref.shape[1]
    rows = (freq_ref[:, 0:HALF], freq_ref[:, modes - HALF : modes], *halo_freq(halo_ref, own))
    least = jnp.min(functools.reduce(jnp.minimum, rows), axis=1, keepdims=True)
    most = jnp.max(functools.reduce(jnp.maximum, rows), axis=1, keepdims=True)
    out_ref[...] = jnp.where(iota(out_ref.shape, 0) < 4, least, most)


def weigh_kernel(count, own, freq_ref, ends_ref, band_ref, halo_one, halo_two, main_one, main_two, side_one, side_two, out_ref):
    comps = main_one.shape[0]
    modes = freq_ref.shape[1]
    second = lax.rem(lax.axis_index("atom"), 2) == 1
    high = lax.rem(lax.axis_index("mode"), 2) == 1
    shift = jnp.where(second, HALF, 0)
    start = lax.axis_index("mode") * modes + shift
    (one_first, one_last), (two_first, two_last) = halo_freq(halo_one, own), halo_freq(halo_two, own)
    one, two = jnp.where(high, one_last, one_first), jnp.where(high, two_first, two_last)
    outside = jnp.where(high == second, two, one)
    inside = jnp.where(second, freq_ref[:, 0:HALF], freq_ref[:, HALF:modes])
    freq = jnp.where(second, freq_ref[:, HALF:modes], freq_ref[:, 0:HALF])
    prev = jnp.where(second, inside, outside)
    following = jnp.where(second, outside, inside)
    prev = jnp.where(start == 0, 1.0, prev)
    following = jnp.where(start == count - HALF, 1.0, following)
    band = jnp.where(second, band_ref[:, HALF:modes], band_ref[:, 0:HALF])
    low_end, high_end = band[0:1], band[1:2]
    eta = BROAD * (ends_ref[7:8, :] - ends_ref[0:1, :]) / (count - 1)

    def column(row):
        return jnp.transpose(jnp.broadcast_to(row, (HALF, HALF)))

    def weight(partner_freq, partner_ids, own_ids):
        within = (partner_ids >= low_end) & (partner_ids < high_end) & (partner_ids != own_ids)
        detune = freq - partner_freq
        total = freq + partner_freq
        scale = (eta / math.pi) * (total * total)
        value = scale / ((detune * detune + eta * eta) * (4.0 * freq * partner_freq))
        return jnp.where(within, value, 0.0)

    rows, columns = iota((HALF, HALF), 0), iota((HALF, HALF), 1)
    own_ids = start + columns
    corner = rows == columns
    corner_freq, corner_shift = jnp.where(second, prev, following), jnp.where(second, -HALF, HALF)
    main_freq = jnp.where(corner, corner_freq, column(freq))
    main_weight = weight(main_freq, start + rows + jnp.where(corner, corner_shift, 0), own_ids)
    lower = rows + jnp.where(second, 0, 1) > columns
    side_freq = jnp.where(lower, column(prev), column(following))
    side_weight = weight(side_freq, start + rows + jnp.where(lower, -HALF, HALF), own_ids)
    main_strength = jnp.zeros((HALF, HALF), F32)
    side_strength = jnp.zeros((HALF, HALF), F32)
    for k in range(comps):
        main = main_one[k].astype(F32) + main_two[k].astype(F32)
        side = side_one[k].astype(F32) + side_two[k].astype(F32)
        main_strength += main * main
        side_strength += side * side
    total = jnp.sum(main_weight * main_strength + side_weight * side_strength, axis=0, keepdims=True)
    diff = math.pi / (3.0 * freq * freq) * total
    grown = jnp.exp(freq)
    carried = freq * freq * grown / ((grown - 1.0) * (grown - 1.0)) * diff
    out_ref[0:1] = diff
    out_ref[1:2] = carried
    out_ref[2:8] = jnp.broadcast_to(jnp.sum(carried, axis=1, keepdims=True), (6, HALF))


def local_call(kernel, out_shape, *operands):
    return pl.pallas_call(
        kernel,
        out_shape=out_shape,
        in_specs=[VMEM] * len(operands),
        out_specs=jax.tree.map(lambda _: VMEM, out_shape),
        compiler_params=pltpu.CompilerParams(vmem_limit_bytes=SMALL),
        cost_estimate=pl.CostEstimate(flops=10**6, bytes_accessed=10**6, transcendentals=0),
    )(*operands)


def running_kernel(modes, own_ref, other_ref, diff_ref, run_ref):
    odd = lax.rem(lax.axis_index("atom"), 2) == 1
    own, other = own_ref[...], other_ref[...]
    whole = jnp.concatenate([jnp.where(odd, other, own), jnp.where(odd, own, other)], axis=1)
    diff_ref[...] = whole[0:1]
    until = jnp.where(iota((modes, modes), 0) <= iota((modes, modes), 1), 1.0, 0.0)
    running = jnp.dot(whole, until, precision=lax.Precision.HIGHEST, preferred_element_type=F32)
    run_ref[...] = running[1:2]


def last_kernel(run_ref, earlier_ref, out_ref):
    modes = run_ref.shape[1]
    out_ref[...] = (run_ref[...] + earlier_ref[0:1, 0:1]) / modes


def swap(x, axis, bit):
    return lax.ppermute(x, axis, [(i, i ^ bit) for i in range(lax.axis_size(axis))])


def bits_of(axis):
    return [1 << b for b in range(lax.axis_size(axis).bit_length() - 1)]


def rounded_sum(own, other):
    total = own.astype(F32) + other.astype(F32)
    return lax.reduce_precision(total, 8, 7).astype(BF16)


def body(eigvec, force, bond, nbr, band, freq):
    domains, blocks = lax.axis_size("atom"), lax.axis_size("mode")
    comps, own, modes = eigvec.shape
    atoms, count = own * domains, modes * blocks
    block = lax.axis_index("mode")
    freq_row = freq.reshape(1, modes)
    inner = [(i, i ^ 1) for i in range(domains)]
    outer = [(i, (i + 1) % domains if i % 2 else (i - 1) % domains) for i in range(domains)]
    near = [(i, i ^ 1) for i in range(blocks)]
    far = [(i, i + 1 if i % 2 else i - 1) for i in range(1, blocks - 1)]
    inner_edge, outer_edge = edge_call(rim_kernel, (comps, RIM, modes), COST, eigvec)
    outer_edge, later = lax.optimization_barrier((outer_edge, freq_row))
    near_edge, far_edge = edge_call(halo_kernel, (comps, own + EXTRA, HALF), COST, eigvec, later)
    far_edge, held = lax.optimization_barrier((far_edge, eigvec))
    rim_two = lax.ppermute(outer_edge, "atom", outer)
    rim_one = lax.ppermute(inner_edge, "atom", inner)
    halo_one = lax.ppermute(near_edge, "mode", near)
    hops = []
    for a in range(domains):
        for i in range(blocks):
            inside = 0 < i < blocks - 1
            hops.append((a * blocks + i, a * blocks + (i + 1 if i % 2 else i - 1) if inside else (a ^ 1) * blocks + i))
    halo_two = lax.ppermute(far_edge, ("atom", "mode"), hops)

    image, matrix = own_image(force, bond, nbr, held, atoms)
    square = (comps, HALF, HALF)
    keep_main, send_main, cross, flux = pair_call(
        main_kernel,
        ((square, F32), (square, BF16), ((2, *square), F32), ((comps, own, comps * modes), BF16)),
        10**9, image, matrix, eigvec, rim_one, rim_two,
    )
    keep_side, send_side = pair_call(
        side_kernel, ((square, F32), (square, BF16)), 10**9, flux, cross, halo_one, halo_two
    )

    tile = jax.ShapeDtypeStruct((8, HALF), F32)
    row = jax.ShapeDtypeStruct((1, modes), F32)
    main = rounded_sum(keep_main, swap(send_main, "atom", 1))
    side = rounded_sum(keep_side, swap(send_side, "atom", 1))
    side, own_freq = lax.optimization_barrier((side, freq_row))
    ends = local_call(functools.partial(ends_kernel, own), tile, own_freq, halo_one)
    steps = bits_of("atom")[1:]
    for step, (one, two) in enumerate(zip(steps, reversed(steps))):
        main_other, side_other = swap(main, "atom", one), swap(side, "atom", two)
        if step < len(steps) - 1:
            main, side = rounded_sum(main, main_other), rounded_sum(side, side_other)
    for bit in bits_of("mode")[1:]:
        other = swap(ends, "mode", bit)
        ends = jnp.where(iota((8, HALF), 0) < 4, jnp.minimum(ends, other), jnp.maximum(ends, other))
    summary = local_call(
        functools.partial(weigh_kernel, count, own),
        tile, freq_row, ends, band, halo_one, halo_two, main, main_other, side, side_other,
    )

    other = swap(summary, "atom", 1)
    diff, running = local_call(functools.partial(running_kernel, modes), (row, row), summary, other)
    total = summary + other
    parts = [(bit, swap(total, "mode", bit)) for bit in reversed(range(1, blocks))]
    earlier = sum(jnp.where((block ^ bit) < block, part, 0.0) for bit, part in parts)
    conductivity = local_call(last_kernel, row, running, earlier[2:3])
    return diff.reshape(modes), conductivity.reshape(modes)


def solution(mesh):
    in_specs = (
        P(None, "atom", "mode"),
        P(None, None, None, "atom"),
        P(None, None, "atom"),
        P(None, "atom"),
        P(None, "mode"),
        P("mode"),
    )
    out_specs = (P("mode"), P("mode"))
    return jax.shard_map(body, mesh=mesh, in_specs=in_specs, out_specs=out_specs, check_vma=False)
```

```python
import functools
import math

import jax
import jax.numpy as jnp
from jax import lax
from jax.experimental import pallas as pl
from jax.experimental.pallas import tpu as pltpu
from jax.sharding import PartitionSpec as P

RIM = 128
HALF = 128
BROAD = 128
GROUP = 16
EXTRA = 16
F32 = jnp.float32
BF16 = jnp.bfloat16
VMEM = pl.BlockSpec(memory_space=pltpu.VMEM)
HBM = pl.BlockSpec(memory_space=pltpu.HBM)
SMALL = 8 * 2**20
COST = 10**10
LARGE = 24 * 2**20


def iota(shape, dim):
    return lax.broadcasted_iota(jnp.int32, shape, dim)


def rim_kernel(eig_ref, inner_ref, outer_ref, sems):
    own = eig_ref.shape[1]
    odd = lax.rem(lax.axis_index("atom"), 2)
    copies = []
    for place, (flag, ref) in enumerate(((odd, outer_ref), (1 - odd, inner_ref))):
        rows = pl.ds(pl.multiple_of(flag * (own - RIM), RIM), RIM)
        copies.append(pltpu.make_async_copy(eig_ref.at[:, rows, :], ref, sems.at[place]))
    for copy in copies:
        copy.start()
    for copy in copies:
        copy.wait()


def halo_kernel(eig_ref, freq_ref, near_ref, far_ref, sems):
    comps, own, modes = eig_ref.shape
    high = lax.rem(lax.axis_index("mode"), 2)
    copies = []
    for place, (flag, ref) in enumerate(((1 - high, near_ref), (high, far_ref))):
        columns = pl.ds(pl.multiple_of(flag * (modes - HALF), HALF), HALF)
        target = ref.at[:, pl.ds(0, own), :]
        copies.append(pltpu.make_async_copy(eig_ref.at[:, :, columns], target, sems.at[place]))
    for copy in copies:
        copy.start()
    freq = freq_ref[...]
    rest = jnp.where(iota((EXTRA, HALF), 0) < EXTRA // 2, freq[:, 0:HALF], freq[:, modes - HALF : modes])
    for part in range(comps):
        piece = rest.astype(BF16)
        rest = rest - piece.astype(F32)
        near_ref[part, own : own + EXTRA, :] = piece
        far_ref[part, own : own + EXTRA, :] = piece
    for copy in copies:
        copy.wait()


def edge_call(kernel, shape, cost, *operands):
    return pl.pallas_call(
        kernel,
        out_shape=(jax.ShapeDtypeStruct(shape, BF16),) * 2,
        in_specs=[VMEM] * len(operands),
        out_specs=(VMEM,) * 2,
        scratch_shapes=[pltpu.SemaphoreType.DMA((2,))],
        compiler_params=pltpu.CompilerParams(vmem_limit_bytes=SMALL),
        cost_estimate=pl.CostEstimate(flops=cost, bytes_accessed=10**6, transcendentals=0),
    )(*operands)


def coupling_kernel(atoms, force_ref, bond_ref, nbr_ref, eig_ref, image_ref, rim_ref, *scratch):
    cpl_ref, diag_ref, hot_ref, own_ref = scratch
    comps, _, slots, own = force_ref.shape
    wide = slots * GROUP
    span = own + RIM
    start = lax.axis_index("atom") * own
    offset = nbr_ref[...] - start
    offset = jnp.where(offset < -RIM, offset + atoms, offset)
    offset = jnp.where(offset >= own + RIM, offset - atoms, offset)
    place = jnp.transpose((offset - RIM).astype(F32)).astype(BF16)
    spread = jnp.where(iota((slots, wide), 1) // GROUP == iota((slots, wide), 0), 1.0, 0.0).astype(BF16)
    same = iota((GROUP, wide), 0) == iota((GROUP, wide), 1) % GROUP
    placed = jnp.dot(place, spread, preferred_element_type=F32)
    bonds = [jnp.transpose(bond_ref[k]) for k in range(comps)]
    for c in range(comps):
        for d in range(comps):
            column = jnp.transpose(force_ref[c, d])
            for k in range(comps):
                cpl_ref[(k * comps + c) * comps + d] = (bonds[k] * column).astype(BF16)
    own_ids = iota((own, wide), 0) - RIM
    halves, groups, tall = own // RIM, RIM // GROUP, comps**3 * GROUP
    for h in range(halves):
        rim_ids = iota((RIM, wide), 0) + (-2 * RIM if h == 0 else own - RIM)
        ids = jnp.concatenate([own_ids, rim_ids], axis=0)
        for g in range(groups):
            base = h * RIM + g * GROUP
            row = jnp.sum(jnp.where(same, placed[base : base + GROUP], 0.0), axis=0, keepdims=True)
            hot_ref[h * groups + g] = jnp.where(ids == row.astype(jnp.int32), 1.0, 0.0).astype(BF16)
            part = cpl_ref[:, base : base + GROUP, :].reshape(tall, slots)
            diag = jnp.dot(part, spread, preferred_element_type=F32).reshape(comps**3, GROUP, wide)
            diag_ref[h * groups + g] = jnp.where(same[None], diag, 0.0).astype(BF16).reshape(tall, wide)
    eig = eig_ref[...].reshape(comps * own, eig_ref.shape[2])
    for h in range(halves):
        for g in range(groups):
            diag, hot = diag_ref[h * groups + g], hot_ref[h * groups + g]
            block = lax.dot_general(diag, hot, (((1,), (1,)), ((), ())), preferred_element_type=F32)
            block = block.astype(BF16)
            for kc in range(comps * comps):
                rows = slice(kc * RIM + g * GROUP, kc * RIM + (g + 1) * GROUP)
                for d in range(comps):
                    top = (kc * comps + d) * GROUP
                    piece = block[top : top + GROUP]
                    own_ref[h, rows, d * own : (d + 1) * own] = piece[:, :own]
                    rim_ref[h, rows, d * RIM : (d + 1) * RIM] = piece[:, own:span]
        image_ref[h] = jnp.dot(own_ref[h], eig, preferred_element_type=F32)


def own_image(force, bond, nbr, eigvec, atoms):
    comps, _, slots, own = force.shape
    halves, rows = own // RIM, comps * comps * RIM
    return pl.pallas_call(
        functools.partial(coupling_kernel, atoms),
        out_shape=(
            jax.ShapeDtypeStruct((halves, rows, eigvec.shape[2]), F32),
            jax.ShapeDtypeStruct((halves, rows, comps * RIM), BF16),
        ),
        in_specs=[VMEM] * 4,
        out_specs=(VMEM,) * 2,
        scratch_shapes=[
            pltpu.VMEM((comps**3, own, slots), BF16),
            pltpu.VMEM((own // GROUP, comps**3 * GROUP, slots * GROUP), BF16),
            pltpu.VMEM((own // GROUP, own + RIM, slots * GROUP), BF16),
            pltpu.VMEM((halves, rows, comps * own), BF16),
        ],
        compiler_params=pltpu.CompilerParams(vmem_limit_bytes=LARGE),
        cost_estimate=pl.CostEstimate(flops=4 * 10**9, bytes_accessed=6 * 10**6, transcendentals=0),
    )(force, bond, nbr, eigvec)


def main_kernel(image_ref, cpl_ref, own_ref, rim_one, rim_two, keep_ref, send_ref, cross_ref, flux_ref):
    comps, own, modes = own_ref.shape
    depth = comps * own
    odd = lax.rem(lax.axis_index("atom"), 2) == 1
    one = rim_one[...].reshape(comps * RIM, modes)
    two = rim_two[...].reshape(comps * RIM, modes)
    for h, rim in enumerate((jnp.where(odd, one, two), jnp.where(odd, two, one))):
        image = (image_ref[h] + jnp.dot(cpl_ref[h], rim, preferred_element_type=F32)).astype(BF16)
        for k in range(comps):
            for c in range(comps):
                top = (k * comps + c) * RIM
                flux_ref[c, h * RIM : (h + 1) * RIM, k * modes : (k + 1) * modes] = image[top : top + RIM]
    flux = flux_ref[...].reshape(depth, comps * modes)
    eig = own_ref[...].reshape(depth, modes)
    pairs = lax.dot_general(eig, flux, (((0,), (0,)), ((), ())), preferred_element_type=F32)
    equal = iota((HALF, HALF), 0) == iota((HALF, HALF), 1)
    for k in range(comps):
        left, middle, right = k * modes, k * modes + HALF, (k + 1) * modes
        above, below = pairs[HALF : 2 * HALF, left:middle], pairs[0:HALF, middle:right]
        first = jnp.where(equal, above, pairs[0:HALF, left:middle])
        second = jnp.where(equal, below, pairs[HALF : 2 * HALF, middle:right])
        keep_ref[k] = jnp.where(odd, second, first)
        send_ref[k] = jnp.where(odd, first, second).astype(BF16)
        cross_ref[0, k] = above
        cross_ref[1, k] = below


def side_kernel(flux_ref, cross_ref, halo_one, halo_two, keep_ref, send_ref):
    comps, own, wide = flux_ref.shape
    modes, depth = wide // comps, comps * own
    odd = lax.rem(lax.axis_index("atom"), 2) == 1
    high = lax.rem(lax.axis_index("mode"), 2) == 1
    flux = flux_ref[...].reshape(depth, wide)
    first = halo_one[:, 0:own, :].reshape(depth, HALF)
    second = halo_two[:, 0:own, :].reshape(depth, HALF)
    before = jnp.where(high, first, second)
    after = jnp.where(high, second, first)
    low_flux = jnp.concatenate([flux[:, k * modes : k * modes + HALF] for k in range(comps)], axis=1)
    high_flux = jnp.concatenate([flux[:, k * modes + HALF : (k + 1) * modes] for k in range(comps)], axis=1)
    contract = (((0,), (0,)), ((), ()))
    below = lax.dot_general(before, low_flux, contract, preferred_element_type=F32)
    above = lax.dot_general(after, high_flux, contract, preferred_element_type=F32)
    rows, columns = iota((HALF, HALF), 0), iota((HALF, HALF), 1)
    for k in range(comps):
        here = slice(k * HALF, (k + 1) * HALF)
        first = jnp.where(rows >= columns, below[:, here], cross_ref[0, k])
        second = jnp.where(rows > columns, cross_ref[1, k], above[:, here])
        keep_ref[k] = jnp.where(odd, second, first)
        send_ref[k] = jnp.where(odd, first, second).astype(BF16)


def pair_call(kernel, out_shape, flops, *operands):
    return pl.pallas_call(
        kernel,
        out_shape=tuple(jax.ShapeDtypeStruct(shape, kind) for shape, kind in out_shape),
        in_specs=[VMEM] * len(operands),
        out_specs=(VMEM,) * len(out_shape),
        compiler_params=pltpu.CompilerParams(vmem_limit_bytes=LARGE),
        cost_estimate=pl.CostEstimate(flops=flops, bytes_accessed=10**6, transcendentals=0),
    )(*operands)


def halo_freq(halo_ref, own):
    total = jnp.zeros((EXTRA, HALF), F32)
    for part in reversed(range(halo_ref.shape[0])):
        total = halo_ref[part, own : own + EXTRA, :].astype(F32) + total
    return total[0:1], total[EXTRA // 2 : EXTRA // 2 + 1]


def ends_kernel(own, freq_ref, halo_ref, out_ref):
    modes = freq_ref.shape[1]
    rows = (freq_ref[:, 0:HALF], freq_ref[:, modes - HALF : modes], *halo_freq(halo_ref, own))
    least = jnp.min(functools.reduce(jnp.minimum, rows), axis=1, keepdims=True)
    most = jnp.max(functools.reduce(jnp.maximum, rows), axis=1, keepdims=True)
    out_ref[...] = jnp.where(iota(out_ref.shape, 0) < 4, least, most)


def weigh_kernel(count, own, freq_ref, ends_ref, band_ref, halo_one, halo_two, main_one, main_two, side_one, side_two, out_ref):
    comps = main_one.shape[0]
    modes = freq_ref.shape[1]
    second = lax.rem(lax.axis_index("atom"), 2) == 1
    high = lax.rem(lax.axis_index("mode"), 2) == 1
    shift = jnp.where(second, HALF, 0)
    start = lax.axis_index("mode") * modes + shift
    (one_first, one_last), (two_first, two_last) = halo_freq(halo_one, own), halo_freq(halo_two, own)
    one, two = jnp.where(high, one_last, one_first), jnp.where(high, two_first, two_last)
    outside = jnp.where(high == second, two, one)
    inside = jnp.where(second, freq_ref[:, 0:HALF], freq_ref[:, HALF:modes])
    freq = jnp.where(second, freq_ref[:, HALF:modes], freq_ref[:, 0:HALF])
    prev = jnp.where(second, inside, outside)
    following = jnp.where(second, outside, inside)
    prev = jnp.where(start == 0, 1.0, prev)
    following = jnp.where(start == count - HALF, 1.0, following)
    band = jnp.where(second, band_ref[:, HALF:modes], band_ref[:, 0:HALF])
    low_end, high_end = band[0:1], band[1:2]
    eta = BROAD * (ends_ref[7:8, :] - ends_ref[0:1, :]) / (count - 1)

    def column(row):
        return jnp.transpose(jnp.broadcast_to(row, (HALF, HALF)))

    def weight(partner_freq, partner_ids, own_ids):
        within = (partner_ids >= low_end) & (partner_ids < high_end) & (partner_ids != own_ids)
        detune = freq - partner_freq
        total = freq + partner_freq
        scale = (eta / math.pi) * (total * total)
        value = scale / ((detune * detune + eta * eta) * (4.0 * freq * partner_freq))
        return jnp.where(within, value, 0.0)

    rows, columns = iota((HALF, HALF), 0), iota((HALF, HALF), 1)
    own_ids = start + columns
    corner = rows == columns
    corner_freq, corner_shift = jnp.where(second, prev, following), jnp.where(second, -HALF, HALF)
    main_freq = jnp.where(corner, corner_freq, column(freq))
    main_weight = weight(main_freq, start + rows + jnp.where(corner, corner_shift, 0), own_ids)
    lower = rows + jnp.where(second, 0, 1) > columns
    side_freq = jnp.where(lower, column(prev), column(following))
    side_weight = weight(side_freq, start + rows + jnp.where(lower, -HALF, HALF), own_ids)
    main_strength = jnp.zeros((HALF, HALF), F32)
    side_strength = jnp.zeros((HALF, HALF), F32)
    for k in range(comps):
        main = main_one[k].astype(F32) + main_two[k].astype(F32)
        side = side_one[k].astype(F32) + side_two[k].astype(F32)
        main_strength += main * main
        side_strength += side * side
    total = jnp.sum(main_weight * main_strength + side_weight * side_strength, axis=0, keepdims=True)
    diff = math.pi / (3.0 * freq * freq) * total
    grown = jnp.exp(freq)
    carried = freq * freq * grown / ((grown - 1.0) * (grown - 1.0)) * diff
    out_ref[0:1] = diff
    out_ref[1:2] = carried
    out_ref[2:8] = jnp.broadcast_to(jnp.sum(carried, axis=1, keepdims=True), (6, HALF))


def local_call(kernel, out_shape, *operands):
    return pl.pallas_call(
        kernel,
        out_shape=out_shape,
        in_specs=[VMEM] * len(operands),
        out_specs=jax.tree.map(lambda _: VMEM, out_shape),
        compiler_params=pltpu.CompilerParams(vmem_limit_bytes=SMALL),
        cost_estimate=pl.CostEstimate(flops=10**6, bytes_accessed=10**6, transcendentals=0),
    )(*operands)


def running_kernel(modes, own_ref, other_ref, diff_ref, run_ref):
    odd = lax.rem(lax.axis_index("atom"), 2) == 1
    own, other = own_ref[...], other_ref[...]
    whole = jnp.concatenate([jnp.where(odd, other, own), jnp.where(odd, own, other)], axis=1)
    diff_ref[...] = whole[0:1]
    until = jnp.where(iota((modes, modes), 0) <= iota((modes, modes), 1), 1.0, 0.0)
    running = jnp.dot(whole, until, precision=lax.Precision.HIGHEST, preferred_element_type=F32)
    run_ref[...] = running[1:2]


def last_kernel(run_ref, earlier_ref, out_ref):
    modes = run_ref.shape[1]
    out_ref[...] = (run_ref[...] + earlier_ref[0:1, 0:1]) / modes


def swap(x, axis, bit):
    return lax.ppermute(x, axis, [(i, i ^ bit) for i in range(lax.axis_size(axis))])


def upward(blocks, bit):
    low = [i for i in range(blocks) if i < i ^ bit]
    high = [i for i in range(blocks) if i > i ^ bit]
    return {**{i: i ^ bit for i in low}, **dict(zip(high, low))}


def bits_of(axis):
    return [1 << b for b in range(lax.axis_size(axis).bit_length() - 1)]


def rounded_sum(own, other):
    total = own.astype(F32) + other.astype(F32)
    return lax.reduce_precision(total, 8, 7).astype(BF16)


def body(eigvec, force, bond, nbr, band, freq):
    domains, blocks = lax.axis_size("atom"), lax.axis_size("mode")
    comps, own, modes = eigvec.shape
    atoms, count = own * domains, modes * blocks
    block = lax.axis_index("mode")
    freq_row = freq.reshape(1, modes)
    inner = [(i, i ^ 1) for i in range(domains)]
    outer = [(i, (i + 1) % domains if i % 2 else (i - 1) % domains) for i in range(domains)]
    near = [(i, i ^ 1) for i in range(blocks)]
    far = [(i, i + 1 if i % 2 else i - 1) for i in range(1, blocks - 1)]
    inner_edge, outer_edge = edge_call(rim_kernel, (comps, RIM, modes), COST, eigvec)
    outer_edge, later = lax.optimization_barrier((outer_edge, freq_row))
    near_edge, far_edge = edge_call(halo_kernel, (comps, own + EXTRA, HALF), COST, eigvec, later)
    near_edge, held = lax.optimization_barrier((near_edge, eigvec))
    rim_two = lax.ppermute(outer_edge, "atom", outer)
    rim_one = lax.ppermute(inner_edge, "atom", inner)
    halo_one = lax.ppermute(near_edge, "mode", near)
    hops = []
    for a in range(domains):
        for i in range(blocks):
            inside = 0 < i < blocks - 1
            hops.append((a * blocks + i, a * blocks + (i + 1 if i % 2 else i - 1) if inside else (a ^ 1) * blocks + i))
    halo_two = lax.ppermute(far_edge, ("atom", "mode"), hops)

    image, matrix = own_image(force, bond, nbr, held, atoms)
    square = (comps, HALF, HALF)
    keep_main, send_main, cross, flux = pair_call(
        main_kernel,
        ((square, F32), (square, BF16), ((2, *square), F32), ((comps, own, comps * modes), BF16)),
        10**9, image, matrix, eigvec, rim_one, rim_two,
    )
    keep_side, send_side = pair_call(
        side_kernel, ((square, F32), (square, BF16)), 10**9, flux, cross, halo_one, halo_two
    )

    tile = jax.ShapeDtypeStruct((8, HALF), F32)
    row = jax.ShapeDtypeStruct((1, modes), F32)
    main = rounded_sum(keep_main, swap(send_main, "atom", 1))
    side = rounded_sum(keep_side, swap(send_side, "atom", 1))
    side, own_freq = lax.optimization_barrier((side, freq_row))
    ends = local_call(functools.partial(ends_kernel, own), tile, own_freq, halo_one)
    steps = bits_of("atom")[1:]
    for step, (one, two) in enumerate(zip(steps, reversed(steps))):
        main_other, side_other = swap(main, "atom", one), swap(side, "atom", two)
        if step < len(steps) - 1:
            main, side = rounded_sum(main, main_other), rounded_sum(side, side_other)
    for bit in bits_of("mode")[1:]:
        other = swap(ends, "mode", bit)
        ends = jnp.where(iota((8, HALF), 0) < 4, jnp.minimum(ends, other), jnp.maximum(ends, other))
    summary = local_call(
        functools.partial(weigh_kernel, count, own),
        tile, freq_row, ends, band, halo_one, halo_two, main, main_other, side, side_other,
    )

    other = swap(summary, "atom", 1)
    diff, running = local_call(functools.partial(running_kernel, modes), (row, row), summary, other)
    total = summary + other
    odd = lax.rem(lax.axis_index("atom"), 2) == 1
    held = jnp.zeros_like(total)
    for high in range(blocks - 1, 1, -2):
        routes = upward(blocks, high), upward(blocks, high - 1)
        mixed = [(a * blocks + i, a * blocks + routes[a % 2][i]) for a in range(domains) for i in range(blocks)]
        part = lax.ppermute(total, ("atom", "mode"), mixed)
        source = block ^ jnp.where(odd, high - 1, high)
        held = held + jnp.where(source < block, part, 0.0)
    near_part = jnp.where((block & 1) != 0, swap(total, "mode", 1), 0.0)
    earlier = (held + swap(held, "atom", 1)) + near_part
    conductivity = local_call(last_kernel, row, running, earlier[2:3])
    return diff.reshape(modes), conductivity.reshape(modes)


def solution(mesh):
    in_specs = (
        P(None, "atom", "mode"),
        P(None, None, None, "atom"),
        P(None, None, "atom"),
        P(None, "atom"),
        P(None, "mode"),
        P("mode"),
    )
    out_specs = (P("mode"), P("mode"))
    return jax.shard_map(body, mesh=mesh, in_specs=in_specs, out_specs=out_specs, check_vma=False)
```

```python
import functools
import math

import jax
import jax.numpy as jnp
from jax import lax
from jax.experimental import pallas as pl
from jax.experimental.pallas import tpu as pltpu
from jax.sharding import PartitionSpec as P

RIM = 128
HALF = 128
BROAD = 128
GROUP = 16
EXTRA = 16
F32 = jnp.float32
BF16 = jnp.bfloat16
VMEM = pl.BlockSpec(memory_space=pltpu.VMEM)
HBM = pl.BlockSpec(memory_space=pltpu.HBM)
SMALL = 8 * 2**20
COST = 10**10
LARGE = 24 * 2**20


def iota(shape, dim):
    return lax.broadcasted_iota(jnp.int32, shape, dim)


def rim_kernel(eig_ref, inner_ref, outer_ref, sems):
    own = eig_ref.shape[1]
    odd = lax.rem(lax.axis_index("atom"), 2)
    copies = []
    for place, (flag, ref) in enumerate(((odd, outer_ref), (1 - odd, inner_ref))):
        rows = pl.ds(pl.multiple_of(flag * (own - RIM), RIM), RIM)
        copies.append(pltpu.make_async_copy(eig_ref.at[:, rows, :], ref, sems.at[place]))
    for copy in copies:
        copy.start()
    for copy in copies:
        copy.wait()


def halo_kernel(eig_ref, freq_ref, near_ref, far_ref, sems):
    comps, own, modes = eig_ref.shape
    high = lax.rem(lax.axis_index("mode"), 2)
    copies = []
    for place, (flag, ref) in enumerate(((1 - high, near_ref), (high, far_ref))):
        columns = pl.ds(pl.multiple_of(flag * (modes - HALF), HALF), HALF)
        for c in range(comps):
            target = ref.at[pl.ds(c * own, own), :]
            copies.append(pltpu.make_async_copy(eig_ref.at[c, :, columns], target, sems.at[place * comps + c]))
    for copy in copies:
        copy.start()
    freq = freq_ref[...]
    row = iota((EXTRA, HALF), 0)
    rest = jnp.where(row < EXTRA // 2, freq[:, 0:HALF], freq[:, modes - HALF : modes])
    tail = jnp.zeros((EXTRA, HALF), F32)
    for part in range(comps):
        piece = rest.astype(BF16).astype(F32)
        rest = rest - piece
        tail = jnp.where(row % (EXTRA // 2) == part, piece, tail)
    near_ref[comps * own : comps * own + EXTRA, :] = tail.astype(BF16)
    far_ref[comps * own : comps * own + EXTRA, :] = tail.astype(BF16)
    for copy in copies:
        copy.wait()


def edge_call(kernel, shape, cost, *operands):
    return pl.pallas_call(
        kernel,
        out_shape=(jax.ShapeDtypeStruct(shape, BF16),) * 2,
        in_specs=[VMEM] * len(operands),
        out_specs=(VMEM,) * 2,
        scratch_shapes=[pltpu.SemaphoreType.DMA((2 * operands[0].shape[0],))],
        compiler_params=pltpu.CompilerParams(vmem_limit_bytes=SMALL),
        cost_estimate=pl.CostEstimate(flops=cost, bytes_accessed=10**6, transcendentals=0),
    )(*operands)


def coupling_kernel(atoms, force_ref, bond_ref, nbr_ref, eig_ref, image_ref, rim_ref, *scratch):
    cpl_ref, diag_ref, hot_ref, own_ref = scratch
    comps, _, slots, own = force_ref.shape
    wide = slots * GROUP
    span = own + RIM
    start = lax.axis_index("atom") * own
    offset = nbr_ref[...] - start
    offset = jnp.where(offset < -RIM, offset + atoms, offset)
    offset = jnp.where(offset >= own + RIM, offset - atoms, offset)
    place = jnp.transpose((offset - RIM).astype(F32)).astype(BF16)
    spread = jnp.where(iota((slots, wide), 1) // GROUP == iota((slots, wide), 0), 1.0, 0.0).astype(BF16)
    same = iota((GROUP, wide), 0) == iota((GROUP, wide), 1) % GROUP
    placed = jnp.dot(place, spread, preferred_element_type=F32)
    bonds = [jnp.transpose(bond_ref[k]) for k in range(comps)]
    for c in range(comps):
        for d in range(comps):
            column = jnp.transpose(force_ref[c, d])
            for k in range(comps):
                cpl_ref[(k * comps + c) * comps + d] = (bonds[k] * column).astype(BF16)
    own_ids = iota((own, wide), 0) - RIM
    halves, groups, tall = own // RIM, RIM // GROUP, comps**3 * GROUP
    for h in range(halves):
        rim_ids = iota((RIM, wide), 0) + (-2 * RIM if h == 0 else own - RIM)
        ids = jnp.concatenate([own_ids, rim_ids], axis=0)
        for g in range(groups):
            base = h * RIM + g * GROUP
            row = jnp.sum(jnp.where(same, placed[base : base + GROUP], 0.0), axis=0, keepdims=True)
            hot_ref[h * groups + g] = jnp.where(ids == row.astype(jnp.int32), 1.0, 0.0).astype(BF16)
            part = cpl_ref[:, base : base + GROUP, :].reshape(tall, slots)
            diag = jnp.dot(part, spread, preferred_element_type=F32).reshape(comps**3, GROUP, wide)
            diag_ref[h * groups + g] = jnp.where(same[None], diag, 0.0).astype(BF16).reshape(tall, wide)
    eig = eig_ref[...].reshape(comps * own, eig_ref.shape[2])
    for h in range(halves):
        for g in range(groups):
            diag, hot = diag_ref[h * groups + g], hot_ref[h * groups + g]
            block = lax.dot_general(diag, hot, (((1,), (1,)), ((), ())), preferred_element_type=F32)
            block = block.astype(BF16)
            for kc in range(comps * comps):
                rows = slice(kc * RIM + g * GROUP, kc * RIM + (g + 1) * GROUP)
                for d in range(comps):
                    top = (kc * comps + d) * GROUP
                    piece = block[top : top + GROUP]
                    own_ref[h, rows, d * own : (d + 1) * own] = piece[:, :own]
                    rim_ref[h, rows, d * RIM : (d + 1) * RIM] = piece[:, own:span]
        image_ref[h] = jnp.dot(own_ref[h], eig, preferred_element_type=F32)


def own_image(force, bond, nbr, eigvec, atoms):
    comps, _, slots, own = force.shape
    halves, rows = own // RIM, comps * comps * RIM
    return pl.pallas_call(
        functools.partial(coupling_kernel, atoms),
        out_shape=(
            jax.ShapeDtypeStruct((halves, rows, eigvec.shape[2]), F32),
            jax.ShapeDtypeStruct((halves, rows, comps * RIM), BF16),
        ),
        in_specs=[VMEM] * 4,
        out_specs=(VMEM,) * 2,
        scratch_shapes=[
            pltpu.VMEM((comps**3, own, slots), BF16),
            pltpu.VMEM((own // GROUP, comps**3 * GROUP, slots * GROUP), BF16),
            pltpu.VMEM((own // GROUP, own + RIM, slots * GROUP), BF16),
            pltpu.VMEM((halves, rows, comps * own), BF16),
        ],
        compiler_params=pltpu.CompilerParams(vmem_limit_bytes=LARGE),
        cost_estimate=pl.CostEstimate(flops=4 * 10**9, bytes_accessed=6 * 10**6, transcendentals=0),
    )(force, bond, nbr, eigvec)


def main_kernel(image_ref, cpl_ref, own_ref, rim_one, rim_two, keep_ref, send_ref, cross_ref, flux_ref):
    comps, own, modes = own_ref.shape
    depth = comps * own
    odd = lax.rem(lax.axis_index("atom"), 2) == 1
    one = rim_one[...].reshape(comps * RIM, modes)
    two = rim_two[...].reshape(comps * RIM, modes)
    for h, rim in enumerate((jnp.where(odd, one, two), jnp.where(odd, two, one))):
        image = (image_ref[h] + jnp.dot(cpl_ref[h], rim, preferred_element_type=F32)).astype(BF16)
        for k in range(comps):
            for c in range(comps):
                top = (k * comps + c) * RIM
                flux_ref[c, h * RIM : (h + 1) * RIM, k * modes : (k + 1) * modes] = image[top : top + RIM]
    flux = flux_ref[...].reshape(depth, comps * modes)
    eig = own_ref[...].reshape(depth, modes)
    pairs = lax.dot_general(eig, flux, (((0,), (0,)), ((), ())), preferred_element_type=F32)
    equal = iota((HALF, HALF), 0) == iota((HALF, HALF), 1)
    for k in range(comps):
        left, middle, right = k * modes, k * modes + HALF, (k + 1) * modes
        above, below = pairs[HALF : 2 * HALF, left:middle], pairs[0:HALF, middle:right]
        first = jnp.where(equal, above, pairs[0:HALF, left:middle])
        second = jnp.where(equal, below, pairs[HALF : 2 * HALF, middle:right])
        keep_ref[k] = jnp.where(odd, second, first)
        send_ref[k] = jnp.where(odd, first, second).astype(BF16)
        cross_ref[0, k] = above
        cross_ref[1, k] = below


def side_kernel(flux_ref, cross_ref, halo_one, halo_two, keep_ref, send_ref):
    comps, own, wide = flux_ref.shape
    modes, depth = wide // comps, comps * own
    odd = lax.rem(lax.axis_index("atom"), 2) == 1
    high = lax.rem(lax.axis_index("mode"), 2) == 1
    flux = flux_ref[...].reshape(depth, wide)
    first, second = halo_one[0:depth, :], halo_two[0:depth, :]
    before = jnp.where(high, first, second)
    after = jnp.where(high, second, first)
    low_flux = jnp.concatenate([flux[:, k * modes : k * modes + HALF] for k in range(comps)], axis=1)
    high_flux = jnp.concatenate([flux[:, k * modes + HALF : (k + 1) * modes] for k in range(comps)], axis=1)
    contract = (((0,), (0,)), ((), ()))
    below = lax.dot_general(before, low_flux, contract, preferred_element_type=F32)
    above = lax.dot_general(after, high_flux, contract, preferred_element_type=F32)
    rows, columns = iota((HALF, HALF), 0), iota((HALF, HALF), 1)
    for k in range(comps):
        here = slice(k * HALF, (k + 1) * HALF)
        first = jnp.where(rows >= columns, below[:, here], cross_ref[0, k])
        second = jnp.where(rows > columns, cross_ref[1, k], above[:, here])
        keep_ref[k] = jnp.where(odd, second, first)
        send_ref[k] = jnp.where(odd, first, second).astype(BF16)


def pair_call(kernel, out_shape, flops, *operands):
    return pl.pallas_call(
        kernel,
        out_shape=tuple(jax.ShapeDtypeStruct(shape, kind) for shape, kind in out_shape),
        in_specs=[VMEM] * len(operands),
        out_specs=(VMEM,) * len(out_shape),
        compiler_params=pltpu.CompilerParams(vmem_limit_bytes=LARGE),
        cost_estimate=pl.CostEstimate(flops=flops, bytes_accessed=10**6, transcendentals=0),
    )(*operands)


def halo_freq(halo_ref, comps):
    tail = halo_ref[halo_ref.shape[0] - EXTRA :, :].astype(F32)
    rows = []
    for top in (0, EXTRA // 2):
        total = jnp.zeros((1, HALF), F32)
        for part in reversed(range(comps)):
            total = tail[top + part : top + part + 1] + total
        rows.append(total)
    return rows


def ends_kernel(comps, freq_ref, halo_ref, out_ref):
    modes = freq_ref.shape[1]
    rows = (freq_ref[:, 0:HALF], freq_ref[:, modes - HALF : modes], *halo_freq(halo_ref, comps))
    least = jnp.min(functools.reduce(jnp.minimum, rows), axis=1, keepdims=True)
    most = jnp.max(functools.reduce(jnp.maximum, rows), axis=1, keepdims=True)
    out_ref[...] = jnp.where(iota(out_ref.shape, 0) < 4, least, most)


def weigh_kernel(count, comps, freq_ref, ends_ref, band_ref, halo_one, halo_two, main_one, main_two, side_one, side_two, out_ref):
    modes = freq_ref.shape[1]
    second = lax.rem(lax.axis_index("atom"), 2) == 1
    high = lax.rem(lax.axis_index("mode"), 2) == 1
    shift = jnp.where(second, HALF, 0)
    start = lax.axis_index("mode") * modes + shift
    (one_first, one_last), (two_first, two_last) = halo_freq(halo_one, comps), halo_freq(halo_two, comps)
    one, two = jnp.where(high, one_last, one_first), jnp.where(high, two_first, two_last)
    outside = jnp.where(high == second, two, one)
    inside = jnp.where(second, freq_ref[:, 0:HALF], freq_ref[:, HALF:modes])
    freq = jnp.where(second, freq_ref[:, HALF:modes], freq_ref[:, 0:HALF])
    prev = jnp.where(second, inside, outside)
    following = jnp.where(second, outside, inside)
    prev = jnp.where(start == 0, 1.0, prev)
    following = jnp.where(start == count - HALF, 1.0, following)
    band = jnp.where(second, band_ref[:, HALF:modes], band_ref[:, 0:HALF])
    low_end, high_end = band[0:1], band[1:2]
    eta = BROAD * (ends_ref[7:8, :] - ends_ref[0:1, :]) / (count - 1)

    def column(row):
        return jnp.transpose(jnp.broadcast_to(row, (HALF, HALF)))

    def weight(partner_freq, partner_ids, own_ids):
        within = (partner_ids >= low_end) & (partner_ids < high_end) & (partner_ids != own_ids)
        detune = freq - partner_freq
        total = freq + partner_freq
        scale = (eta / math.pi) * (total * total)
        value = scale / ((detune * detune + eta * eta) * (4.0 * freq * partner_freq))
        return jnp.where(within, value, 0.0)

    rows, columns = iota((HALF, HALF), 0), iota((HALF, HALF), 1)
    own_ids = start + columns
    corner = rows == columns
    corner_freq, corner_shift = jnp.where(second, prev, following), jnp.where(second, -HALF, HALF)
    main_freq = jnp.where(corner, corner_freq, column(freq))
    main_weight = weight(main_freq, start + rows + jnp.where(corner, corner_shift, 0), own_ids)
    lower = rows + jnp.where(second, 0, 1) > columns
    side_freq = jnp.where(lower, column(prev), column(following))
    side_weight = weight(side_freq, start + rows + jnp.where(lower, -HALF, HALF), own_ids)
    main_strength = jnp.zeros((HALF, HALF), F32)
    side_strength = jnp.zeros((HALF, HALF), F32)
    for k in range(comps):
        main = main_one[k].astype(F32) + main_two[k].astype(F32)
        side = side_one[k].astype(F32) + side_two[k].astype(F32)
        main_strength += main * main
        side_strength += side * side
    total = jnp.sum(main_weight * main_strength + side_weight * side_strength, axis=0, keepdims=True)
    diff = math.pi / (3.0 * freq * freq) * total
    grown = jnp.exp(freq)
    carried = freq * freq * grown / ((grown - 1.0) * (grown - 1.0)) * diff
    out_ref[0:1] = diff
    out_ref[1:2] = carried
    out_ref[2:8] = jnp.broadcast_to(jnp.sum(carried, axis=1, keepdims=True), (6, HALF))


def local_call(kernel, out_shape, *operands):
    return pl.pallas_call(
        kernel,
        out_shape=out_shape,
        in_specs=[VMEM] * len(operands),
        out_specs=jax.tree.map(lambda _: VMEM, out_shape),
        compiler_params=pltpu.CompilerParams(vmem_limit_bytes=SMALL),
        cost_estimate=pl.CostEstimate(flops=10**6, bytes_accessed=10**6, transcendentals=0),
    )(*operands)


def running_kernel(modes, own_ref, other_ref, diff_ref, run_ref):
    odd = lax.rem(lax.axis_index("atom"), 2) == 1
    own, other = own_ref[...], other_ref[...]
    whole = jnp.concatenate([jnp.where(odd, other, own), jnp.where(odd, own, other)], axis=1)
    diff_ref[...] = whole[0:1]
    until = jnp.where(iota((modes, modes), 0) <= iota((modes, modes), 1), 1.0, 0.0)
    running = jnp.dot(whole, until, precision=lax.Precision.HIGHEST, preferred_element_type=F32)
    run_ref[...] = running[1:2]


def last_kernel(run_ref, earlier_ref, out_ref):
    modes = run_ref.shape[1]
    out_ref[...] = (run_ref[...] + earlier_ref[0:1, 0:1]) / modes


def swap(x, axis, bit):
    return lax.ppermute(x, axis, [(i, i ^ bit) for i in range(lax.axis_size(axis))])


def upward(blocks, bit):
    low = [i for i in range(blocks) if i < i ^ bit]
    high = [i for i in range(blocks) if i > i ^ bit]
    return {**{i: i ^ bit for i in low}, **dict(zip(high, low))}


def bits_of(axis):
    return [1 << b for b in range(lax.axis_size(axis).bit_length() - 1)]


def rounded_sum(own, other):
    total = own.astype(F32) + other.astype(F32)
    return lax.reduce_precision(total, 8, 7).astype(BF16)


def body(eigvec, force, bond, nbr, band, freq):
    domains, blocks = lax.axis_size("atom"), lax.axis_size("mode")
    comps, own, modes = eigvec.shape
    atoms, count = own * domains, modes * blocks
    block = lax.axis_index("mode")
    freq_row = freq.reshape(1, modes)
    inner = [(i, i ^ 1) for i in range(domains)]
    outer = [(i, (i + 1) % domains if i % 2 else (i - 1) % domains) for i in range(domains)]
    near = [(i, i ^ 1) for i in range(blocks)]
    far = [(i, i + 1 if i % 2 else i - 1) for i in range(1, blocks - 1)]
    inner_edge, outer_edge = edge_call(rim_kernel, (comps, RIM, modes), COST, eigvec)
    outer_edge, later = lax.optimization_barrier((outer_edge, freq_row))
    near_edge, far_edge = edge_call(halo_kernel, (comps * own + EXTRA, HALF), COST, eigvec, later)
    near_edge, held = lax.optimization_barrier((near_edge, eigvec))
    rim_two = lax.ppermute(outer_edge, "atom", outer)
    rim_one = lax.ppermute(inner_edge, "atom", inner)
    halo_one = lax.ppermute(near_edge, "mode", near)
    hops = []
    for a in range(domains):
        for i in range(blocks):
            inside = 0 < i < blocks - 1
            hops.append((a * blocks + i, a * blocks + (i + 1 if i % 2 else i - 1) if inside else (a ^ 1) * blocks + i))
    halo_two = lax.ppermute(far_edge, ("atom", "mode"), hops)

    image, matrix = own_image(force, bond, nbr, held, atoms)
    square = (comps, HALF, HALF)
    keep_main, send_main, cross, flux = pair_call(
        main_kernel,
        ((square, F32), (square, BF16), ((2, *square), F32), ((comps, own, comps * modes), BF16)),
        10**9, image, matrix, eigvec, rim_one, rim_two,
    )
    keep_side, send_side = pair_call(
        side_kernel, ((square, F32), (square, BF16)), 10**9, flux, cross, halo_one, halo_two
    )

    tile = jax.ShapeDtypeStruct((8, HALF), F32)
    row = jax.ShapeDtypeStruct((1, modes), F32)
    main = rounded_sum(keep_main, swap(send_main, "atom", 1))
    side = rounded_sum(keep_side, swap(send_side, "atom", 1))
    side, own_freq = lax.optimization_barrier((side, freq_row))
    ends = local_call(functools.partial(ends_kernel, comps), tile, own_freq, halo_one)
    steps = bits_of("atom")[1:]
    for step, (one, two) in enumerate(zip(steps, reversed(steps))):
        main_other, side_other = swap(main, "atom", one), swap(side, "atom", two)
        if step < len(steps) - 1:
            main, side = rounded_sum(main, main_other), rounded_sum(side, side_other)
    for bit in bits_of("mode")[1:]:
        other = swap(ends, "mode", bit)
        ends = jnp.where(iota((8, HALF), 0) < 4, jnp.minimum(ends, other), jnp.maximum(ends, other))
    summary = local_call(
        functools.partial(weigh_kernel, count, comps),
        tile, freq_row, ends, band, halo_one, halo_two, main, main_other, side, side_other,
    )

    other = swap(summary, "atom", 1)
    diff, running = local_call(functools.partial(running_kernel, modes), (row, row), summary, other)
    total = summary + other
    odd = lax.rem(lax.axis_index("atom"), 2) == 1
    held = jnp.zeros_like(total)
    for high in range(blocks - 1, 1, -2):
        routes = upward(blocks, high), upward(blocks, high - 1)
        mixed = [(a * blocks + i, a * blocks + routes[a % 2][i]) for a in range(domains) for i in range(blocks)]
        part = lax.ppermute(total, ("atom", "mode"), mixed)
        source = block ^ jnp.where(odd, high - 1, high)
        held = held + jnp.where(source < block, part, 0.0)
    near_part = jnp.where((block & 1) != 0, swap(total, "mode", 1), 0.0)
    earlier = (held + swap(held, "atom", 1)) + near_part
    conductivity = local_call(last_kernel, row, running, earlier[2:3])
    return diff.reshape(modes), conductivity.reshape(modes)


def solution(mesh):
    in_specs = (
        P(None, "atom", "mode"),
        P(None, None, None, "atom"),
        P(None, None, "atom"),
        P(None, "atom"),
        P(None, "mode"),
        P("mode"),
    )
    out_specs = (P("mode"), P("mode"))
    return jax.shard_map(body, mesh=mesh, in_specs=in_specs, out_specs=out_specs, check_vma=False)
```

```python
import functools
import math

import jax
import jax.numpy as jnp
from jax import lax
from jax.experimental import pallas as pl
from jax.experimental.pallas import tpu as pltpu
from jax.sharding import PartitionSpec as P

RIM = 128
HALF = 128
BROAD = 128
GROUP = 16
EXTRA = 16
F32 = jnp.float32
BF16 = jnp.bfloat16
VMEM = pl.BlockSpec(memory_space=pltpu.VMEM)
HBM = pl.BlockSpec(memory_space=pltpu.HBM)
SMALL = 8 * 2**20
COST = 10**10
LARGE = 24 * 2**20


def iota(shape, dim):
    return lax.broadcasted_iota(jnp.int32, shape, dim)


def rim_kernel(eig_ref, inner_ref, outer_ref, sems):
    own = eig_ref.shape[1]
    odd = lax.rem(lax.axis_index("atom"), 2)
    copies = []
    for place, (flag, ref) in enumerate(((odd, outer_ref), (1 - odd, inner_ref))):
        rows = pl.ds(pl.multiple_of(flag * (own - RIM), RIM), RIM)
        copies.append(pltpu.make_async_copy(eig_ref.at[:, rows, :], ref, sems.at[place]))
    for copy in copies:
        copy.start()
    for copy in copies:
        copy.wait()


def halo_kernel(eig_ref, freq_ref, near_ref, far_ref, sems):
    comps, own, modes = eig_ref.shape
    high = lax.rem(lax.axis_index("mode"), 2)
    copies = []
    for place, (flag, ref) in enumerate(((1 - high, near_ref), (high, far_ref))):
        columns = pl.ds(pl.multiple_of(flag * (modes - HALF), HALF), HALF)
        for c in range(comps):
            target = ref.at[pl.ds(c * own, own), :]
            copies.append(pltpu.make_async_copy(eig_ref.at[c, :, columns], target, sems.at[place * comps + c]))
    for copy in copies:
        copy.start()
    freq = freq_ref[...]
    row = iota((EXTRA, HALF), 0)
    rest = jnp.where(row < EXTRA // 2, freq[:, 0:HALF], freq[:, modes - HALF : modes])
    tail = jnp.zeros((EXTRA, HALF), F32)
    for part in range(comps):
        piece = rest.astype(BF16).astype(F32)
        rest = rest - piece
        tail = jnp.where(row % (EXTRA // 2) == part, piece, tail)
    near_ref[comps * own : comps * own + EXTRA, :] = tail.astype(BF16)
    far_ref[comps * own : comps * own + EXTRA, :] = tail.astype(BF16)
    for copy in copies:
        copy.wait()


def edge_call(kernel, shape, cost, *operands):
    return pl.pallas_call(
        kernel,
        out_shape=(jax.ShapeDtypeStruct(shape, BF16),) * 2,
        in_specs=[VMEM] * len(operands),
        out_specs=(VMEM,) * 2,
        scratch_shapes=[pltpu.SemaphoreType.DMA((2 * operands[0].shape[0],))],
        compiler_params=pltpu.CompilerParams(vmem_limit_bytes=SMALL),
        cost_estimate=pl.CostEstimate(flops=cost, bytes_accessed=10**6, transcendentals=0),
    )(*operands)


def coupling_kernel(atoms, force_ref, bond_ref, nbr_ref, eig_ref, image_ref, rim_ref, *scratch):
    cpl_ref, diag_ref, hot_ref, own_ref = scratch
    comps, _, slots, own = force_ref.shape
    wide = slots * GROUP
    span = own + RIM
    start = lax.axis_index("atom") * own
    offset = nbr_ref[...] - start
    offset = jnp.where(offset < -RIM, offset + atoms, offset)
    offset = jnp.where(offset >= own + RIM, offset - atoms, offset)
    place = jnp.transpose((offset - RIM).astype(F32)).astype(BF16)
    spread = jnp.where(iota((slots, wide), 1) // GROUP == iota((slots, wide), 0), 1.0, 0.0).astype(BF16)
    same = iota((GROUP, wide), 0) == iota((GROUP, wide), 1) % GROUP
    placed = jnp.dot(place, spread, preferred_element_type=F32)
    bonds = [jnp.transpose(bond_ref[k]) for k in range(comps)]
    for c in range(comps):
        for d in range(comps):
            column = jnp.transpose(force_ref[c, d])
            for k in range(comps):
                cpl_ref[(k * comps + c) * comps + d] = (bonds[k] * column).astype(BF16)
    own_ids = iota((own, wide), 0) - RIM
    halves, groups, tall = own // RIM, RIM // GROUP, comps**3 * GROUP
    for h in range(halves):
        rim_ids = iota((RIM, wide), 0) + (-2 * RIM if h == 0 else own - RIM)
        ids = jnp.concatenate([own_ids, rim_ids], axis=0)
        for g in range(groups):
            base = h * RIM + g * GROUP
            row = jnp.sum(jnp.where(same, placed[base : base + GROUP], 0.0), axis=0, keepdims=True)
            hot_ref[h * groups + g] = jnp.where(ids == row.astype(jnp.int32), 1.0, 0.0).astype(BF16)
            part = cpl_ref[:, base : base + GROUP, :].reshape(tall, slots)
            diag = jnp.dot(part, spread, preferred_element_type=F32).reshape(comps**3, GROUP, wide)
            diag_ref[h * groups + g] = jnp.where(same[None], diag, 0.0).astype(BF16).reshape(tall, wide)
    eig = eig_ref[...].reshape(comps * own, eig_ref.shape[2])
    for h in range(halves):
        for g in range(groups):
            diag, hot = diag_ref[h * groups + g], hot_ref[h * groups + g]
            block = lax.dot_general(diag, hot, (((1,), (1,)), ((), ())), preferred_element_type=F32)
            block = block.astype(BF16)
            for kc in range(comps * comps):
                rows = slice(kc * RIM + g * GROUP, kc * RIM + (g + 1) * GROUP)
                for d in range(comps):
                    top = (kc * comps + d) * GROUP
                    piece = block[top : top + GROUP]
                    own_ref[h, rows, d * own : (d + 1) * own] = piece[:, :own]
                    rim_ref[h, rows, d * RIM : (d + 1) * RIM] = piece[:, own:span]
        image_ref[h] = jnp.dot(own_ref[h], eig, preferred_element_type=F32)


def own_image(force, bond, nbr, eigvec, atoms):
    comps, _, slots, own = force.shape
    halves, rows = own // RIM, comps * comps * RIM
    return pl.pallas_call(
        functools.partial(coupling_kernel, atoms),
        out_shape=(
            jax.ShapeDtypeStruct((halves, rows, eigvec.shape[2]), F32),
            jax.ShapeDtypeStruct((halves, rows, comps * RIM), BF16),
        ),
        in_specs=[VMEM] * 4,
        out_specs=(VMEM,) * 2,
        scratch_shapes=[
            pltpu.VMEM((comps**3, own, slots), BF16),
            pltpu.VMEM((own // GROUP, comps**3 * GROUP, slots * GROUP), BF16),
            pltpu.VMEM((own // GROUP, own + RIM, slots * GROUP), BF16),
            pltpu.VMEM((halves, rows, comps * own), BF16),
        ],
        compiler_params=pltpu.CompilerParams(vmem_limit_bytes=LARGE),
        cost_estimate=pl.CostEstimate(flops=4 * 10**9, bytes_accessed=6 * 10**6, transcendentals=0),
    )(force, bond, nbr, eigvec)


def main_kernel(image_ref, cpl_ref, own_ref, rim_one, rim_two, keep_ref, send_ref, cross_ref, flux_ref):
    comps, own, modes = own_ref.shape
    depth = comps * own
    odd = lax.rem(lax.axis_index("atom"), 2) == 1
    one = rim_one[...].reshape(comps * RIM, modes)
    two = rim_two[...].reshape(comps * RIM, modes)
    for h, rim in enumerate((jnp.where(odd, one, two), jnp.where(odd, two, one))):
        image = (image_ref[h] + jnp.dot(cpl_ref[h], rim, preferred_element_type=F32)).astype(BF16)
        for k in range(comps):
            for c in range(comps):
                top = (k * comps + c) * RIM
                flux_ref[c, h * RIM : (h + 1) * RIM, k * modes : (k + 1) * modes] = image[top : top + RIM]
    flux = flux_ref[...].reshape(depth, comps * modes)
    eig = own_ref[...].reshape(depth, modes)
    pairs = lax.dot_general(eig, flux, (((0,), (0,)), ((), ())), preferred_element_type=F32)
    equal = iota((HALF, HALF), 0) == iota((HALF, HALF), 1)
    for k in range(comps):
        left, middle, right = k * modes, k * modes + HALF, (k + 1) * modes
        above, below = pairs[HALF : 2 * HALF, left:middle], pairs[0:HALF, middle:right]
        first = jnp.where(equal, above, pairs[0:HALF, left:middle])
        second = jnp.where(equal, below, pairs[HALF : 2 * HALF, middle:right])
        keep_ref[k] = jnp.where(odd, second, first)
        send_ref[k] = jnp.where(odd, first, second).astype(BF16)
        cross_ref[0, k] = above
        cross_ref[1, k] = below


def side_kernel(flux_ref, cross_ref, halo_one, halo_two, keep_ref, send_ref):
    comps, own, wide = flux_ref.shape
    modes, depth = wide // comps, comps * own
    odd = lax.rem(lax.axis_index("atom"), 2) == 1
    high = lax.rem(lax.axis_index("mode"), 2) == 1
    flux = flux_ref[...].reshape(depth, wide)
    first, second = halo_one[0:depth, :], halo_two[0:depth, :]
    before = jnp.where(high, first, second)
    after = jnp.where(high, second, first)
    low_flux = jnp.concatenate([flux[:, k * modes : k * modes + HALF] for k in range(comps)], axis=1)
    high_flux = jnp.concatenate([flux[:, k * modes + HALF : (k + 1) * modes] for k in range(comps)], axis=1)
    contract = (((0,), (0,)), ((), ()))
    below = lax.dot_general(before, low_flux, contract, preferred_element_type=F32)
    above = lax.dot_general(after, high_flux, contract, preferred_element_type=F32)
    rows, columns = iota((HALF, HALF), 0), iota((HALF, HALF), 1)
    for k in range(comps):
        here = slice(k * HALF, (k + 1) * HALF)
        first = jnp.where(rows >= columns, below[:, here], cross_ref[0, k])
        second = jnp.where(rows > columns, cross_ref[1, k], above[:, here])
        keep_ref[k] = jnp.where(odd, second, first)
        send_ref[k] = jnp.where(odd, first, second).astype(BF16)


def pair_call(kernel, out_shape, flops, *operands):
    return pl.pallas_call(
        kernel,
        out_shape=tuple(jax.ShapeDtypeStruct(shape, kind) for shape, kind in out_shape),
        in_specs=[VMEM] * len(operands),
        out_specs=(VMEM,) * len(out_shape),
        compiler_params=pltpu.CompilerParams(vmem_limit_bytes=LARGE),
        cost_estimate=pl.CostEstimate(flops=flops, bytes_accessed=10**6, transcendentals=0),
    )(*operands)


def halo_freq(halo_ref, comps):
    tail = halo_ref[halo_ref.shape[0] - EXTRA :, :].astype(F32)
    rows = []
    for top in (0, EXTRA // 2):
        total = jnp.zeros((1, HALF), F32)
        for part in reversed(range(comps)):
            total = tail[top + part : top + part + 1] + total
        rows.append(total)
    return rows


def ends_kernel(comps, freq_ref, halo_ref, out_ref):
    modes = freq_ref.shape[1]
    rows = (freq_ref[:, 0:HALF], freq_ref[:, modes - HALF : modes], *halo_freq(halo_ref, comps))
    least = jnp.min(functools.reduce(jnp.minimum, rows), axis=1, keepdims=True)
    most = jnp.max(functools.reduce(jnp.maximum, rows), axis=1, keepdims=True)
    out_ref[...] = jnp.where(iota(out_ref.shape, 0) < 4, least, most)


def weigh_kernel(count, comps, freq_ref, ends_ref, band_ref, halo_one, halo_two, main_one, main_two, side_one, side_two, out_ref):
    modes = freq_ref.shape[1]
    second = lax.rem(lax.axis_index("atom"), 2) == 1
    high = lax.rem(lax.axis_index("mode"), 2) == 1
    shift = jnp.where(second, HALF, 0)
    start = lax.axis_index("mode") * modes + shift
    (one_first, one_last), (two_first, two_last) = halo_freq(halo_one, comps), halo_freq(halo_two, comps)
    one, two = jnp.where(high, one_last, one_first), jnp.where(high, two_first, two_last)
    outside = jnp.where(high == second, two, one)
    inside = jnp.where(second, freq_ref[:, 0:HALF], freq_ref[:, HALF:modes])
    freq = jnp.where(second, freq_ref[:, HALF:modes], freq_ref[:, 0:HALF])
    prev = jnp.where(second, inside, outside)
    following = jnp.where(second, outside, inside)
    prev = jnp.where(start == 0, 1.0, prev)
    following = jnp.where(start == count - HALF, 1.0, following)
    band = jnp.where(second, band_ref[:, HALF:modes], band_ref[:, 0:HALF])
    low_end, high_end = band[0:1], band[1:2]
    eta = BROAD * (ends_ref[7:8, :] - ends_ref[0:1, :]) / (count - 1)

    def column(row):
        return jnp.transpose(jnp.broadcast_to(row, (HALF, HALF)))

    def weight(partner_freq, partner_ids, own_ids):
        within = (partner_ids >= low_end) & (partner_ids < high_end) & (partner_ids != own_ids)
        detune = freq - partner_freq
        total = freq + partner_freq
        scale = (eta / math.pi) * (total * total)
        value = scale / ((detune * detune + eta * eta) * (4.0 * freq * partner_freq))
        return jnp.where(within, value, 0.0)

    rows, columns = iota((HALF, HALF), 0), iota((HALF, HALF), 1)
    own_ids = start + columns
    corner = rows == columns
    corner_freq, corner_shift = jnp.where(second, prev, following), jnp.where(second, -HALF, HALF)
    main_freq = jnp.where(corner, corner_freq, column(freq))
    main_weight = weight(main_freq, start + rows + jnp.where(corner, corner_shift, 0), own_ids)
    lower = rows + jnp.where(second, 0, 1) > columns
    side_freq = jnp.where(lower, column(prev), column(following))
    side_weight = weight(side_freq, start + rows + jnp.where(lower, -HALF, HALF), own_ids)
    main_strength = jnp.zeros((HALF, HALF), F32)
    side_strength = jnp.zeros((HALF, HALF), F32)
    for k in range(comps):
        main = main_one[k].astype(F32) + main_two[k].astype(F32)
        side = side_one[k].astype(F32) + side_two[k].astype(F32)
        main_strength += main * main
        side_strength += side * side
    total = jnp.sum(main_weight * main_strength + side_weight * side_strength, axis=0, keepdims=True)
    diff = math.pi / (3.0 * freq * freq) * total
    grown = jnp.exp(freq)
    carried = freq * freq * grown / ((grown - 1.0) * (grown - 1.0)) * diff
    out_ref[0:1] = diff
    out_ref[1:2] = carried
    out_ref[2:8] = jnp.broadcast_to(jnp.sum(carried, axis=1, keepdims=True), (6, HALF))


def local_call(kernel, out_shape, *operands):
    return pl.pallas_call(
        kernel,
        out_shape=out_shape,
        in_specs=[VMEM] * len(operands),
        out_specs=jax.tree.map(lambda _: VMEM, out_shape),
        compiler_params=pltpu.CompilerParams(vmem_limit_bytes=SMALL),
        cost_estimate=pl.CostEstimate(flops=10**6, bytes_accessed=10**6, transcendentals=0),
    )(*operands)


def running_kernel(modes, own_ref, other_ref, diff_ref, run_ref):
    odd = lax.rem(lax.axis_index("atom"), 2) == 1
    own, other = own_ref[...], other_ref[...]
    whole = jnp.concatenate([jnp.where(odd, other, own), jnp.where(odd, own, other)], axis=1)
    diff_ref[...] = whole[0:1]
    until = jnp.where(iota((modes, modes), 0) <= iota((modes, modes), 1), 1.0, 0.0)
    running = jnp.dot(whole, until, precision=lax.Precision.HIGHEST, preferred_element_type=F32)
    run_ref[...] = running[1:2]


def last_kernel(run_ref, earlier_ref, out_ref):
    modes = run_ref.shape[1]
    out_ref[...] = (run_ref[...] + earlier_ref[0:1, 0:1]) / modes


def swap(x, axis, bit):
    return lax.ppermute(x, axis, [(i, i ^ bit) for i in range(lax.axis_size(axis))])


def upward(blocks, bit):
    low = [i for i in range(blocks) if i < i ^ bit]
    high = [i for i in range(blocks) if i > i ^ bit]
    return {**{i: i ^ bit for i in low}, **dict(zip(high, low))}


def bits_of(axis):
    return [1 << b for b in range(lax.axis_size(axis).bit_length() - 1)]


def rounded_sum(own, other):
    total = own.astype(F32) + other.astype(F32)
    return lax.reduce_precision(total, 8, 7).astype(BF16)


def body(eigvec, force, bond, nbr, band, freq):
    domains, blocks = lax.axis_size("atom"), lax.axis_size("mode")
    comps, own, modes = eigvec.shape
    atoms, count = own * domains, modes * blocks
    block = lax.axis_index("mode")
    freq_row = freq.reshape(1, modes)
    inner = [(i, i ^ 1) for i in range(domains)]
    outer = [(i, (i + 1) % domains if i % 2 else (i - 1) % domains) for i in range(domains)]
    near = [(i, i ^ 1) for i in range(blocks)]
    far = [(i, i + 1 if i % 2 else i - 1) for i in range(1, blocks - 1)]
    inner_edge, outer_edge = edge_call(rim_kernel, (comps, RIM, modes), COST, eigvec)
    outer_edge, later = lax.optimization_barrier((outer_edge, freq_row))
    near_edge, far_edge = edge_call(halo_kernel, (comps * own + EXTRA, HALF), COST, eigvec, later)
    near_edge, held = lax.optimization_barrier((near_edge, eigvec))
    rim_two = lax.ppermute(outer_edge, "atom", outer)
    rim_one = lax.ppermute(inner_edge, "atom", inner)
    halo_one = lax.ppermute(near_edge, "mode", near)
    hops = []
    for a in range(domains):
        for i in range(blocks):
            inside = 0 < i < blocks - 1
            hops.append((a * blocks + i, a * blocks + (i + 1 if i % 2 else i - 1) if inside else (a ^ 1) * blocks + i))
    halo_two = lax.ppermute(far_edge, ("atom", "mode"), hops)

    image, matrix = own_image(force, bond, nbr, held, atoms)
    square = (comps, HALF, HALF)
    keep_main, send_main, cross, flux = pair_call(
        main_kernel,
        ((square, F32), (square, BF16), ((2, *square), F32), ((comps, own, comps * modes), BF16)),
        10**9, image, matrix, eigvec, rim_one, rim_two,
    )
    keep_side, send_side = pair_call(
        side_kernel, ((square, F32), (square, BF16)), 10**9, flux, cross, halo_one, halo_two
    )

    tile = jax.ShapeDtypeStruct((8, HALF), F32)
    row = jax.ShapeDtypeStruct((1, modes), F32)
    main = rounded_sum(keep_main, swap(send_main, "atom", 1))
    side = rounded_sum(keep_side, swap(send_side, "atom", 1))
    side, own_freq = lax.optimization_barrier((side, freq_row))
    ends = local_call(functools.partial(ends_kernel, comps), tile, own_freq, halo_one)
    steps = bits_of("atom")[1:]
    for step, (one, two) in enumerate(zip(steps, reversed(steps))):
        main_other, side_other = swap(main, "atom", one), swap(side, "atom", two)
        if step < len(steps) - 1:
            main, side = rounded_sum(main, main_other), rounded_sum(side, side_other)
    for bit in bits_of("mode")[1:]:
        other = swap(ends, "mode", bit)
        ends = jnp.where(iota((8, HALF), 0) < 4, jnp.minimum(ends, other), jnp.maximum(ends, other))
    summary = local_call(
        functools.partial(weigh_kernel, count, comps),
        tile, freq_row, ends, band, halo_one, halo_two, main, main_other, side, side_other,
    )

    other = swap(summary, "atom", 1)
    diff, running = local_call(functools.partial(running_kernel, modes), (row, row), summary, other)
    total = summary[2:3] + other[2:3]
    odd = lax.rem(lax.axis_index("atom"), 2) == 1
    held = jnp.zeros_like(total)
    for high in range(blocks - 1, 1, -2):
        routes = upward(blocks, high), upward(blocks, high - 1)
        mixed = [(a * blocks + i, a * blocks + routes[a % 2][i]) for a in range(domains) for i in range(blocks)]
        part = lax.ppermute(total, ("atom", "mode"), mixed)
        source = block ^ jnp.where(odd, high - 1, high)
        held = held + jnp.where(source < block, part, 0.0)
    near_part = jnp.where((block & 1) != 0, swap(total, "mode", 1), 0.0)
    earlier = (held + swap(held, "atom", 1)) + near_part
    conductivity = local_call(last_kernel, row, running, earlier)
    return diff.reshape(modes), conductivity.reshape(modes)


def solution(mesh):
    in_specs = (
        P(None, "atom", "mode"),
        P(None, None, None, "atom"),
        P(None, None, "atom"),
        P(None, "atom"),
        P(None, "mode"),
        P("mode"),
    )
    out_specs = (P("mode"), P("mode"))
    return jax.shard_map(body, mesh=mesh, in_specs=in_specs, out_specs=out_specs, check_vma=False)
```
